128 devices in a mesh: shard: 4 (over x), ctx: 4 (over y_hi, core), tp: 8 (over y_lo, z).
Axes of the slice: x: 4, y: 4 (y_hi: 2, y_lo: 2; y = y_hi * 2 + y_lo), z: 4, core: 2. Of those that a mesh axis runs over, the one named last changes fastest.
Arguments:
- tokens: bfloat16 [12288, 2048], P(('shard', 'ctx')), may hold values from -6 to 6
- cotangent: bfloat16 [12288, 2048], P(('shard', 'ctx')), may hold values from -6 to 6
- lengths: int32 [8], replicated, may hold values from 128 to 3072, as said below
- groups: int32 [8], replicated, may hold values from 0 to 3
- query_weight: float32 [2048, 2048], P(('shard', 'ctx'), 'tp'), may hold values from -0.125 to 0.125
- query_m: float32 [2048, 2048], P(('shard', 'ctx'), 'tp'), may hold values from -64 to 64
- query_v: float32 [2048, 2048], P(('shard', 'ctx'), 'tp'), may hold values from 651.264 to 2580.48
- kv_weight: float32 [2048, 8, 128], P(('shard', 'ctx'), 'tp'), may hold values from -0.125 to 0.125
- kv_m: float32 [2048, 8, 128], P(('shard', 'ctx'), 'tp'), may hold values from -64 to 64
- kv_v: float32 [2048, 8, 128], P(('shard', 'ctx'), 'tp'), may hold values from 651.264 to 2580.48
- out_weight: float32 [2048, 2048], P('tp', ('shard', 'ctx')), may hold values from -4 to 4
- out_m: float32 [2048, 2048], P('tp', ('shard', 'ctx')), may hold values from -4 to 4
- out_v: float32 [2048, 2048], P('tp', ('shard', 'ctx')), may hold values from 0.64 to 2.52
- gate_weight: float32 [2048, 8192], P(('shard', 'ctx'), 'tp'), may hold values from -0.125 to 0.125
- gate_m: float32 [2048, 8192], P(('shard', 'ctx'), 'tp'), may hold values from -20 to 20
- gate_v: float32 [2048, 8192], P(('shard', 'ctx'), 'tp'), may hold values from 58.9824 to 233.472
- up_weight: float32 [2048, 8192], P(('shard', 'ctx'), 'tp'), may hold values from -0.125 to 0.125
- up_m: float32 [2048, 8192], P(('shard', 'ctx'), 'tp'), may hold values from -20 to 20
- up_v: float32 [2048, 8192], P(('shard', 'ctx'), 'tp'), may hold values from 58.9824 to 233.472
- down_weight: float32 [8192, 2048], P('tp', ('shard', 'ctx')), may hold values from -0.0625 to 0.0625
- down_m: float32 [8192, 2048], P('tp', ('shard', 'ctx')), may hold values from -28 to 28
- down_v: float32 [8192, 2048], P('tp', ('shard', 'ctx')), may hold values from 104.448 to 417.792
- norm_gains: float32 [2, 2048], P(None, ('shard', 'ctx')), may hold values from 0.5 to 1.5
- gains_m: float32 [2, 2048], P(None, ('shard', 'ctx')), may hold values from -64 to 64
- gains_v: float32 [2, 2048], P(None, ('shard', 'ctx')), may hold values from 651.264 to 2580.48
Outputs:
- output: bfloat16 [12288, 2048], P(('shard', 'ctx'))
- tokens_grad: bfloat16 [12288, 2048], P(('shard', 'ctx'))
- query_m_new: float32 [2048, 2048], P(('shard', 'ctx'), 'tp')
- query_v_new: float32 [2048, 2048], P(('shard', 'ctx'), 'tp')
- query_new: float32 [2048, 2048], P(('shard', 'ctx'), 'tp')
- kv_m_new: float32 [2048, 8, 128], P(('shard', 'ctx'), 'tp')
- kv_v_new: float32 [2048, 8, 128], P(('shard', 'ctx'), 'tp')
- kv_new: float32 [2048, 8, 128], P(('shard', 'ctx'), 'tp')
- out_m_new: float32 [2048, 2048], P('tp', ('shard', 'ctx'))
- out_v_new: float32 [2048, 2048], P('tp', ('shard', 'ctx'))
- out_new: float32 [2048, 2048], P('tp', ('shard', 'ctx'))
- gate_m_new: float32 [2048, 8192], P(('shard', 'ctx'), 'tp')
- gate_v_new: float32 [2048, 8192], P(('shard', 'ctx'), 'tp')
- gate_new: float32 [2048, 8192], P(('shard', 'ctx'), 'tp')
- up_m_new: float32 [2048, 8192], P(('shard', 'ctx'), 'tp')
- up_v_new: float32 [2048, 8192], P(('shard', 'ctx'), 'tp')
- up_new: float32 [2048, 8192], P(('shard', 'ctx'), 'tp')
- down_m_new: float32 [8192, 2048], P('tp', ('shard', 'ctx'))
- down_v_new: float32 [8192, 2048], P('tp', ('shard', 'ctx'))
- down_new: float32 [8192, 2048], P('tp', ('shard', 'ctx'))
- gains_m_new: float32 [2, 2048], P(None, ('shard', 'ctx'))
- gains_v_new: float32 [2, 2048], P(None, ('shard', 'ctx'))
- gains_new: float32 [2, 2048], P(None, ('shard', 'ctx'))
The draws below stay inside these ranges and needn't reach their ends.
Inputs may be any that keep to these rules, and one draw needn't show every extreme that they name: Lengths are multiples of 128. Sequence g < 4 belongs to group g; the others belong to any group. The lengths of one group's sequences sum to at most 3072, and to exactly 3072 in some group.
All inputs are finite; a program needn't handle non-finite values.
Results may differ from the reference program's by a relative error of at most 0.013.
The reference program's roundings to bfloat16 on the way count: a program that leaves them out, or rounds other values in their place, can miss the bound.
Values may be sent and summed in bfloat16 or wider, within the bound.
No kernel may reach another device: no remote copies, remote signals or barrier semaphores. Data moves between devices by JAX's collectives and lax.ppermute only.
A program may use at most 192 MiB of HBM per device.

```python
import math
import jax
import jax.numpy as jnp
from jax import lax

D = 2048
QH = 32
KVH = 8
HD = 64
FF = 8192
UNIT = 128
TOK_DEV = 768
STEP = 5
GROUP = 3072
TOKENS = 12288
N_SHARD = 4
N_CTX = 4


def sequence_layout(key):
    draw_group, draw_short, draw_long, draw_full = jax.random.split(key, 4)
    owners = jnp.arange(N_SHARD, dtype=jnp.int32)
    filled = jax.random.randint(draw_full, (), 0, N_SHARD)
    short_group = (filled + 1 + jax.random.randint(draw_group, (N_SHARD,), 0, N_SHARD - 1)) % N_SHARD
    crowding = jnp.sum((short_group[:, None] == short_group[None, :]).astype(jnp.int32), axis=1)
    spare_units = TOK_DEV // UNIT - 1
    ceiling = jnp.maximum(1, spare_units // crowding)
    short_units = jax.random.randint(draw_short, (N_SHARD,), 1, ceiling + 1)
    short_units = jnp.where(owners == 0, 1, short_units)
    taken = jnp.sum(jnp.where(short_group[None, :] == owners[:, None], short_units[None, :], 0), axis=1)
    free_units = GROUP // UNIT - taken
    lowest = (N_CTX - 1) * TOK_DEV // UNIT + 1
    long_units = jax.random.randint(draw_long, (N_SHARD,), lowest, free_units + 1)
    long_units = jnp.where(owners == filled, free_units, long_units)
    lengths = jnp.concatenate([long_units, short_units]) * UNIT
    groups = jnp.concatenate([owners, short_group])
    return (lengths.astype(jnp.int32), groups.astype(jnp.int32))


def draw_lengths(key, part):
    lengths, groups = sequence_layout(key)
    return lengths


def draw_groups(key, part):
    lengths, groups = sequence_layout(key)
    return groups


def levels(rng, extent, cuts, smallest, top_value):
    def one(dim, blocks):
        draws = jax.random.uniform(jax.random.fold_in(jax.random.fold_in(rng, 6), dim), (blocks,), jnp.float32, smallest / len(cuts), top_value / len(cuts))
        return jnp.repeat(jnp.exp(draws), extent[dim] // blocks).reshape((-1,) + (1,) * (len(extent) - dim - 1))

    level = one(*cuts[0])
    for cut in cuts[1:]:
        level = level * one(*cut)
    return level


def bell_draw(stream_key, dims, scale, reach, cuts=(), kind=jnp.bfloat16):
    array = scale * jax.random.normal(stream_key, dims, jnp.float32)
    if cuts:
        array = array * levels(stream_key, dims, cuts, -0.22, 0.18)
    return jnp.clip(array, -reach, reach).astype(kind)


def setup_inputs(seed: int = 0) -> dict:
    key_of = jax.random.split(jax.random.key(seed), 26)
    tokens = bell_draw(key_of[0], (TOKENS, D), 1.0, 6.0, ((0, 16),))
    cotangent = bell_draw(key_of[1], (TOKENS, D), 1.0, 6.0, ((0, 16),))
    lengths = draw_lengths(jax.random.fold_in(key_of[25], 71), 0)
    groups = draw_groups(jax.random.fold_in(key_of[25], 71), 0)
    query_weight = bell_draw(key_of[4], (D, QH * HD), D ** -0.5, 0.125, ((0, 16), (1, 8)), jnp.float32)
    query_m = bell_draw(key_of[5], (D, QH * HD), (0.11 * TOKENS ** 0.5), 64.0, ((0, 16), (1, 8)), jnp.float32)
    query_v = jnp.clip(jnp.exp(math.log(2580.48) - 1.37681564 * jax.random.uniform(key_of[6], (D, QH * HD), jnp.float32) ** levels(key_of[6], (D, QH * HD), ((0, 16), (1, 8)), -0.2, 0.2)), 651.264, 2580.48)
    kv_weight = bell_draw(key_of[7], (D, KVH, 2 * HD), D ** -0.5, 0.125, ((0, 16), (1, 8)), jnp.float32)
    kv_m = bell_draw(key_of[8], (D, KVH, 2 * HD), (0.11 * TOKENS ** 0.5), 64.0, ((0, 16), (1, 8)), jnp.float32)
    kv_v = jnp.clip(jnp.exp(math.log(2580.48) - 1.37681564 * jax.random.uniform(key_of[9], (D, KVH, 2 * HD), jnp.float32) ** levels(key_of[9], (D, KVH, 2 * HD), ((0, 16), (1, 8)), -0.2, 0.2)), 651.264, 2580.48)
    out_weight = bell_draw(key_of[10], (QH * HD, D), (max(1, 4 * D // GROUP)) ** -0.5, 4.0, ((0, 8), (1, 16)), jnp.float32)
    out_m = bell_draw(key_of[11], (QH * HD, D), (0.19 * (TOKENS / GROUP) ** 0.5), 4.0, ((0, 8), (1, 16)), jnp.float32)
    out_v = jnp.clip(jnp.exp(math.log(2.52) - 1.370546 * jax.random.uniform(key_of[12], (QH * HD, D), jnp.float32) ** levels(key_of[12], (QH * HD, D), ((0, 8), (1, 16)), -0.2, 0.2)), 0.64, 2.52)
    gate_weight = bell_draw(key_of[13], (D, FF), D ** -0.5, 0.125, ((0, 16), (1, 8)), jnp.float32)
    gate_m = bell_draw(key_of[14], (D, FF), (0.033 * TOKENS ** 0.5), 20.0, ((0, 16), (1, 8)), jnp.float32)
    gate_v = jnp.clip(jnp.exp(math.log(233.472) - 1.375823 * jax.random.uniform(key_of[15], (D, FF), jnp.float32) ** levels(key_of[15], (D, FF), ((0, 16), (1, 8)), -0.2, 0.2)), 58.9824, 233.472)
    up_weight = bell_draw(key_of[16], (D, FF), D ** -0.5, 0.125, ((0, 16), (1, 8)), jnp.float32)
    up_m = bell_draw(key_of[17], (D, FF), (0.033 * TOKENS ** 0.5), 20.0, ((0, 16), (1, 8)), jnp.float32)
    up_v = jnp.clip(jnp.exp(math.log(233.472) - 1.375823 * jax.random.uniform(key_of[18], (D, FF), jnp.float32) ** levels(key_of[18], (D, FF), ((0, 16), (1, 8)), -0.2, 0.2)), 58.9824, 233.472)
    down_weight = bell_draw(key_of[19], (FF, D), FF ** -0.5, 0.0625, ((0, 8), (1, 16)), jnp.float32)
    down_m = bell_draw(key_of[20], (FF, D), (0.044 * TOKENS ** 0.5), 28.0, ((0, 8), (1, 16)), jnp.float32)
    down_v = jnp.clip(jnp.exp(math.log(417.792) - 1.3862944 * jax.random.uniform(key_of[21], (FF, D), jnp.float32) ** levels(key_of[21], (FF, D), ((0, 8), (1, 16)), -0.2, 0.2)), 104.448, 417.792)
    norm_gains = jnp.clip(1.0 + 0.1 * jax.random.normal(key_of[22], (2, D), jnp.float32), 0.5, 1.5)
    gains_m = bell_draw(key_of[23], (2, D), (0.11 * TOKENS ** 0.5), 64.0, ((1, 16),), jnp.float32)
    gains_v = jnp.clip(jnp.exp(math.log(2580.48) - 1.37681564 * jax.random.uniform(key_of[24], (2, D), jnp.float32) ** levels(key_of[24], (2, D), ((1, 16),), -0.2, 0.2)), 651.264, 2580.48)
    return {"tokens": tokens, "cotangent": cotangent, "lengths": lengths, "groups": groups, "query_weight": query_weight, "query_m": query_m, "query_v": query_v, "kv_weight": kv_weight, "kv_m": kv_m, "kv_v": kv_v, "out_weight": out_weight, "out_m": out_m, "out_v": out_v, "gate_weight": gate_weight, "gate_m": gate_m, "gate_v": gate_v, "up_weight": up_weight, "up_m": up_m, "up_v": up_v, "down_weight": down_weight, "down_m": down_m, "down_v": down_v, "norm_gains": norm_gains, "gains_m": gains_m, "gains_v": gains_v}


@jax.custom_vjp
def low(v):
    return lax.optimization_barrier(v.astype(jnp.bfloat16)).astype(jnp.float32)

@jax.custom_vjp
def low_back(v):
    return v

def low_keep(v):
    return (low(v), None)

def low_pass(kept, grad):
    return (grad,)

def back_keep(v):
    return (v, None)

def back_low(kept, grad):
    return (low(grad),)
low.defvjp(low_keep, low_pass)
low_back.defvjp(back_keep, back_low)
NORM_EPS = 1e-05
BETA_FIRST = 0.9
BETA_SECOND = 0.95
ADAM_EPS = 1e-08
DECAY_RATE = 0.1
ROPE_BASE = 500000.0
MASKED_SCORE = -1e+30

def layout_slots(lengths, groups, group_id, slot_ids):
    seq_count = lengths.shape[0]
    seq_order = jnp.arange(seq_count, dtype=jnp.int32)
    same_group = groups[None, :] == groups[:, None]
    before = seq_order[None, :] < seq_order[:, None]
    starts = lax.optimization_barrier(jnp.sum(jnp.where(same_group & before, lengths[None, :], 0), axis=1)).astype(jnp.int32)
    ends = (starts + lengths).astype(jnp.int32)
    inside = (groups == group_id)[:, None] & (slot_ids[None, :] >= starts[:, None]) & (slot_ids[None, :] < ends[:, None])
    document = (lax.optimization_barrier(jnp.sum(jnp.where(inside, seq_order[:, None] + 1, 0), axis=0)) - 1).astype(jnp.int32)
    position = lax.optimization_barrier(jnp.sum(jnp.where(inside, slot_ids[None, :] - starts[:, None], 0), axis=0)).astype(jnp.int32)
    document = jnp.where(document < 0, seq_count + slot_ids, document).astype(jnp.int32)
    return (document, position)

def rotate(values, position, direction):
    half_dim = values.shape[-1] // 2
    frequency = ROPE_BASE ** (-2.0 * jnp.arange(half_dim, dtype=jnp.float32) / values.shape[-1])
    angles = position.astype(jnp.float32)[:, None] * frequency[None, :]
    cosine = jnp.cos(angles)[:, None, :]
    sine_part = direction * jnp.sin(angles)[:, None, :]
    first_half = values[..., :half_dim]
    second = values[..., half_dim:]
    return jnp.concatenate([first_half * cosine - second * sine_part, second * cosine + first_half * sine_part], axis=-1)

def matmul(left, right):
    return jnp.dot(left, right, precision=lax.Precision.HIGHEST)

def attend(query_head, key_head, value_head, visible, scale):
    scores = matmul(query_head, key_head.T) * scale
    scores = low_back(jnp.where(visible, scores, MASKED_SCORE))
    row_peak = lax.optimization_barrier(jnp.max(scores, axis=-1, keepdims=True))
    powers = jnp.exp(scores - row_peak)
    chances = low(powers / lax.optimization_barrier(jnp.sum(powers, axis=-1, keepdims=True)))
    return matmul(chances, value_head)

def layer(inputs, gains, w_query, w_kv, w_out, w_gate, w_up, w_down, document, position):
    group_rows = inputs.shape[0]
    gains_low = low(gains)
    inv_one = lax.rsqrt(lax.optimization_barrier(jnp.mean(inputs * inputs, axis=-1, keepdims=True)) + NORM_EPS)
    normed_one = low(inputs * inv_one * gains_low[0])
    query_raw = matmul(normed_one, low(w_query)).reshape(group_rows, QH, HD)
    queries = low(rotate(low_back(query_raw), position, 1.0))
    kv_raw = low_back(matmul(normed_one, low(w_kv).reshape(D, KVH * 2 * HD)).reshape(group_rows, KVH, 2 * HD))
    keys = low(rotate(kv_raw[..., :HD], position, 1.0))
    values = low(kv_raw[..., HD:])
    visible = (document[:, None] == document[None, :]) & (position[None, :] <= position[:, None])
    head_share = QH // KVH
    key_heads = jnp.repeat(keys, head_share, axis=1).transpose(1, 0, 2)
    value_heads = jnp.repeat(values, head_share, axis=1).transpose(1, 0, 2)
    scale = HD ** (-0.5)

    def one_head(operands):
        return attend(operands[0], operands[1], operands[2], visible, scale)
    mixed = lax.map(jax.checkpoint(one_head), (queries.transpose(1, 0, 2), key_heads, value_heads))
    mixed = low(low_back(mixed.transpose(1, 0, 2).reshape(group_rows, QH * HD)))
    hidden_one = inputs + low_back(matmul(mixed, low(w_out)))
    inv_two = lax.rsqrt(lax.optimization_barrier(jnp.mean(hidden_one * hidden_one, axis=-1, keepdims=True)) + NORM_EPS)
    normed_two = low(hidden_one * inv_two * gains_low[1])
    gate_value = low_back(matmul(normed_two, low(w_gate)))
    up_value = low_back(matmul(normed_two, low(w_up)))
    hidden = low(jax.nn.silu(gate_value) * up_value)
    return hidden_one + matmul(hidden, low(w_down))

def adamw_step(weight, first, second, grad, rate, decay):
    first_new = BETA_FIRST * first + (1.0 - BETA_FIRST) * grad
    second_new = BETA_SECOND * second + (1.0 - BETA_SECOND) * grad * grad
    first_hat = first_new / (1.0 - BETA_FIRST ** STEP)
    second_hat = second_new / (1.0 - BETA_SECOND ** STEP)
    weight_new = weight - rate * (first_hat / (jnp.sqrt(second_hat) + ADAM_EPS) + decay * weight)
    return (first_new, second_new, weight_new)

def reference(tokens, cotangent, lengths, groups, query_weight, query_m, query_v, kv_weight, kv_m, kv_v, out_weight, out_m, out_v, gate_weight, gate_m, gate_v, up_weight, up_m, up_v, down_weight, down_m, down_v, norm_gains, gains_m, gains_v):
    params = (norm_gains, query_weight, kv_weight, out_weight, gate_weight, up_weight, down_weight)
    inputs = tokens.astype(jnp.float32).reshape(N_SHARD, GROUP, D)
    upstream = cotangent.astype(jnp.float32).reshape(N_SHARD, GROUP, D)
    slot_ids = jnp.arange(GROUP, dtype=jnp.int32)

    def per_group(totals, operands):
        group_in, group_up, group_id = operands
        document, position = layout_slots(lengths, groups, group_id, slot_ids)

        def run(inputs_now, *weights):
            return layer(inputs_now, *weights, document, position)
        result, pullback = jax.vjp(run, group_in, *params)
        grads = pullback(group_up)
        totals = tuple((total_now + grad_now for total_now, grad_now in zip(totals, grads[1:])))
        return (totals, (result.astype(jnp.bfloat16), grads[0].astype(jnp.bfloat16)))
    zeros = tuple((jnp.zeros_like(weight) for weight in params))
    totals, (outputs, input_grads) = lax.scan(per_group, zeros, (inputs, upstream, jnp.arange(N_SHARD, dtype=jnp.int32)))
    grad_gains, grad_query, grad_kv, grad_out, grad_gate, grad_up, grad_down = totals
    out_fan = max(1, 4 * D // GROUP)
    query_new = adamw_step(query_weight, query_m, query_v, grad_query, D ** (-0.5), DECAY_RATE)
    kv_new = adamw_step(kv_weight, kv_m, kv_v, grad_kv, D ** (-0.5), DECAY_RATE)
    out_new = adamw_step(out_weight, out_m, out_v, grad_out, out_fan ** (-0.5), DECAY_RATE)
    gate_new = adamw_step(gate_weight, gate_m, gate_v, grad_gate, D ** (-0.5), DECAY_RATE)
    up_new = adamw_step(up_weight, up_m, up_v, grad_up, D ** (-0.5), DECAY_RATE)
    down_new = adamw_step(down_weight, down_m, down_v, grad_down, FF ** (-0.5), DECAY_RATE)
    gains_new = adamw_step(norm_gains, gains_m, gains_v, grad_gains, 0.5, 0.0)
    return (outputs.reshape(TOKENS, D), input_grads.reshape(TOKENS, D), query_new[0], query_new[1], query_new[2], kv_new[0], kv_new[1], kv_new[2], out_new[0], out_new[1], out_new[2], gate_new[0], gate_new[1], gate_new[2], up_new[0], up_new[1], up_new[2], down_new[0], down_new[1], down_new[2], gains_new[0], gains_new[1], gains_new[2])
```

```python
import functools

import jax
import jax.numpy as jnp
from jax import lax
from jax.experimental import pallas as pl
from jax.experimental.pallas import tpu as pltpu
from jax.sharding import Mesh
from jax.sharding import PartitionSpec as P

D = 2048
HD = 64
FF = 8192
STEP = 5


NORM_EPS = 1e-05
BETA_FIRST = 0.9
BETA_SECOND = 0.95
ADAM_EPS = 1e-08
DECAY_RATE = 0.1
ROPE_BASE = 500000.0
MASKED_SCORE = -1e30

F32 = jnp.float32
BF16 = jnp.bfloat16
SWAP = ((0, 1), (1, 0))


def ring(step):
    return tuple((i, (i + step) % 4) for i in range(4))


def layout_slots(lengths, groups, group_id, slot_ids):
    seq_count = lengths.shape[0]
    seq_order = jnp.arange(seq_count, dtype=jnp.int32)
    same_group = groups[None, :] == groups[:, None]
    before = seq_order[None, :] < seq_order[:, None]
    starts = jnp.sum(jnp.where(same_group & before, lengths[None, :], 0), axis=1)
    ends = starts + lengths
    inside = (
        (groups == group_id)[:, None]
        & (slot_ids[None, :] >= starts[:, None])
        & (slot_ids[None, :] < ends[:, None])
    )
    document = jnp.sum(jnp.where(inside, seq_order[:, None] + 1, 0), axis=0) - 1
    position = jnp.sum(jnp.where(inside, slot_ids[None, :] - starts[:, None], 0), axis=0)
    document = jnp.where(document < 0, seq_count + slot_ids, document)
    return (document, position)


def rotate(values, position, direction):
    half_dim = values.shape[-1] // 2
    frequency = ROPE_BASE ** (-2.0 * jnp.arange(half_dim, dtype=jnp.float32) / values.shape[-1])
    angles = position.astype(jnp.float32)[:, None] * frequency[None, :]
    cosine = jnp.cos(angles)[:, None, :]
    sine_part = direction * jnp.sin(angles)[:, None, :]
    first_half = values[..., :half_dim]
    second = values[..., half_dim:]
    return jnp.concatenate(
        [first_half * cosine - second * sine_part, second * cosine + first_half * sine_part],
        axis=-1,
    )


def adamw_step(weight, first, second, grad, rate, decay):
    first_new = BETA_FIRST * first + (1.0 - BETA_FIRST) * grad
    second_new = BETA_SECOND * second + (1.0 - BETA_SECOND) * grad * grad
    first_hat = first_new / (1.0 - BETA_FIRST**STEP)
    second_hat = second_new / (1.0 - BETA_SECOND**STEP)
    weight_new = weight - rate * (first_hat / (jnp.sqrt(second_hat) + ADAM_EPS) + decay * weight)
    return (first_new, second_new, weight_new)


def place(pieces, plan, table, out_shapes):
    moves = len(plan)
    size = sum(p.size * p.dtype.itemsize for p in pieces)

    def kernel(table_ref, *refs):
        sources, outs, sem = refs[: len(pieces)], refs[len(pieces) : -1], refs[-1]
        copies = []
        for n, (piece, source_index, out, entry) in enumerate(plan):
            source = sources[piece]
            if source_index is not None:
                source = source.at[source_index]
            copies.append(
                pltpu.make_async_copy(source, outs[out].at[table_ref[entry]], sem.at[n])
            )
        for copy in copies:
            copy.start()
        for copy in copies:
            copy.wait()

    return pl.pallas_call(
        kernel,
        out_shape=[jax.ShapeDtypeStruct(s, BF16) for s in out_shapes],
        in_specs=[pl.BlockSpec(memory_space=pltpu.SMEM)]
        + [pl.BlockSpec(memory_space=pl.ANY)] * len(pieces),
        out_specs=[pl.BlockSpec(memory_space=pl.ANY)] * len(out_shapes),
        scratch_shapes=[pltpu.SemaphoreType.DMA((moves,))],
        cost_estimate=pl.CostEstimate(flops=0, bytes_accessed=2 * size, transcendentals=0),
    )(table, *pieces)


def pick(blocks, axis, index):
    return lax.dynamic_index_in_dim(blocks, index, axis, keepdims=False)


class Here:
    def __init__(self):
        self.x, self.yh, self.c, self.yl, self.z = (
            lax.axis_index(a) for a in ("x", "yh", "c", "yl", "z")
        )

    def ztable(self):
        own = [self.yl * 4 + (self.z + k) % 4 for k in range(4)]
        other = [(1 - self.yl) * 4 + (self.z + k) % 4 for k in range(4)]
        return jnp.stack(own + other).astype(jnp.int32)

    def xtable(self):
        table = []
        for dc in range(2):
            core = self.c if dc == 0 else 1 - self.c
            for dy in range(2):
                yh = self.yh if dy == 0 else 1 - self.yh
                for k in range(4):
                    table.append(((self.x + k) % 4) * 4 + yh * 2 + core)
        return jnp.stack(table).astype(jnp.int32)

    def gather_tp(self, own, z_first, table):
        n, w = own.shape
        if not z_first:
            pair = jnp.stack([own, lax.ppermute(own, "yl", SWAP)])
            pieces = [pair] + [lax.ppermute(pair, "z", ring(-k)) for k in (1, 2, 3)]
            plan = [(k, d, 0, 4 * d + k) for k in range(4) for d in range(2)]
        else:
            mine = [own] + [lax.ppermute(own, "z", ring(-k)) for k in (1, 2, 3)]
            theirs = [lax.ppermute(p, "yl", SWAP) for p in mine]
            pieces = mine + theirs
            plan = [(i, None, 0, i) for i in range(8)]
        return place(pieces, plan, table, [(8, n, w)])[0].reshape(8 * n, w)

    def scatter_tp(self, terms, z_first):
        w = terms.shape[1]
        blocks = terms.reshape(2, 4, -1, w)
        if z_first:
            got = [
                lax.ppermute(pick(blocks, 1, (self.z + k) % 4), "z", ring(k)) for k in (1, 2, 3)
            ]
            keep = pick(pick(blocks, 1, self.z), 0, self.yl).astype(F32)
            give = pick(pick(blocks, 1, self.z), 0, 1 - self.yl).astype(F32)
            for g in got:
                keep = keep + pick(g, 0, self.yl).astype(F32)
                give = give + pick(g, 0, 1 - self.yl).astype(F32)
            return keep + lax.ppermute(give.astype(BF16), "yl", SWAP).astype(F32)
        got = lax.ppermute(pick(blocks, 0, 1 - self.yl), "yl", SWAP)
        both = pick(blocks, 0, self.yl).astype(F32) + got.astype(F32)
        low = both.astype(BF16)
        total = pick(both, 0, self.z)
        for k in (1, 2, 3):
            total = total + lax.ppermute(pick(low, 0, (self.z + k) % 4), "z", ring(k)).astype(F32)
        return total

    def gather_weights(self, shard):
        pair = jnp.stack([shard, lax.ppermute(shard, "yh", SWAP)])
        mine = [pair] + [lax.ppermute(pair, "x", ring(-k)) for k in (1, 2, 3)]
        return mine + [lax.ppermute(p, "c", SWAP) for p in mine]

    def scatter_weights(self, terms):
        w = terms.shape[1]
        blocks = terms.reshape(4, 2, 2, D // 16, w)
        got = lax.ppermute(pick(blocks, 2, 1 - self.c), "c", SWAP)
        both = pick(blocks, 2, self.c).astype(F32) + got.astype(F32)
        low = both.astype(BF16)
        total = pick(both, 0, self.x)
        for k in (1, 2, 3):
            total = total + lax.ppermute(pick(low, 0, (self.x + k) % 4), "x", ring(k)).astype(F32)
        give = pick(total, 0, 1 - self.yh).astype(BF16)
        return pick(total, 0, self.yh) + lax.ppermute(give, "yh", SWAP).astype(F32)

    def gather_ctx(self, own):
        over = lax.ppermute(own, "yh", SWAP)
        pieces = [own, over, lax.ppermute(own, "c", SWAP), lax.ppermute(over, "c", SWAP)]
        table = jnp.stack(
            [
                self.yh * 2 + self.c,
                (1 - self.yh) * 2 + self.c,
                self.yh * 2 + 1 - self.c,
                (1 - self.yh) * 2 + 1 - self.c,
            ]
        ).astype(jnp.int32)
        n, w = own.shape
        plan = [(i, None, 0, i) for i in range(4)]
        return place(pieces, plan, table, [(4, n, w)])[0].reshape(4 * n, w)

    def scatter_ctx(self, terms):
        w = terms.shape[1]
        blocks = terms.reshape(2, 2, -1, w)
        got = lax.ppermute(pick(blocks, 1, 1 - self.c).astype(BF16), "c", SWAP)
        both = pick(blocks, 1, self.c) + got.astype(F32)
        give = pick(both, 0, 1 - self.yh).astype(BF16)
        return pick(both, 0, self.yh) + lax.ppermute(give, "yh", SWAP).astype(F32)

    def sum_tp(self, value):
        value = value + lax.ppermute(value, "yl", SWAP)
        got = [lax.ppermute(value, "z", ring(k)) for k in (1, 2, 3)]
        parts = jnp.stack([value] + got)
        order = jnp.stack([(self.z - j) % 4 for j in range(4)])
        return jnp.sum(jnp.take(parts, order, axis=0), axis=0)


def per_device(
    tokens,
    cotangent,
    lengths,
    groups,
    query_weight,
    query_m,
    query_v,
    kv_weight,
    kv_m,
    kv_v,
    out_weight,
    out_m,
    out_v,
    gate_weight,
    gate_m,
    gate_v,
    up_weight,
    up_m,
    up_v,
    down_weight,
    down_m,
    down_v,
    norm_gains,
    gains_m,
    gains_v,
):
    here = Here()
    row_count = tokens.shape[0]
    group_rows = row_count * 4
    group_id = here.x
    ctx_id = here.yh * 2 + here.c
    tp_id = here.yl * 4 + here.z
    half = row_count // 2
    part = half // 8
    scale = HD ** (-0.5)
    ztable = here.ztable()
    xtable = here.xtable()

    kv_flat = kv_weight.reshape(D // 16, 2 * HD)
    attn_shard = jnp.concatenate([query_weight, kv_flat, out_weight.T], axis=1).astype(BF16)
    q_cols, kv_cols, o_cols = query_weight.shape[1], 2 * HD, out_weight.shape[0]
    cols = q_cols + kv_cols + o_cols
    gains_low = norm_gains.astype(BF16)
    gain_rows = jnp.zeros((16, cols), BF16).at[:2, : D // 16].set(gains_low)
    attn_pieces = here.gather_weights(jnp.concatenate([attn_shard, gain_rows], axis=0))
    plan = []
    for i in range(8):
        for d in range(2):
            entry = (i // 4) * 8 + d * 4 + i % 4
            rows = pl.ds(0, D // 16)
            plan.append((i, (d, rows, pl.ds(0, q_cols)), 0, entry))
            plan.append((i, (d, rows, pl.ds(q_cols, kv_cols)), 1, entry))
            plan.append((i, (d, rows, pl.ds(q_cols + kv_cols, o_cols)), 2, entry))
            plan.append((i, (d, pl.ds(D // 16, 16), pl.ds(0, D // 16)), 3, entry))
    w_query, w_kv, w_out, gain_blocks = place(
        attn_pieces,
        plan,
        xtable,
        [(16, D // 16, q_cols), (16, D // 16, kv_cols), (16, D // 16, o_cols), (16, 16, D // 16)],
    )
    w_query = w_query.reshape(D, q_cols)
    w_kv = w_kv.reshape(D, kv_cols)
    w_out = w_out.reshape(D, o_cols)
    gain_values = gain_blocks[:, :2].transpose(1, 0, 2).reshape(2, D).astype(F32)

    units = gate_weight.shape[1]
    ff_shard = jnp.stack([gate_weight, up_weight, down_weight.T]).astype(BF16)
    ff_shard, _ = lax.optimization_barrier((ff_shard, attn_pieces[1]))
    ff_pieces = here.gather_weights(ff_shard)
    plan = []
    for i in range(8):
        for d in range(2):
            for o in range(3):
                plan.append((i, (d, o), o, (i // 4) * 8 + d * 4 + i % 4))
    w_gate, w_up, w_down = (
        w.reshape(D, units) for w in place(ff_pieces, plan, xtable, [(16, D // 16, units)] * 3)
    )

    key_doc, key_pos = layout_slots(
        lengths, groups, group_id, jnp.arange(group_rows, dtype=jnp.int32)
    )
    own_doc, own_pos = layout_slots(
        lengths, groups, group_id, ctx_id * row_count + jnp.arange(row_count, dtype=jnp.int32)
    )
    visible = (own_doc[:, None] == key_doc[None, :]) & (key_pos[None, :] <= own_pos[:, None])

    inputs = tokens.astype(F32)
    inv_one = lax.rsqrt(jnp.mean(inputs * inputs, axis=-1, keepdims=True) + NORM_EPS)
    normed_one = (inputs * inv_one * gain_values[0]).astype(BF16)
    head_count = q_cols // HD
    kv_raw = jnp.dot(normed_one, w_kv, preferred_element_type=F32).reshape(row_count, 1, 2 * HD)
    kv_local = jnp.concatenate(
        [rotate(kv_raw[..., :HD], own_pos, 1.0), kv_raw[..., HD:]], axis=-1
    ).astype(BF16)
    kv_whole = here.gather_ctx(kv_local.reshape(row_count, 2 * HD))
    key_head, value_head = kv_whole[:, :HD], kv_whole[:, HD:]
    query_raw = jnp.dot(normed_one, w_query, preferred_element_type=F32).reshape(
        row_count, head_count, HD
    )
    queries = rotate(query_raw, own_pos, 1.0).astype(BF16).transpose(1, 0, 2)

    def forward_head(query_head):
        scores = (
            jnp.einsum("rd,kd->rk", query_head, key_head, preferred_element_type=F32) * scale
        )
        scores = jnp.where(visible, scores, MASKED_SCORE)
        row_peak = jnp.max(scores, axis=-1, keepdims=True)
        powers = jnp.exp(scores - row_peak)
        summed = jnp.sum(powers, axis=-1, keepdims=True)
        chances = (powers / summed).astype(BF16)
        mixed_head = jnp.dot(chances, value_head, preferred_element_type=F32)
        return (mixed_head, (row_peak + jnp.log(summed))[:, 0])

    mixed_heads, log_totals = lax.map(forward_head, queries)
    mixed = mixed_heads.transpose(1, 0, 2).reshape(row_count, head_count * HD).astype(BF16)

    halves = (0, 1)
    z_first = (False, True)
    mixed_half = [mixed[:half], mixed[half:]]
    cotangent_half = [cotangent[:half], cotangent[half:]]
    own_start = [h * half + tp_id * part for h in halves]
    own_inputs = [
        lax.dynamic_slice_in_dim(tokens, s, part, axis=0).astype(F32) for s in own_start
    ]
    own_upstream = [
        lax.dynamic_slice_in_dim(cotangent, s, part, axis=0).astype(F32) for s in own_start
    ]

    hidden_one, inv_two, pre_two, normed_two = [], [], [], []
    for h in halves:
        term = jnp.einsum("ra,da->rd", mixed_half[h], w_out, preferred_element_type=F32)
        total = here.scatter_tp(term.astype(BF16), z_first[h])
        hidden_one.append(own_inputs[h] + total)
        inv_two.append(
            lax.rsqrt(jnp.mean(hidden_one[h] * hidden_one[h], axis=-1, keepdims=True) + NORM_EPS)
        )
        pre_two.append(hidden_one[h] * inv_two[h])
        own_normed = (pre_two[h] * gain_values[1]).astype(BF16)
        normed_two.append(here.gather_tp(own_normed, z_first[h], ztable))

    hidden, d_gate, d_up, d_hidden_one, d_branch = [], [], [], [], []
    for h in halves:
        gate_value = jnp.dot(normed_two[h], w_gate, preferred_element_type=F32)
        up_value = jnp.dot(normed_two[h], w_up, preferred_element_type=F32)
        d_hidden = jnp.dot(cotangent_half[h], w_down, preferred_element_type=F32)
        sigmoid_gate = jax.nn.sigmoid(gate_value)
        activated = gate_value * sigmoid_gate
        hidden.append((activated * up_value).astype(BF16))
        d_gate.append(
            (
                d_hidden * up_value * sigmoid_gate * (1.0 + gate_value * (1.0 - sigmoid_gate))
            ).astype(BF16)
        )
        d_up.append((d_hidden * activated).astype(BF16))
        d_two_term = jnp.einsum(
            "rf,df->rd", d_gate[h], w_gate, preferred_element_type=F32
        ) + jnp.einsum("rf,df->rd", d_up[h], w_up, preferred_element_type=F32)
        d_normed_two = here.scatter_tp(d_two_term.astype(BF16), z_first[h])
        scaled = d_normed_two * gain_values[1]
        d_through = inv_two[h] * (
            scaled - pre_two[h] * jnp.mean(scaled * pre_two[h], axis=-1, keepdims=True)
        )
        d_hidden_one.append(own_upstream[h] + d_through)
        d_branch.append(
            here.gather_tp(d_hidden_one[h].astype(BF16), z_first[h], ztable)
        )

    d_mixed = jnp.concatenate(
        [jnp.dot(d_branch[h], w_out, preferred_element_type=F32).astype(BF16) for h in halves]
    )

    outputs = []
    for h in halves:
        term = jnp.einsum("rf,df->rd", hidden[h], w_down, preferred_element_type=F32)
        total = here.scatter_tp(term.astype(BF16), z_first[h])
        own_out = (hidden_one[h] + total).astype(BF16)
        outputs.append(here.gather_tp(own_out, z_first[h], ztable))
    output = jnp.concatenate(outputs)

    both = lambda pair: jnp.concatenate(pair, axis=0)
    normed_two_all = both(normed_two)
    outer = lambda a, b: jnp.einsum("rd,rf->df", a, b, preferred_element_type=F32).astype(BF16)
    grad_gate = here.scatter_weights(outer(normed_two_all, both(d_gate)))
    grad_up = here.scatter_weights(outer(normed_two_all, both(d_up)))
    grad_down = here.scatter_weights(outer(cotangent, both(hidden))).T

    d_mixed = d_mixed.reshape(row_count, head_count, HD).transpose(1, 0, 2)

    def backward_head(operands):
        query_head, d_head, log_total = operands
        scores = (
            jnp.einsum("rd,kd->rk", query_head, key_head, preferred_element_type=F32) * scale
        )
        scores = jnp.where(visible, scores, MASKED_SCORE)
        chances = jnp.exp(scores - log_total[:, None])
        d_value = jnp.einsum("rk,rd->kd", chances.astype(BF16), d_head, preferred_element_type=F32)
        d_chances = jnp.einsum("rd,kd->rk", d_head, value_head, preferred_element_type=F32)
        centre = jnp.sum(chances * d_chances, axis=-1, keepdims=True)
        d_scores = (chances * (d_chances - centre)).astype(BF16)
        d_query = jnp.dot(d_scores, key_head, preferred_element_type=F32) * scale
        d_key = jnp.einsum("rk,rd->kd", d_scores, query_head, preferred_element_type=F32) * scale
        return (d_query, d_key, d_value)

    d_queries, d_keys, d_values = lax.map(backward_head, (queries, d_mixed, log_totals))
    d_kv = jnp.concatenate([d_keys.sum(axis=0), d_values.sum(axis=0)], axis=-1)
    d_kv_own = here.scatter_ctx(d_kv)[:, None]
    d_kv_low = (
        jnp.concatenate([rotate(d_kv_own[..., :HD], own_pos, -1.0), d_kv_own[..., HD:]], axis=-1)
        .astype(BF16)
        .reshape(row_count, 2 * HD)
    )
    d_query_low = (
        rotate(d_queries.transpose(1, 0, 2), own_pos, -1.0)
        .astype(BF16)
        .reshape(row_count, head_count * HD)
    )

    tokens_grads = []
    for h in halves:
        rows = slice(h * half, (h + 1) * half)
        d_one_term = jnp.einsum(
            "ra,da->rd", d_query_low[rows], w_query, preferred_element_type=F32
        ) + jnp.einsum("rc,dc->rd", d_kv_low[rows], w_kv, preferred_element_type=F32)
        d_normed_one = here.scatter_tp(d_one_term.astype(BF16), z_first[h])
        own_inv = lax.rsqrt(
            jnp.mean(own_inputs[h] * own_inputs[h], axis=-1, keepdims=True) + NORM_EPS
        )
        pre_one = own_inputs[h] * own_inv
        scaled = d_normed_one * gain_values[0]
        d_through = own_inv * (
            scaled - pre_one * jnp.mean(scaled * pre_one, axis=-1, keepdims=True)
        )
        own_grad = (d_hidden_one[h] + d_through).astype(BF16)
        tokens_grads.append(here.gather_tp(own_grad, z_first[h], ztable))
    tokens_grad = jnp.concatenate(tokens_grads)

    grad_attn = here.scatter_weights(
        jnp.concatenate(
            [
                outer(normed_one, d_query_low),
                outer(normed_one, d_kv_low),
                outer(both(d_branch), mixed),
            ],
            axis=1,
        )
    )
    grad_query = grad_attn[:, :q_cols]
    grad_kv_flat = grad_attn[:, q_cols : q_cols + kv_cols]
    grad_out = grad_attn[:, q_cols + kv_cols :].T

    low = lambda w: w.astype(BF16).astype(F32)
    gain_one = jnp.sum(low(query_weight) * grad_query, axis=1) + jnp.sum(
        low(kv_flat) * grad_kv_flat, axis=1
    )
    gain_two = jnp.sum(low(gate_weight) * grad_gate + low(up_weight) * grad_up, axis=1)
    grad_gains = here.sum_tp(jnp.stack([gain_one, gain_two])) / gains_low.astype(F32)
    grad_kv = grad_kv_flat.reshape(kv_weight.shape)

    out_fan = max(1, 4 * D // group_rows)
    query_new = adamw_step(query_weight, query_m, query_v, grad_query, D ** (-0.5), DECAY_RATE)
    kv_new = adamw_step(kv_weight, kv_m, kv_v, grad_kv, D ** (-0.5), DECAY_RATE)
    out_new = adamw_step(out_weight, out_m, out_v, grad_out, out_fan ** (-0.5), DECAY_RATE)
    gate_new = adamw_step(gate_weight, gate_m, gate_v, grad_gate, D ** (-0.5), DECAY_RATE)
    up_new = adamw_step(up_weight, up_m, up_v, grad_up, D ** (-0.5), DECAY_RATE)
    down_new = adamw_step(down_weight, down_m, down_v, grad_down, FF ** (-0.5), DECAY_RATE)
    gains_new = adamw_step(norm_gains, gains_m, gains_v, grad_gains, 0.5, 0.0)
    return (
        output,
        tokens_grad,
        *query_new,
        *kv_new,
        *out_new,
        *gate_new,
        *up_new,
        *down_new,
        *gains_new,
    )


def solution(mesh):
    fine = Mesh(mesh.devices.reshape(4, 2, 2, 2, 4), ("x", "yh", "c", "yl", "z"))
    rows = ("x", "yh", "c")
    tp = ("yl", "z")
    by_row, by_col, by_unit = P(rows, None), P(rows, tp), P(tp, rows)
    by_kv, by_gain = P(rows, tp, None), P(None, rows)
    in_specs = (
        (by_row,) * 2
        + (P(),) * 2
        + (by_col,) * 3
        + (by_kv,) * 3
        + (by_unit,) * 3
        + (by_col,) * 6
        + (by_unit,) * 3
        + (by_gain,) * 3
    )
    out_specs = (
        (by_row,) * 2
        + (by_col,) * 3
        + (by_kv,) * 3
        + (by_unit,) * 3
        + (by_col,) * 6
        + (by_unit,) * 3
        + (by_gain,) * 3
    )
    return jax.shard_map(
        per_device, mesh=fine, in_specs=in_specs, out_specs=out_specs, check_vma=False
    )
```

```python
import functools

import jax
import jax.numpy as jnp
from jax import lax
from jax.experimental import pallas as pl
from jax.experimental.pallas import tpu as pltpu
from jax.sharding import Mesh
from jax.sharding import PartitionSpec as P

D = 2048
HD = 64
FF = 8192
STEP = 5


NORM_EPS = 1e-05
BETA_FIRST = 0.9
BETA_SECOND = 0.95
ADAM_EPS = 1e-08
DECAY_RATE = 0.1
ROPE_BASE = 500000.0
MASKED_SCORE = -1e30

F32 = jnp.float32
BF16 = jnp.bfloat16
QB = 128
KB = 512


SWAP = ((0, 1), (1, 0))


def ring(step):
    return tuple((i, (i + step) % 4) for i in range(4))


def dot(a, b):
    return jnp.dot(a, b, preferred_element_type=F32)


def turn(value, cosine, sine):
    a, b = value[: HD // 2], value[HD // 2 :]
    return jnp.concatenate([a * cosine - b * sine, b * cosine + a * sine], axis=0)


def heads_to_lanes(wide, heads):
    return jnp.concatenate([wide[h * HD : (h + 1) * HD] for h in range(heads)], axis=1)


def lanes_to_heads(tall, heads):
    n = tall.shape[1] // heads
    return jnp.concatenate([tall[:, h * n : (h + 1) * n] for h in range(heads)], axis=0)


def normed_projections(tokens, gain, w_query, w_kv, cosine, sine, eps):
    rows, width = tokens.shape
    block = 256

    def kernel(t_ref, g_ref, wq_ref, wkv_ref, cos_ref, sin_ref, n_ref, q_ref, kv_ref):
        x = t_ref[...].astype(F32)
        inv = lax.rsqrt(jnp.mean(x * x, axis=-1, keepdims=True) + eps)
        normed = (x * inv * g_ref[...].astype(F32)).astype(BF16)
        n_ref[...] = normed
        q_ref[...] = dot(normed, wq_ref[...])
        kv = jnp.transpose(dot(normed, wkv_ref[...]))
        kv = jnp.concatenate([turn(kv[:HD], cos_ref[...], sin_ref[...]), kv[HD:]], axis=0)
        kv_ref[...] = jnp.transpose(kv).astype(BF16)

    whole = lambda a: pl.BlockSpec(a.shape, lambda i: (0,) * a.ndim)
    by_row = lambda w: pl.BlockSpec((block, w), lambda i: (i, 0))
    by_lane = pl.BlockSpec((HD // 2, block), lambda i: (0, i))
    return pl.pallas_call(
        kernel,
        grid=(rows // block,),
        in_specs=[by_row(width), whole(gain), whole(w_query), whole(w_kv), by_lane, by_lane],
        out_specs=[by_row(width), by_row(w_query.shape[1]), by_row(2 * HD)],
        out_shape=[
            jax.ShapeDtypeStruct((rows, width), BF16),
            jax.ShapeDtypeStruct((rows, w_query.shape[1]), F32),
            jax.ShapeDtypeStruct((rows, 2 * HD), BF16),
        ],
        cost_estimate=pl.CostEstimate(
            flops=rows * width * 384, bytes_accessed=4 << 20, transcendentals=0
        ),
        compiler_params=pltpu.CompilerParams(vmem_limit_bytes=32 << 20),
    )(tokens, gain, w_query, w_kv, cosine, sine)


def key_ranges(bounds_ref, step):
    return [bounds_ref[step * 4 + n] for n in range(4)]


def attention_forward(query_raw, kv, bounds, starts, slots, cosine, sine, row_offset, rows):
    heads = query_raw.shape[1] // HD
    keys = kv.shape[0]
    wide = heads * QB
    steps, base = rows // QB, row_offset // QB

    def kernel(b_ref, q_ref, kv_ref, start_ref, slot_ref, cos_ref, sin_ref, m_ref, qt_ref, ot_ref, lse_ref, kvt_ref, qp_ref):
        step = pl.program_id(0)

        @pl.when(step == 0)
        def _():
            kvt_ref[...] = jnp.transpose(kv_ref[...].astype(F32)).astype(BF16)

        raw = jnp.transpose(q_ref[...])
        turned = jnp.concatenate(
            [turn(raw[h * HD : (h + 1) * HD], cos_ref[...], sin_ref[...]) for h in range(heads)],
            axis=1,
        ).astype(BF16)
        qt_ref[0] = turned
        scaled = (turned.astype(F32) * HD**-0.5).astype(BF16)
        qp_ref[...] = jnp.concatenate([scaled, jnp.zeros_like(scaled)], axis=0)
        start = jnp.concatenate([start_ref[0]] * heads, axis=1)
        slot = jnp.concatenate([slot_ref[0]] * heads, axis=1)

        def body(masked, j, carry):
            peak, total, acc = carry
            at = pl.multiple_of(j * KB, KB)
            scores = dot(kv_ref[pl.ds(at, KB), :], qp_ref[...])
            if masked:
                key = at + lax.broadcasted_iota(jnp.int32, (KB, wide), 0)
                scores = jnp.where((key >= start) & (key <= slot), scores, MASKED_SCORE)
            new_peak = jnp.maximum(peak, jnp.max(scores, axis=0, keepdims=True))
            powers = jnp.exp(scores - new_peak)
            shrink = jnp.exp(peak - new_peak)
            total = total * shrink + jnp.sum(powers, axis=0, keepdims=True)
            values = kvt_ref[HD:, pl.ds(at, KB)]
            acc = acc * shrink + dot(values, powers.astype(BF16))
            return (new_peak, total, acc)

        first, full_first, full_end, end = key_ranges(b_ref, base + step)
        carry = (
            jnp.full((1, wide), MASKED_SCORE, F32),
            jnp.zeros((1, wide), F32),
            jnp.zeros((HD, wide), F32),
        )
        carry = lax.fori_loop(first, full_first, functools.partial(body, True), carry)
        carry = lax.fori_loop(full_first, full_end, functools.partial(body, False), carry)
        carry = lax.fori_loop(full_end, end, functools.partial(body, True), carry)
        peak, total, acc = carry
        mixed = acc / total
        ot_ref[0] = mixed
        lse_ref[0] = peak + jnp.log(total)
        m_ref[...] = jnp.transpose(lanes_to_heads(mixed, heads)).astype(BF16)

    lane = lambda: pl.BlockSpec((HD // 2, QB), lambda i: (0, base + i))
    row = lambda: pl.BlockSpec((1, 1, QB), lambda i: (base + i, 0, 0))
    return pl.pallas_call(
        kernel,
        grid=(steps,),
        in_specs=[
            pl.BlockSpec(memory_space=pltpu.SMEM),
            pl.BlockSpec((QB, heads * HD), lambda i: (base + i, 0)),
            pl.BlockSpec((keys, 2 * HD), lambda i: (0, 0)),
            row(),
            row(),
            lane(),
            lane(),
        ],
        out_specs=[
            pl.BlockSpec((QB, heads * HD), lambda i: (i, 0)),
            pl.BlockSpec((1, HD, wide), lambda i: (i, 0, 0)),
            pl.BlockSpec((1, HD, wide), lambda i: (i, 0, 0)),
            pl.BlockSpec((1, 1, wide), lambda i: (i, 0, 0)),
        ],
        out_shape=[
            jax.ShapeDtypeStruct((rows, heads * HD), BF16),
            jax.ShapeDtypeStruct((steps, HD, wide), BF16),
            jax.ShapeDtypeStruct((steps, HD, wide), F32),
            jax.ShapeDtypeStruct((steps, 1, wide), F32),
        ],
        scratch_shapes=[pltpu.VMEM((2 * HD, keys), BF16), pltpu.VMEM((2 * HD, wide), BF16)],
        cost_estimate=pl.CostEstimate(
            flops=rows * 2 * keys * heads * HD, bytes_accessed=2 << 20, transcendentals=0
        ),
        compiler_params=pltpu.CompilerParams(vmem_limit_bytes=32 << 20),
    )(bounds, query_raw, kv, starts, slots, cosine, sine)


def attention_backward(d_mixed, kv, queries, mixed, lse, bounds, starts, slots, cosine, sine):
    rows, width = d_mixed.shape
    heads = width // HD
    keys = kv.shape[0]
    wide = heads * QB
    steps = rows // QB

    def kernel(b_ref, d_ref, kv_ref, qt_ref, ot_ref, lse_ref, start_ref, slot_ref, cos_ref, sin_ref, dq_ref, dkv_ref, kvt_ref, qp_ref, dp_ref, qr_ref, dr_ref):
        step = pl.program_id(0)

        @pl.when(step == 0)
        def _():
            kvt_ref[...] = jnp.transpose(kv_ref[...].astype(F32)).astype(BF16)
            dkv_ref[...] = jnp.zeros_like(dkv_ref)

        scaled = qt_ref[0].astype(F32) * HD**-0.5
        grads = heads_to_lanes(jnp.transpose(d_ref[...].astype(F32)), heads)
        delta = jnp.sum(grads * ot_ref[0], axis=0, keepdims=True)
        empty = jnp.zeros_like(scaled)
        q_pad = jnp.concatenate([scaled, empty], axis=0)
        d_pad = jnp.concatenate([empty, grads], axis=0)
        qp_ref[...] = q_pad.astype(BF16)
        dp_ref[...] = d_pad.astype(BF16)
        qr_ref[...] = jnp.transpose(q_pad).astype(BF16)
        dr_ref[...] = jnp.transpose(d_pad).astype(BF16)
        start = jnp.concatenate([start_ref[0]] * heads, axis=1)
        slot = jnp.concatenate([slot_ref[0]] * heads, axis=1)
        log_total = lse_ref[0]

        def body(masked, j, d_query):
            at = pl.multiple_of(j * KB, KB)
            block = kv_ref[pl.ds(at, KB), :]
            scores = dot(block, qp_ref[...])
            if masked:
                key = at + lax.broadcasted_iota(jnp.int32, (KB, wide), 0)
                scores = jnp.where((key >= start) & (key <= slot), scores, MASKED_SCORE)
            chances = jnp.exp(scores - log_total)
            d_chances = dot(block, dp_ref[...])
            d_scores = (chances * (d_chances - delta)).astype(BF16)
            dkv_ref[pl.ds(at, KB), :] += dot(chances.astype(BF16), dr_ref[...]) + dot(
                d_scores, qr_ref[...]
            )
            return d_query + dot(kvt_ref[:HD, pl.ds(at, KB)], d_scores)

        first, full_first, full_end, end = key_ranges(b_ref, step)
        d_query = jnp.zeros((HD, wide), F32)
        d_query = lax.fori_loop(first, full_first, functools.partial(body, True), d_query)
        d_query = lax.fori_loop(full_first, full_end, functools.partial(body, False), d_query)
        d_query = lax.fori_loop(full_end, end, functools.partial(body, True), d_query)
        d_query = lanes_to_heads(d_query * HD**-0.5, heads)
        turned = jnp.concatenate(
            [turn(d_query[h * HD : (h + 1) * HD], cos_ref[...], -sin_ref[...]) for h in range(heads)],
            axis=0,
        )
        dq_ref[...] = jnp.transpose(turned).astype(BF16)

    lane = lambda: pl.BlockSpec((HD // 2, QB), lambda i: (0, i))
    row = lambda: pl.BlockSpec((1, 1, QB), lambda i: (i, 0, 0))
    kept = lambda n: pl.BlockSpec((1, n, wide), lambda i: (i, 0, 0))
    return pl.pallas_call(
        kernel,
        grid=(steps,),
        in_specs=[
            pl.BlockSpec(memory_space=pltpu.SMEM),
            pl.BlockSpec((QB, width), lambda i: (i, 0)),
            pl.BlockSpec((keys, 2 * HD), lambda i: (0, 0)),
            kept(HD),
            kept(HD),
            kept(1),
            row(),
            row(),
            lane(),
            lane(),
        ],
        out_specs=[
            pl.BlockSpec((QB, width), lambda i: (i, 0)),
            pl.BlockSpec((keys, 2 * HD), lambda i: (0, 0)),
        ],
        out_shape=[
            jax.ShapeDtypeStruct((rows, width), BF16),
            jax.ShapeDtypeStruct((keys, 2 * HD), F32),
        ],
        scratch_shapes=[
            pltpu.VMEM((2 * HD, keys), BF16),
            pltpu.VMEM((2 * HD, wide), BF16),
            pltpu.VMEM((2 * HD, wide), BF16),
            pltpu.VMEM((wide, 2 * HD), BF16),
            pltpu.VMEM((wide, 2 * HD), BF16),
        ],
        cost_estimate=pl.CostEstimate(
            flops=rows * 4 * keys * heads * HD, bytes_accessed=2 << 20, transcendentals=0
        ),
        compiler_params=pltpu.CompilerParams(vmem_limit_bytes=32 << 20),
    )(bounds, d_mixed, kv, queries, mixed, lse, starts, slots, cosine, sine)


def slot_tables(lengths, groups, group_id, first_slot, rows):
    seq_count = lengths.shape[0]
    seq_order = jnp.arange(seq_count, dtype=jnp.int32)
    same_group = groups[None, :] == groups[:, None]
    before = seq_order[None, :] < seq_order[:, None]
    begins = jnp.sum(jnp.where(same_group & before, lengths[None, :], 0), axis=1)
    ends = begins + lengths
    slots = first_slot + jnp.arange(rows, dtype=jnp.int32)
    inside = (
        (groups == group_id)[:, None]
        & (slots[None, :] >= begins[:, None])
        & (slots[None, :] < ends[:, None])
    )
    starts = jnp.where(
        jnp.any(inside, axis=0), jnp.sum(jnp.where(inside, begins[:, None], 0), axis=0), slots
    )
    return slots, starts


def block_bounds(slots, starts):
    first_row, last_row = slots[::QB], slots[QB - 1 :: QB]
    low, high = starts[::QB], starts[QB - 1 :: QB]
    first = low // KB
    end = last_row // KB + 1
    full_first = jnp.clip((high + KB - 1) // KB, first, end)
    full_end = jnp.clip((first_row + 1) // KB, full_first, end)
    return jnp.stack([first, full_first, full_end, end], axis=1).reshape(-1).astype(jnp.int32)


def adamw_step(weight, first, second, grad, rate, decay):
    first_new = BETA_FIRST * first + (1.0 - BETA_FIRST) * grad
    second_new = BETA_SECOND * second + (1.0 - BETA_SECOND) * grad * grad
    first_hat = first_new / (1.0 - BETA_FIRST**STEP)
    second_hat = second_new / (1.0 - BETA_SECOND**STEP)
    weight_new = weight - rate * (first_hat / (jnp.sqrt(second_hat) + ADAM_EPS) + decay * weight)
    return (first_new, second_new, weight_new)


def place(pieces, plan, table, out_shapes):
    moves = len(plan)
    size = sum(p.size * p.dtype.itemsize for p in pieces)

    def kernel(table_ref, *refs):
        count = len(pieces)
        sources, refs = refs[:count], refs[count:]
        outs, refs = refs[: len(out_shapes)], refs[len(out_shapes) :]
        held, into, back = refs[:count], refs[count], refs[count + 1]
        loads = [
            pltpu.make_async_copy(sources[i], held[i], into.at[i]) for i in range(count)
        ]
        for load in loads:
            load.start()
        stores = []
        for i in range(count):
            loads[i].wait()
            for piece, source_index, out, entry in plan:
                if piece != i:
                    continue
                source = held[i] if source_index is None else held[i].at[source_index]
                store = pltpu.make_async_copy(
                    source, outs[out].at[table_ref[entry]], back.at[len(stores)]
                )
                store.start()
                stores.append(store)
        for store in stores:
            store.wait()

    return pl.pallas_call(
        kernel,
        out_shape=[jax.ShapeDtypeStruct(s, BF16) for s in out_shapes],
        in_specs=[pl.BlockSpec(memory_space=pltpu.SMEM)]
        + [pl.BlockSpec(memory_space=pltpu.HBM)] * len(pieces),
        out_specs=[pl.BlockSpec(memory_space=pltpu.HBM)] * len(out_shapes),
        scratch_shapes=[pltpu.VMEM(p.shape, p.dtype) for p in pieces]
        + [pltpu.SemaphoreType.DMA((len(pieces),)), pltpu.SemaphoreType.DMA((moves,))],
        cost_estimate=pl.CostEstimate(flops=0, bytes_accessed=2 * size, transcendentals=0),
        compiler_params=pltpu.CompilerParams(vmem_limit_bytes=size + (2 << 20)),
    )(table, *pieces)


def outer_blocks(table, groups):
    lefts, rights, plan = [], [], []
    for pairs in groups:
        entry = []
        for left, right in pairs:
            spot = next((n for n, known in enumerate(lefts) if known is left), None)
            if spot is None:
                spot = len(lefts)
                lefts.append(left)
            entry.append((spot, len(rights)))
            rights.append(right)
        plan.append(entry)
    width = sum(pairs[0][1].shape[1] for pairs in groups)
    block = D // 16

    def kernel(table_ref, *refs):
        left_refs, refs = refs[: len(lefts)], refs[len(lefts) :]
        right_refs, (give_ref, keep_ref) = refs[: len(rights)], refs[len(rights) :]
        step = pl.program_id(0)
        turned = [jnp.transpose(r[...]) for r in left_refs]
        parts = []
        for entry in plan:
            part = None
            for spot, n in entry:
                term = dot(turned[spot], right_refs[n][...])
                part = term if part is None else part + term
            parts.append(part.astype(BF16))
        whole = parts[0] if len(parts) == 1 else jnp.concatenate(parts, axis=1)

        @pl.when(step < 8)
        def _():
            give_ref[...] = whole

        @pl.when(step >= 8)
        def _():
            keep_ref[...] = whole

    flops = sum(2 * left.shape[0] * D * right.shape[1] for g in groups for left, right in g)
    return pl.pallas_call(
        kernel,
        grid_spec=pltpu.PrefetchScalarGridSpec(
            num_scalar_prefetch=1,
            grid=(16,),
            in_specs=[pl.BlockSpec((v.shape[0], block), lambda i, t: (0, t[i])) for v in lefts]
            + [pl.BlockSpec(v.shape, lambda i, t: (0, 0)) for v in rights],
            out_specs=[
                pl.BlockSpec((block, width), lambda i, t: (jnp.minimum(i, 7), 0)),
                pl.BlockSpec((block, width), lambda i, t: (jnp.maximum(i - 8, 0), 0)),
            ],
        ),
        out_shape=[jax.ShapeDtypeStruct((8 * block, width), BF16)] * 2,
        cost_estimate=pl.CostEstimate(flops=flops, bytes_accessed=4 << 20, transcendentals=0),
        compiler_params=pltpu.CompilerParams(vmem_limit_bytes=32 << 20),
    )(table, *lefts, *rights)


def adamw_kernel(weight, first, second, keep, got, rate, flip):
    def kernel(w_ref, m_ref, v_ref, keep_ref, got_ref, m_out, v_out, w_out, sum_ref):
        grad = keep_ref[...] + got_ref[...].astype(F32)
        if flip:
            grad = jnp.transpose(grad)
        weight = w_ref[...]
        first_new, second_new, weight_new = adamw_step(
            weight, m_ref[...], v_ref[...], grad, rate, DECAY_RATE
        )
        m_out[...] = first_new
        v_out[...] = second_new
        w_out[...] = weight_new
        if flip:
            sum_ref[...] = jnp.zeros_like(sum_ref)
        else:
            sum_ref[...] = jnp.sum(weight.astype(BF16).astype(F32) * grad, axis=1, keepdims=True)

    shape = jax.ShapeDtypeStruct(weight.shape, F32)
    return pl.pallas_call(
        kernel,
        out_shape=[shape] * 3 + [jax.ShapeDtypeStruct((D // 16, 1), F32)],
        cost_estimate=pl.CostEstimate(
            flops=0, bytes_accessed=28 * weight.size, transcendentals=0
        ),
        compiler_params=pltpu.CompilerParams(vmem_limit_bytes=16 << 20),
    )(weight, first, second, keep, got)


def pick(blocks, axis, index):
    return lax.dynamic_index_in_dim(blocks, index, axis, keepdims=False)


class Here:
    def __init__(self):
        self.x, self.yh, self.c, self.yl, self.z = (
            lax.axis_index(a) for a in ("x", "yh", "c", "yl", "z")
        )

    def ztable(self):
        own = [self.yl * 4 + (self.z + k) % 4 for k in range(4)]
        other = [(1 - self.yl) * 4 + (self.z + k) % 4 for k in range(4)]
        return jnp.stack(own + other).astype(jnp.int32)

    def xtable(self):
        table = []
        for dc in range(2):
            core = self.c if dc == 0 else 1 - self.c
            for k in range(4):
                for dy in range(2):
                    yh = self.yh if dy == 0 else 1 - self.yh
                    table.append(((self.x + k) % 4) * 4 + yh * 2 + core)
        return jnp.stack(table).astype(jnp.int32)

    def gather_tp(self, own, z_first, table):
        n, w = own.shape
        if not z_first:
            pair = jnp.stack([own, lax.ppermute(own, "yl", SWAP)])
            pieces = [pair] + [lax.ppermute(pair, "z", ring(-k)) for k in (1, 2, 3)]
            plan = [(k, d, 0, 4 * d + k) for k in range(4) for d in range(2)]
        else:
            mine = [own] + [lax.ppermute(own, "z", ring(-k)) for k in (1, 2, 3)]
            theirs = [lax.ppermute(p, "yl", SWAP) for p in mine]
            pieces = mine + theirs
            plan = [(i, None, 0, i) for i in range(8)]
        return place(pieces, plan, table, [(8, n, w)])[0].reshape(8 * n, w)

    def scatter_tp(self, terms, z_first):
        w = terms.shape[1]
        blocks = terms.reshape(2, 4, -1, w)
        if z_first:
            got = [
                lax.ppermute(pick(blocks, 1, (self.z + k) % 4), "z", ring(k)) for k in (1, 2, 3)
            ]
            keep = pick(pick(blocks, 1, self.z), 0, self.yl).astype(F32)
            give = pick(pick(blocks, 1, self.z), 0, 1 - self.yl).astype(F32)
            for g in got:
                keep = keep + pick(g, 0, self.yl).astype(F32)
                give = give + pick(g, 0, 1 - self.yl).astype(F32)
            return keep + lax.ppermute(give.astype(BF16), "yl", SWAP).astype(F32)
        got = lax.ppermute(pick(blocks, 0, 1 - self.yl), "yl", SWAP)
        both = pick(blocks, 0, self.yl).astype(F32) + got.astype(F32)
        low = both.astype(BF16)
        total = pick(both, 0, self.z)
        for k in (1, 2, 3):
            total = total + lax.ppermute(pick(low, 0, (self.z + k) % 4), "z", ring(k)).astype(F32)
        return total

    def gather_weights(self, shard):
        pair = jnp.stack([shard, lax.ppermute(shard, "yh", SWAP)])
        mine = [pair] + [lax.ppermute(pair, "x", ring(-k)) for k in (1, 2, 3)]
        return mine + [lax.ppermute(p, "c", SWAP) for p in mine]

    def scatter_weights(self, give, keep):
        got = lax.ppermute(give, "c", SWAP)
        n = D // 8
        both = lambda k: keep[k * n : (k + 1) * n].astype(F32) + got[k * n : (k + 1) * n].astype(F32)
        total = both(0)
        for k in (1, 2, 3):
            total = total + lax.ppermute(both(k).astype(BF16), "x", ring(k)).astype(F32)
        back = lax.ppermute(total[n // 2 :].astype(BF16), "yh", SWAP)
        return total[: n // 2], back

    def gather_ctx(self, own):
        over = lax.ppermute(own, "yh", SWAP)
        pieces = [own, over, lax.ppermute(own, "c", SWAP), lax.ppermute(over, "c", SWAP)]
        table = jnp.stack(
            [
                self.yh * 2 + self.c,
                (1 - self.yh) * 2 + self.c,
                self.yh * 2 + 1 - self.c,
                (1 - self.yh) * 2 + 1 - self.c,
            ]
        ).astype(jnp.int32)
        n, w = own.shape
        plan = [(i, None, 0, i) for i in range(4)]
        return place(pieces, plan, table, [(4, n, w)])[0].reshape(4 * n, w)

    def scatter_ctx(self, terms):
        w = terms.shape[1]
        blocks = terms.reshape(2, 2, -1, w)
        got = lax.ppermute(pick(blocks, 1, 1 - self.c).astype(BF16), "c", SWAP)
        both = pick(blocks, 1, self.c) + got.astype(F32)
        give = pick(both, 0, 1 - self.yh).astype(BF16)
        return pick(both, 0, self.yh) + lax.ppermute(give, "yh", SWAP).astype(F32)

    def sum_tp(self, value):
        value = value + lax.ppermute(value, "yl", SWAP)
        got = [lax.ppermute(value, "z", ring(k)) for k in (1, 2, 3)]
        parts = jnp.stack([value] + got)
        order = jnp.stack([(self.z - j) % 4 for j in range(4)])
        return jnp.sum(jnp.take(parts, order, axis=0), axis=0)


def per_device(
    tokens,
    cotangent,
    lengths,
    groups,
    query_weight,
    query_m,
    query_v,
    kv_weight,
    kv_m,
    kv_v,
    out_weight,
    out_m,
    out_v,
    gate_weight,
    gate_m,
    gate_v,
    up_weight,
    up_m,
    up_v,
    down_weight,
    down_m,
    down_v,
    norm_gains,
    gains_m,
    gains_v,
):
    here = Here()
    row_count = tokens.shape[0]
    group_rows = row_count * 4
    group_id = here.x
    ctx_id = here.yh * 2 + here.c
    tp_id = here.yl * 4 + here.z
    half = row_count // 2
    part = half // 8
    ztable = here.ztable()
    xtable = here.xtable()

    kv_flat = kv_weight.reshape(D // 16, 2 * HD)
    attn_shard = jnp.concatenate([query_weight, kv_flat, out_weight.T], axis=1).astype(BF16)
    q_cols, kv_cols, o_cols = query_weight.shape[1], 2 * HD, out_weight.shape[0]
    cols = q_cols + kv_cols + o_cols
    gains_low = norm_gains.astype(BF16)
    gain_rows = jnp.zeros((16, cols), BF16).at[:2, : D // 16].set(gains_low)
    attn_pieces = here.gather_weights(jnp.concatenate([attn_shard, gain_rows], axis=0))
    plan = []
    for i in range(8):
        for d in range(2):
            entry = 2 * i + d
            rows = pl.ds(0, D // 16)
            plan.append((i, (d, rows, pl.ds(0, q_cols)), 0, entry))
            plan.append((i, (d, rows, pl.ds(q_cols, kv_cols)), 1, entry))
            plan.append((i, (d, rows, pl.ds(q_cols + kv_cols, o_cols)), 2, entry))
            plan.append((i, (d, pl.ds(D // 16, 16), pl.ds(0, D // 16)), 3, entry))
    w_query, w_kv, w_out, gain_blocks = place(
        attn_pieces,
        plan,
        xtable,
        [(16, D // 16, q_cols), (16, D // 16, kv_cols), (16, D // 16, o_cols), (16, 16, D // 16)],
    )
    w_query = w_query.reshape(D, q_cols)
    w_kv = w_kv.reshape(D, kv_cols)
    w_out = w_out.reshape(D, o_cols)
    gain_values = gain_blocks[:, :2].transpose(1, 0, 2).reshape(2, D).astype(F32)

    units = gate_weight.shape[1]
    ff_shard = jnp.stack([gate_weight, up_weight, down_weight.T]).astype(BF16)
    ff_shard, _ = lax.optimization_barrier((ff_shard, attn_pieces[1]))
    ff_pieces = here.gather_weights(ff_shard)
    plan = []
    for i in range(8):
        for d in range(2):
            for o in range(3):
                plan.append((i, (d, o), o, 2 * i + d))
    w_gate, w_up, w_down = (
        w.reshape(D, units) for w in place(ff_pieces, plan, xtable, [(16, D // 16, units)] * 3)
    )

    slots, starts = slot_tables(lengths, groups, group_id, ctx_id * row_count, row_count)
    frequency = ROPE_BASE ** (-2.0 * jnp.arange(HD // 2, dtype=F32) / HD)
    angles = frequency[:, None] * (slots - starts).astype(F32)[None, :]
    cosine, sine = jnp.cos(angles), jnp.sin(angles)
    bounds = block_bounds(slots, starts)
    slot_rows, start_rows = slots.reshape(-1, 1, QB), starts.reshape(-1, 1, QB)

    normed_one, query_raw, kv_local = normed_projections(
        tokens, gain_values[:1].astype(BF16), w_query, w_kv, cosine, sine, NORM_EPS
    )
    kv_whole = here.gather_ctx(kv_local)

    halves = (0, 1)
    z_first = (False, True)
    mixed_half, turned_half, raw_half, total_half = zip(
        *[
            attention_forward(
                query_raw, kv_whole, bounds, start_rows, slot_rows, cosine, sine, h * half, half
            )
            for h in halves
        ]
    )
    cotangent_half = [cotangent[:half], cotangent[half:]]
    own_start = [h * half + tp_id * part for h in halves]
    own_inputs = [
        lax.dynamic_slice_in_dim(tokens, s, part, axis=0).astype(F32) for s in own_start
    ]
    own_upstream = [
        lax.dynamic_slice_in_dim(cotangent, s, part, axis=0).astype(F32) for s in own_start
    ]

    hidden_one, inv_two, pre_two, normed_two = [], [], [], []
    for h in halves:
        term = jnp.einsum("ra,da->rd", mixed_half[h], w_out, preferred_element_type=F32)
        total = here.scatter_tp(term.astype(BF16), z_first[h])
        hidden_one.append(own_inputs[h] + total)
        inv_two.append(
            lax.rsqrt(jnp.mean(hidden_one[h] * hidden_one[h], axis=-1, keepdims=True) + NORM_EPS)
        )
        pre_two.append(hidden_one[h] * inv_two[h])
        own_normed = (pre_two[h] * gain_values[1]).astype(BF16)
        normed_two.append(here.gather_tp(own_normed, z_first[h], ztable))

    hidden, d_gate, d_up, d_hidden_one, d_branch = [], [], [], [], []
    for h in halves:
        gate_value = jnp.dot(normed_two[h], w_gate, preferred_element_type=F32)
        up_value = jnp.dot(normed_two[h], w_up, preferred_element_type=F32)
        d_hidden = jnp.dot(cotangent_half[h], w_down, preferred_element_type=F32)
        sigmoid_gate = jax.nn.sigmoid(gate_value)
        activated = gate_value * sigmoid_gate
        hidden.append((activated * up_value).astype(BF16))
        d_gate.append(
            (
                d_hidden * up_value * sigmoid_gate * (1.0 + gate_value * (1.0 - sigmoid_gate))
            ).astype(BF16)
        )
        d_up.append((d_hidden * activated).astype(BF16))
        d_two_term = jnp.einsum(
            "rf,df->rd", d_gate[h], w_gate, preferred_element_type=F32
        ) + jnp.einsum("rf,df->rd", d_up[h], w_up, preferred_element_type=F32)
        d_normed_two = here.scatter_tp(d_two_term.astype(BF16), z_first[h])
        scaled = d_normed_two * gain_values[1]
        d_through = inv_two[h] * (
            scaled - pre_two[h] * jnp.mean(scaled * pre_two[h], axis=-1, keepdims=True)
        )
        d_hidden_one.append(own_upstream[h] + d_through)
        d_branch.append(
            here.gather_tp(d_hidden_one[h].astype(BF16), z_first[h], ztable)
        )

    d_mixed = jnp.concatenate(
        [jnp.dot(d_branch[h], w_out, preferred_element_type=F32).astype(BF16) for h in halves]
    )

    outputs = []
    for h in halves:
        term = jnp.einsum("rf,df->rd", hidden[h], w_down, preferred_element_type=F32)
        total = here.scatter_tp(term.astype(BF16), z_first[h])
        own_out = (hidden_one[h] + total).astype(BF16)
        outputs.append(here.gather_tp(own_out, z_first[h], ztable))
    output = jnp.concatenate(outputs)

    order = here.xtable()
    order = jnp.concatenate([order[8:], order[:8]])
    pairs = lambda lefts, rights: [tuple(zip(lefts, rights))]
    gate_sum = here.scatter_weights(*outer_blocks(order, pairs(normed_two, d_gate)))
    up_sum = here.scatter_weights(*outer_blocks(order, pairs(normed_two, d_up)))
    down_sum = here.scatter_weights(*outer_blocks(order, pairs(cotangent_half, hidden)))

    d_query_low, d_kv = attention_backward(
        d_mixed,
        kv_whole,
        jnp.concatenate(turned_half),
        jnp.concatenate(raw_half),
        jnp.concatenate(total_half),
        bounds,
        start_rows,
        slot_rows,
        cosine,
        sine,
    )
    d_kv_own = here.scatter_ctx(d_kv).T
    d_kv_low = (
        jnp.concatenate([turn(d_kv_own[:HD], cosine, -sine), d_kv_own[HD:]], axis=0).T
    ).astype(BF16)

    tokens_grads = []
    for h in halves:
        rows = slice(h * half, (h + 1) * half)
        d_one_term = jnp.einsum(
            "ra,da->rd", d_query_low[rows], w_query, preferred_element_type=F32
        ) + jnp.einsum("rc,dc->rd", d_kv_low[rows], w_kv, preferred_element_type=F32)
        d_normed_one = here.scatter_tp(d_one_term.astype(BF16), z_first[h])
        own_inv = lax.rsqrt(
            jnp.mean(own_inputs[h] * own_inputs[h], axis=-1, keepdims=True) + NORM_EPS
        )
        pre_one = own_inputs[h] * own_inv
        scaled = d_normed_one * gain_values[0]
        d_through = own_inv * (
            scaled - pre_one * jnp.mean(scaled * pre_one, axis=-1, keepdims=True)
        )
        own_grad = (d_hidden_one[h] + d_through).astype(BF16)
        tokens_grads.append(here.gather_tp(own_grad, z_first[h], ztable))
    tokens_grad = jnp.concatenate(tokens_grads)

    attn_keep, attn_got = here.scatter_weights(
        *outer_blocks(
            order,
            [((normed_one, d_query_low),), ((normed_one, d_kv_low),)]
            + pairs(d_branch, mixed_half),
        )
    )
    columns = lambda low, high: (attn_keep[:, low:high], attn_got[:, low:high])
    flat = lambda v: v.reshape(kv_flat.shape)
    fan = D ** (-0.5)
    out_fan = max(1, 4 * D // group_rows) ** (-0.5)
    query_new = adamw_kernel(query_weight, query_m, query_v, *columns(0, q_cols), fan, False)
    kv_new = adamw_kernel(
        kv_flat, flat(kv_m), flat(kv_v), *columns(q_cols, q_cols + kv_cols), fan, False
    )
    out_new = adamw_kernel(
        out_weight, out_m, out_v, *columns(q_cols + kv_cols, cols), out_fan, True
    )
    gate_new = adamw_kernel(gate_weight, gate_m, gate_v, *gate_sum, fan, False)
    up_new = adamw_kernel(up_weight, up_m, up_v, *up_sum, fan, False)
    down_new = adamw_kernel(down_weight, down_m, down_v, *down_sum, FF ** (-0.5), True)

    gain_sums = jnp.stack([query_new[3] + kv_new[3], gate_new[3] + up_new[3]])[:, :, 0]
    grad_gains = here.sum_tp(gain_sums) / gains_low.astype(F32)
    gains_new = adamw_step(norm_gains, gains_m, gains_v, grad_gains, 0.5, 0.0)
    return (
        output,
        tokens_grad,
        *query_new[:3],
        *[v.reshape(kv_weight.shape) for v in kv_new[:3]],
        *out_new[:3],
        *gate_new[:3],
        *up_new[:3],
        *down_new[:3],
        *gains_new,
    )


def solution(mesh):
    fine = Mesh(mesh.devices.reshape(4, 2, 2, 2, 4), ("x", "yh", "c", "yl", "z"))
    rows = ("x", "yh", "c")
    tp = ("yl", "z")
    by_row, by_col, by_unit = P(rows, None), P(rows, tp), P(tp, rows)
    by_kv, by_gain = P(rows, tp, None), P(None, rows)
    in_specs = (
        (by_row,) * 2
        + (P(),) * 2
        + (by_col,) * 3
        + (by_kv,) * 3
        + (by_unit,) * 3
        + (by_col,) * 6
        + (by_unit,) * 3
        + (by_gain,) * 3
    )
    out_specs = (
        (by_row,) * 2
        + (by_col,) * 3
        + (by_kv,) * 3
        + (by_unit,) * 3
        + (by_col,) * 6
        + (by_unit,) * 3
        + (by_gain,) * 3
    )
    return jax.shard_map(
        per_device, mesh=fine, in_specs=in_specs, out_specs=out_specs, check_vma=False
    )
```

```python
import functools

import jax
import jax.numpy as jnp
from jax import lax
from jax.experimental import pallas as pl
from jax.experimental.pallas import tpu as pltpu
from jax.sharding import Mesh
from jax.sharding import PartitionSpec as P

D = 2048
HD = 64
FF = 8192
STEP = 5


NORM_EPS = 1e-05
BETA_FIRST = 0.9
BETA_SECOND = 0.95
ADAM_EPS = 1e-08
DECAY_RATE = 0.1
ROPE_BASE = 500000.0
MASKED_SCORE = -1e30

F32 = jnp.float32
BF16 = jnp.bfloat16
QB = 128
KB = 512


SWAP = ((0, 1), (1, 0))


def ring(step):
    return tuple((i, (i + step) % 4) for i in range(4))


def dot(a, b):
    return jnp.dot(a, b, preferred_element_type=F32)


def turn(value, cosine, sine):
    a, b = value[: HD // 2], value[HD // 2 :]
    return jnp.concatenate([a * cosine - b * sine, b * cosine + a * sine], axis=0)


def heads_to_lanes(wide, heads):
    return jnp.concatenate([wide[h * HD : (h + 1) * HD] for h in range(heads)], axis=1)


def lanes_to_heads(tall, heads):
    n = tall.shape[1] // heads
    return jnp.concatenate([tall[:, h * n : (h + 1) * n] for h in range(heads)], axis=0)


def normed_projections(tokens, pieces, table, widths, cosine, sine, eps, deps=()):
    rows, width = tokens.shape
    block, part = 256, D // 16
    q_cols, kv_cols, o_cols = widths
    deps = [token(d) for d in deps]
    count = len(pieces)

    def kernel(table_ref, t_ref, *refs):
        piece_refs, refs = refs[:count], refs[count:]
        cos_ref, sin_ref, n_ref, q_ref, kv_ref, wq_ref, wkv_ref, wo_ref, g_ref = refs

        @pl.when(pl.program_id(0) == 0)
        def _():
            for i in range(count):
                for d in range(2):
                    spot = table_ref[2 * i + d]
                    at = pl.ds(pl.multiple_of(spot * part, part), part)
                    body = piece_refs[i][d, :part, :]
                    wq_ref[at, :] = body[:, :q_cols]
                    wkv_ref[at, :] = body[:, q_cols : q_cols + kv_cols]
                    wo_ref[at, :] = body[:, q_cols + kv_cols :]
                    g_ref[:, at] = piece_refs[i][d, part:, :part].astype(F32)[:8]

        x = t_ref[...].astype(F32)
        inv = lax.rsqrt(jnp.mean(x * x, axis=-1, keepdims=True) + eps)
        normed = (x * inv * g_ref[:1, :]).astype(BF16)
        n_ref[...] = normed
        q_ref[...] = dot(normed, wq_ref[...])
        kv = jnp.transpose(dot(normed, wkv_ref[...]))
        kv = jnp.concatenate([turn(kv[:HD], cos_ref[...], sin_ref[...]), kv[HD:]], axis=0)
        kv_ref[...] = jnp.transpose(kv).astype(BF16)

    whole = lambda *shape: pl.BlockSpec(shape, lambda i: (0,) * len(shape))
    by_row = lambda w: pl.BlockSpec((block, w), lambda i: (i, 0))
    by_lane = pl.BlockSpec((HD // 2, block), lambda i: (0, i))
    return pl.pallas_call(
        after(kernel, 4 + count, deps),
        grid=(rows // block,),
        in_specs=[pl.BlockSpec(memory_space=pltpu.SMEM), by_row(width)]
        + [whole(*p.shape) for p in pieces]
        + [by_lane, by_lane]
        + any_specs(len(deps)),
        out_specs=[
            by_row(width),
            by_row(q_cols),
            by_row(kv_cols),
            whole(D, q_cols),
            whole(D, kv_cols),
            whole(D, o_cols),
            whole(8, D),
        ],
        out_shape=[
            jax.ShapeDtypeStruct((rows, width), BF16),
            jax.ShapeDtypeStruct((rows, q_cols), F32),
            jax.ShapeDtypeStruct((rows, kv_cols), BF16),
            jax.ShapeDtypeStruct((D, q_cols), BF16),
            jax.ShapeDtypeStruct((D, kv_cols), BF16),
            jax.ShapeDtypeStruct((D, o_cols), BF16),
            jax.ShapeDtypeStruct((8, D), F32),
        ],
        cost_estimate=pl.CostEstimate(
            flops=2 * rows * width * 384, bytes_accessed=12 << 20, transcendentals=0
        ),
        compiler_params=pltpu.CompilerParams(vmem_limit_bytes=40 << 20),
    )(table, tokens, *pieces, cosine, sine, *deps)


def key_ranges(bounds_ref, step):
    return [bounds_ref[step * 4 + n] for n in range(4)]


def attention_forward(query_raw, kv, bounds, starts, slots, cosine, sine, row_offset, rows):
    heads = query_raw.shape[1] // HD
    keys = kv.shape[0]
    wide = heads * QB
    steps, base = rows // QB, row_offset // QB

    def kernel(b_ref, q_ref, kv_ref, start_ref, slot_ref, cos_ref, sin_ref, m_ref, qt_ref, ot_ref, lse_ref, kvt_ref, qp_ref):
        step = pl.program_id(0)

        @pl.when(step == 0)
        def _():
            kvt_ref[...] = jnp.transpose(kv_ref[...].astype(F32)).astype(BF16)

        raw = jnp.transpose(q_ref[...])
        turned = jnp.concatenate(
            [turn(raw[h * HD : (h + 1) * HD], cos_ref[...], sin_ref[...]) for h in range(heads)],
            axis=1,
        ).astype(BF16)
        qt_ref[0] = turned
        scaled = (turned.astype(F32) * HD**-0.5).astype(BF16)
        qp_ref[...] = jnp.concatenate([scaled, jnp.zeros_like(scaled)], axis=0)
        start = jnp.concatenate([start_ref[0]] * heads, axis=1)
        slot = jnp.concatenate([slot_ref[0]] * heads, axis=1)

        def body(masked, j, carry):
            peak, total, acc = carry
            at = pl.multiple_of(j * KB, KB)
            scores = dot(kv_ref[pl.ds(at, KB), :], qp_ref[...])
            if masked:
                key = at + lax.broadcasted_iota(jnp.int32, (KB, wide), 0)
                scores = jnp.where((key >= start) & (key <= slot), scores, MASKED_SCORE)
            new_peak = jnp.maximum(peak, jnp.max(scores, axis=0, keepdims=True))
            powers = jnp.exp(scores - new_peak)
            shrink = jnp.exp(peak - new_peak)
            total = total * shrink + jnp.sum(powers, axis=0, keepdims=True)
            values = kvt_ref[HD:, pl.ds(at, KB)]
            acc = acc * shrink + dot(values, powers.astype(BF16))
            return (new_peak, total, acc)

        first, full_first, full_end, end = key_ranges(b_ref, base + step)
        carry = (
            jnp.full((1, wide), MASKED_SCORE, F32),
            jnp.zeros((1, wide), F32),
            jnp.zeros((HD, wide), F32),
        )
        carry = lax.fori_loop(first, full_first, functools.partial(body, True), carry)
        carry = lax.fori_loop(full_first, full_end, functools.partial(body, False), carry)
        carry = lax.fori_loop(full_end, end, functools.partial(body, True), carry)
        peak, total, acc = carry
        mixed = acc / total
        ot_ref[0] = mixed
        lse_ref[0] = peak + jnp.log(total)
        m_ref[...] = jnp.transpose(lanes_to_heads(mixed, heads)).astype(BF16)

    lane = lambda: pl.BlockSpec((HD // 2, QB), lambda i: (0, base + i))
    row = lambda: pl.BlockSpec((1, 1, QB), lambda i: (base + i, 0, 0))
    return pl.pallas_call(
        kernel,
        grid=(steps,),
        in_specs=[
            pl.BlockSpec(memory_space=pltpu.SMEM),
            pl.BlockSpec((QB, heads * HD), lambda i: (base + i, 0)),
            pl.BlockSpec((keys, 2 * HD), lambda i: (0, 0)),
            row(),
            row(),
            lane(),
            lane(),
        ],
        out_specs=[
            pl.BlockSpec((QB, heads * HD), lambda i: (i, 0)),
            pl.BlockSpec((1, HD, wide), lambda i: (i, 0, 0)),
            pl.BlockSpec((1, HD, wide), lambda i: (i, 0, 0)),
            pl.BlockSpec((1, 1, wide), lambda i: (i, 0, 0)),
        ],
        out_shape=[
            jax.ShapeDtypeStruct((rows, heads * HD), BF16),
            jax.ShapeDtypeStruct((steps, HD, wide), BF16),
            jax.ShapeDtypeStruct((steps, HD, wide), F32),
            jax.ShapeDtypeStruct((steps, 1, wide), F32),
        ],
        scratch_shapes=[pltpu.VMEM((2 * HD, keys), BF16), pltpu.VMEM((2 * HD, wide), BF16)],
        cost_estimate=pl.CostEstimate(
            flops=rows * 2 * keys * heads * HD, bytes_accessed=2 << 20, transcendentals=0
        ),
        compiler_params=pltpu.CompilerParams(vmem_limit_bytes=32 << 20),
    )(bounds, query_raw, kv, starts, slots, cosine, sine)


def attention_backward(
    d_mixed, kv, queries, mixed, lse, bounds, starts, slots, cosine, sine, deps=()
):
    rows, width = d_mixed.shape
    heads = width // HD
    keys = kv.shape[0]
    wide = heads * QB
    steps = rows // QB
    deps = [token(d) for d in deps]

    def kernel(b_ref, d_ref, kv_ref, qt_ref, ot_ref, lse_ref, start_ref, slot_ref, cos_ref, sin_ref, dq_ref, dkv_ref, kvt_ref, qp_ref, dp_ref, qr_ref, dr_ref):
        step = pl.program_id(0)

        @pl.when(step == 0)
        def _():
            kvt_ref[...] = jnp.transpose(kv_ref[...].astype(F32)).astype(BF16)
            dkv_ref[...] = jnp.zeros_like(dkv_ref)

        scaled = qt_ref[0].astype(F32) * HD**-0.5
        grads = heads_to_lanes(jnp.transpose(d_ref[...].astype(F32)), heads)
        delta = jnp.sum(grads * ot_ref[0], axis=0, keepdims=True)
        empty = jnp.zeros_like(scaled)
        q_pad = jnp.concatenate([scaled, empty], axis=0)
        d_pad = jnp.concatenate([empty, grads], axis=0)
        qp_ref[...] = q_pad.astype(BF16)
        dp_ref[...] = d_pad.astype(BF16)
        qr_ref[...] = jnp.transpose(q_pad).astype(BF16)
        dr_ref[...] = jnp.transpose(d_pad).astype(BF16)
        start = jnp.concatenate([start_ref[0]] * heads, axis=1)
        slot = jnp.concatenate([slot_ref[0]] * heads, axis=1)
        log_total = lse_ref[0]

        def body(masked, j, d_query):
            at = pl.multiple_of(j * KB, KB)
            block = kv_ref[pl.ds(at, KB), :]
            scores = dot(block, qp_ref[...])
            if masked:
                key = at + lax.broadcasted_iota(jnp.int32, (KB, wide), 0)
                scores = jnp.where((key >= start) & (key <= slot), scores, MASKED_SCORE)
            chances = jnp.exp(scores - log_total)
            d_chances = dot(block, dp_ref[...])
            d_scores = (chances * (d_chances - delta)).astype(BF16)
            dkv_ref[pl.ds(at, KB), :] += dot(chances.astype(BF16), dr_ref[...]) + dot(
                d_scores, qr_ref[...]
            )
            return d_query + dot(kvt_ref[:HD, pl.ds(at, KB)], d_scores)

        first, full_first, full_end, end = key_ranges(b_ref, step)
        d_query = jnp.zeros((HD, wide), F32)
        d_query = lax.fori_loop(first, full_first, functools.partial(body, True), d_query)
        d_query = lax.fori_loop(full_first, full_end, functools.partial(body, False), d_query)
        d_query = lax.fori_loop(full_end, end, functools.partial(body, True), d_query)
        d_query = lanes_to_heads(d_query * HD**-0.5, heads)
        turned = jnp.concatenate(
            [turn(d_query[h * HD : (h + 1) * HD], cos_ref[...], -sin_ref[...]) for h in range(heads)],
            axis=0,
        )
        dq_ref[...] = jnp.transpose(turned).astype(BF16)

    lane = lambda: pl.BlockSpec((HD // 2, QB), lambda i: (0, i))
    row = lambda: pl.BlockSpec((1, 1, QB), lambda i: (i, 0, 0))
    kept = lambda n: pl.BlockSpec((1, n, wide), lambda i: (i, 0, 0))
    return pl.pallas_call(
        after(kernel, 10, deps),
        grid=(steps,),
        in_specs=[
            pl.BlockSpec(memory_space=pltpu.SMEM),
            pl.BlockSpec((QB, width), lambda i: (i, 0)),
            pl.BlockSpec((keys, 2 * HD), lambda i: (0, 0)),
            kept(HD),
            kept(HD),
            kept(1),
            row(),
            row(),
            lane(),
            lane(),
        ]
        + any_specs(len(deps)),
        out_specs=[
            pl.BlockSpec((QB, width), lambda i: (i, 0)),
            pl.BlockSpec((keys, 2 * HD), lambda i: (0, 0)),
        ],
        out_shape=[
            jax.ShapeDtypeStruct((rows, width), BF16),
            jax.ShapeDtypeStruct((keys, 2 * HD), F32),
        ],
        scratch_shapes=[
            pltpu.VMEM((2 * HD, keys), BF16),
            pltpu.VMEM((2 * HD, wide), BF16),
            pltpu.VMEM((2 * HD, wide), BF16),
            pltpu.VMEM((wide, 2 * HD), BF16),
            pltpu.VMEM((wide, 2 * HD), BF16),
        ],
        cost_estimate=pl.CostEstimate(
            flops=rows * 2 * keys * heads * HD, bytes_accessed=2 << 20, transcendentals=0
        ),
        compiler_params=pltpu.CompilerParams(vmem_limit_bytes=32 << 20),
    )(bounds, d_mixed, kv, queries, mixed, lse, starts, slots, cosine, sine, *deps)


def keys_split(d_kv, core, deps=()):
    rows, width = d_kv.shape
    quarter = rows // 4
    deps = [token(d) for d in deps]

    def kernel(core_ref, d_ref, give_ref, keep_ref):
        core = core_ref[0]
        for n in range(2):
            give_at = pl.multiple_of((2 * n + 1 - core) * quarter, quarter)
            keep_at = pl.multiple_of((2 * n + core) * quarter, quarter)
            give_ref[n] = d_ref[pl.ds(give_at, quarter), :].astype(BF16)
            keep_ref[n] = d_ref[pl.ds(keep_at, quarter), :]

    shape = (2, quarter, width)
    return pl.pallas_call(
        after(kernel, 2, deps),
        out_shape=[jax.ShapeDtypeStruct(shape, BF16), jax.ShapeDtypeStruct(shape, F32)],
        in_specs=[pl.BlockSpec(memory_space=pltpu.SMEM), pl.BlockSpec(memory_space=pltpu.VMEM)]
        + any_specs(len(deps)),
        cost_estimate=pl.CostEstimate(flops=0, bytes_accessed=2 << 20, transcendentals=0),
    )(core, d_kv, *deps)


def keys_back(keep, got, cosine, sine, deps=()):
    deps = [token(d) for d in deps]

    def kernel(keep_ref, got_ref, cos_ref, sin_ref, out_ref):
        total = jnp.transpose(keep_ref[...] + got_ref[...].astype(F32))
        turned = turn(total[:HD], cos_ref[...], -sin_ref[...])
        out_ref[...] = jnp.transpose(jnp.concatenate([turned, total[HD:]], axis=0)).astype(BF16)

    return pl.pallas_call(
        after(kernel, 4, deps),
        out_shape=jax.ShapeDtypeStruct(keep.shape, BF16),
        in_specs=[pl.BlockSpec(memory_space=pltpu.VMEM)] * 4 + any_specs(len(deps)),
        cost_estimate=pl.CostEstimate(flops=0, bytes_accessed=2 << 20, transcendentals=0),
    )(keep, got, cosine, sine, *deps)


def slot_tables(lengths, groups, group_id, first_slot, rows):
    seq_count = lengths.shape[0]
    seq_order = jnp.arange(seq_count, dtype=jnp.int32)
    same_group = groups[None, :] == groups[:, None]
    before = seq_order[None, :] < seq_order[:, None]
    begins = jnp.sum(jnp.where(same_group & before, lengths[None, :], 0), axis=1)
    ends = begins + lengths
    slots = first_slot + jnp.arange(rows, dtype=jnp.int32)
    inside = (
        (groups == group_id)[:, None]
        & (slots[None, :] >= begins[:, None])
        & (slots[None, :] < ends[:, None])
    )
    starts = jnp.where(
        jnp.any(inside, axis=0), jnp.sum(jnp.where(inside, begins[:, None], 0), axis=0), slots
    )
    return slots, starts


def block_bounds(slots, starts):
    first_row, last_row = slots[::QB], slots[QB - 1 :: QB]
    low, high = starts[::QB], starts[QB - 1 :: QB]
    first = low // KB
    end = last_row // KB + 1
    full_first = jnp.clip((high + KB - 1) // KB, first, end)
    full_end = jnp.clip((first_row + 1) // KB, full_first, end)
    return jnp.stack([first, full_first, full_end, end], axis=1).reshape(-1).astype(jnp.int32)


def adamw_step(weight, first, second, grad, rate, decay):
    first_new = BETA_FIRST * first + (1.0 - BETA_FIRST) * grad
    second_new = BETA_SECOND * second + (1.0 - BETA_SECOND) * grad * grad
    first_hat = first_new / (1.0 - BETA_FIRST**STEP)
    second_hat = second_new / (1.0 - BETA_SECOND**STEP)
    weight_new = weight - rate * (first_hat / (jnp.sqrt(second_hat) + ADAM_EPS) + decay * weight)
    return (first_new, second_new, weight_new)


def token(array):
    return lax.slice(array, (0,) * array.ndim, (1,) * (array.ndim - 2) + (8, 128))


def after(kernel, inputs, deps):
    count = len(deps)
    if not count:
        return kernel
    return lambda *refs: kernel(*refs[:inputs], *refs[inputs + count :])


def any_specs(count):
    return [pl.BlockSpec(memory_space=pl.ANY)] * count


def tie(value, deps):
    deps = [token(d) for d in deps]
    return pl.pallas_call(
        lambda *refs: None,
        out_shape=jax.ShapeDtypeStruct(value.shape, value.dtype),
        in_specs=any_specs(1 + len(deps)),
        out_specs=pl.BlockSpec(memory_space=pl.ANY),
        input_output_aliases={0: 0},
    )(value, *deps)


def lay(pieces, plan, table, blocks, outputs=1, deps=(), weight=1):
    deps = [token(d) for d in deps]
    n, w = pieces[0].shape[-2:]
    inputs = 1 + len(pieces)

    def kernel(table_ref, *refs):
        out_refs = refs[len(pieces) :]
        for piece, index, out, entry in plan:
            source = refs[piece]
            out_refs[out][table_ref[entry]] = source[...] if index is None else source[index]

    size = sum(p.size * p.dtype.itemsize for p in pieces)
    return pl.pallas_call(
        after(kernel, inputs, deps),
        out_shape=[jax.ShapeDtypeStruct((blocks, n, w), BF16)] * outputs,
        in_specs=[pl.BlockSpec(memory_space=pltpu.SMEM)]
        + [pl.BlockSpec(memory_space=pltpu.VMEM)] * len(pieces)
        + any_specs(len(deps)),
        out_specs=[pl.BlockSpec(memory_space=pltpu.VMEM)] * outputs,
        cost_estimate=pl.CostEstimate(flops=0, bytes_accessed=2 * weight * size, transcendentals=0),
        compiler_params=pltpu.CompilerParams(vmem_limit_bytes=3 * size + (4 << 20)),
    )(table, *pieces, *deps)


def tie_small(value, late):
    def kernel(value_ref, out_ref):
        out_ref[...] = value_ref[...]

    return in_vmem(kernel, [value], [jax.ShapeDtypeStruct(value.shape, F32)], [late])[0]


def in_vmem(kernel, inputs, out_shape, deps=(), weight=1):
    deps = [token(d) for d in deps]
    count = len(inputs)
    size = sum(v.size * v.dtype.itemsize for v in list(inputs) + list(out_shape))
    return pl.pallas_call(
        after(kernel, count, deps),
        out_shape=out_shape,
        in_specs=[pl.BlockSpec(memory_space=pltpu.VMEM)] * len(inputs) + any_specs(len(deps)),
        out_specs=[pl.BlockSpec(memory_space=pltpu.VMEM)] * len(out_shape),
        cost_estimate=pl.CostEstimate(flops=0, bytes_accessed=weight * size, transcendentals=0),
        compiler_params=pltpu.CompilerParams(vmem_limit_bytes=2 * size + (8 << 20)),
    )(*inputs, *deps)


def join(arrays, deps=()):
    arrays = list(arrays)

    def kernel(*refs):
        for n in range(len(arrays)):
            refs[-1][n] = refs[n][...]

    shape = (len(arrays),) + arrays[0].shape
    return in_vmem(kernel, arrays, [jax.ShapeDtypeStruct(shape, BF16)], deps)[0]


def rms_inverse(value):
    return lax.rsqrt(jnp.mean(value * value, axis=-1, keepdims=True) + NORM_EPS)


def through_norm(d_normed, value, gain):
    inverse = rms_inverse(value)
    scaled = d_normed * gain
    pre = value * inverse
    return inverse * (scaled - pre * jnp.mean(scaled * pre, axis=-1, keepdims=True))


def feed_forward(normed, upstream, weights, order):
    rows, units, block = normed.shape[0], weights.shape[2], normed.shape[0] // 2
    part = D // 16

    def across(a, b):
        return lax.dot_general(a, b, (((1,), (1,)), ((), ())), preferred_element_type=F32)

    def kernel(order_ref, n_ref, u_ref, w_ref, hid_ref, dg_ref, du_ref, dn_ref, ff_ref, ng_ref, nk_ref, ug_ref, uk_ref):
        for i in range(16):
            at = pl.ds(pl.multiple_of(order_ref[i] * part, part), part)
            to = slice((i % 8) * part, (i % 8 + 1) * part)
            (ng_ref if i < 8 else nk_ref)[:, to] = n_ref[:, at]
            (ug_ref if i < 8 else uk_ref)[:, to] = u_ref[:, at]
        for f in range(0, units, 256):
            at = slice(f, f + 256)
            gate = dot(n_ref[...], w_ref[0, :, at])
            up = dot(n_ref[...], w_ref[1, :, at])
            d_hidden = dot(u_ref[...], w_ref[2, :, at])
            sigmoid = jax.nn.sigmoid(gate)
            activated = gate * sigmoid
            hid_ref[:, at] = (activated * up).astype(BF16)
            dg_ref[:, at] = (
                d_hidden * up * sigmoid * (1.0 + gate * (1.0 - sigmoid))
            ).astype(BF16)
            du_ref[:, at] = (d_hidden * activated).astype(BF16)
        for d in range(0, D, 512):
            at = slice(d, d + 512)
            dn_ref[:, at] = (
                across(dg_ref[...], w_ref[0, at, :]) + across(du_ref[...], w_ref[1, at, :])
            ).astype(BF16)
            ff_ref[:, at] = across(hid_ref[...], w_ref[2, at, :]).astype(BF16)

    by_row = lambda w: pl.BlockSpec((block, w), lambda i: (i, 0))
    shape = lambda w: jax.ShapeDtypeStruct((rows, w), BF16)
    return pl.pallas_call(
        kernel,
        grid=(rows // block,),
        in_specs=[
            pl.BlockSpec(memory_space=pltpu.SMEM),
            by_row(D),
            by_row(D),
            pl.BlockSpec(weights.shape, lambda i: (0, 0, 0), pipeline_mode=pl.Buffered(1)),
        ],
        out_specs=[by_row(units)] * 3 + [by_row(D)] * 2 + [by_row(D // 2)] * 4,
        out_shape=[shape(units)] * 3 + [shape(D)] * 2 + [shape(D // 2)] * 4,
        cost_estimate=pl.CostEstimate(
            flops=12 * rows * D * units, bytes_accessed=24 << 20, transcendentals=0
        ),
        compiler_params=pltpu.CompilerParams(vmem_limit_bytes=58 << 20),
    )(order, normed, upstream, weights)


def outer_blocks(table, groups):
    lefts, rights, plan = [], [], []
    for pairs in groups:
        entry = []
        for left, right in pairs:
            spot = next((n for n, known in enumerate(lefts) if known is left), None)
            if spot is None:
                spot = len(lefts)
                lefts.append(left)
            entry.append((spot, len(rights)))
            rights.append(right)
        plan.append(entry)
    width = sum(pairs[0][1].shape[1] for pairs in groups)
    block = D // 16

    def kernel(table_ref, *refs):
        left_refs, refs = refs[: len(lefts)], refs[len(lefts) :]
        right_refs, (give_ref, keep_ref) = refs[: len(rights)], refs[len(rights) :]
        step = pl.program_id(0)
        turned = [jnp.transpose(r[...]) for r in left_refs]
        parts = []
        for entry in plan:
            part = None
            for spot, n in entry:
                term = dot(turned[spot], right_refs[n][...])
                part = term if part is None else part + term
            parts.append(part.astype(BF16))
        whole = parts[0] if len(parts) == 1 else jnp.concatenate(parts, axis=1)

        @pl.when(step < 8)
        def _():
            give_ref[...] = whole

        @pl.when(step >= 8)
        def _():
            keep_ref[...] = whole

    flops = sum(2 * left.shape[0] * D * right.shape[1] for g in groups for left, right in g)
    return pl.pallas_call(
        kernel,
        grid_spec=pltpu.PrefetchScalarGridSpec(
            num_scalar_prefetch=1,
            grid=(16,),
            in_specs=[pl.BlockSpec((v.shape[0], block), lambda i, t: (0, t[i])) for v in lefts]
            + [pl.BlockSpec(v.shape, lambda i, t: (0, 0)) for v in rights],
            out_specs=[
                pl.BlockSpec((block, width), lambda i, t: (jnp.minimum(i, 7), 0)),
                pl.BlockSpec((block, width), lambda i, t: (jnp.maximum(i - 8, 0), 0)),
            ],
        ),
        out_shape=[jax.ShapeDtypeStruct((8 * block, width), BF16)] * 2,
        cost_estimate=pl.CostEstimate(flops=flops, bytes_accessed=4 << 20, transcendentals=0),
        compiler_params=pltpu.CompilerParams(vmem_limit_bytes=32 << 20),
    )(table, *lefts, *rights)


def fold_core(keeps, gots, deps=()):
    count, pair = len(keeps), D // 8
    widths = [k.shape[1] for k in keeps]
    starts = [sum(widths[:n]) for n in range(count)]
    deps = [token(d) for d in deps]

    def kernel(*refs):
        keep_refs, got_refs, outs = refs[:count], refs[count : 2 * count], refs[2 * count :]
        for k in range(4):

            @pl.when(pl.program_id(0) == k)
            def _():
                for n in range(count):
                    total = keep_refs[n][...].astype(F32) + got_refs[n][...].astype(F32)
                    to = slice(starts[n], starts[n] + widths[n])
                    outs[k][:, to] = total.astype(outs[k].dtype)

    whole = pl.BlockSpec((pair, sum(widths)), lambda i: (0, 0))
    shape = lambda dtype: jax.ShapeDtypeStruct((pair, sum(widths)), dtype)
    return pl.pallas_call(
        after(kernel, 2 * count, deps),
        grid=(4,),
        in_specs=[pl.BlockSpec((pair, w), lambda i: (i, 0)) for w in widths * 2]
        + any_specs(len(deps)),
        out_specs=[whole] * 4,
        out_shape=[shape(F32)] + [shape(BF16)] * 3,
        cost_estimate=pl.CostEstimate(
            flops=0, bytes_accessed=12 * pair * sum(widths), transcendentals=0
        ),
        compiler_params=pltpu.CompilerParams(vmem_limit_bytes=40 << 20),
    )(*keeps, *gots, *deps)


def adamw_kernel(weight, first, second, sums, spot, rate, flip):
    def kernel(w_ref, m_ref, v_ref, keep_ref, got_ref, m_out, v_out, w_out, sum_ref):
        grad = keep_ref[...] + got_ref[...].astype(F32)
        if flip:
            grad = jnp.transpose(grad)
        weight = w_ref[...]
        first_new, second_new, weight_new = adamw_step(
            weight, m_ref[...], v_ref[...], grad, rate, DECAY_RATE
        )
        m_out[...] = first_new
        v_out[...] = second_new
        w_out[...] = weight_new
        if flip:
            sum_ref[...] = jnp.zeros_like(sum_ref)
        else:
            sum_ref[...] = jnp.sum(weight.astype(BF16).astype(F32) * grad, axis=1, keepdims=True)

    shape = jax.ShapeDtypeStruct(weight.shape, F32)
    columns = weight.shape[0] if flip else weight.shape[1]
    whole = lambda *shape: pl.BlockSpec(shape, lambda i: (0,) * len(shape))
    view = pl.BlockSpec((D // 16, columns), lambda i: (0, spot // columns))
    return pl.pallas_call(
        kernel,
        grid=(1,),
        in_specs=[whole(*weight.shape)] * 3 + [view] * 2,
        out_specs=[whole(*weight.shape)] * 3 + [whole(D // 16, 1)],
        out_shape=[shape] * 3 + [jax.ShapeDtypeStruct((D // 16, 1), F32)],
        cost_estimate=pl.CostEstimate(
            flops=0, bytes_accessed=28 * weight.size, transcendentals=0
        ),
        compiler_params=pltpu.CompilerParams(vmem_limit_bytes=24 << 20),
    )(weight, first, second, *sums)


def pick(blocks, axis, index):
    return lax.dynamic_index_in_dim(blocks, index, axis, keepdims=False)


class Here:
    def __init__(self):
        self.x, self.yh, self.c, self.yl, self.z = (
            lax.axis_index(a) for a in ("x", "yh", "c", "yl", "z")
        )

    def ztable(self):
        own = [self.yl * 4 + (self.z + k) % 4 for k in range(4)]
        other = [(1 - self.yl) * 4 + (self.z + k) % 4 for k in range(4)]
        return jnp.stack(own + other).astype(jnp.int32)

    def xtable(self):
        table = []
        for dc in range(2):
            core = self.c if dc == 0 else 1 - self.c
            for k in range(4):
                for dy in range(2):
                    yh = self.yh if dy == 0 else 1 - self.yh
                    table.append(((self.x + k) % 4) * 4 + yh * 2 + core)
        return jnp.stack(table).astype(jnp.int32)

    def scatter_tp(self, terms, extras, finish, out_shape, deps=(), weight=1):
        parts = lax.all_to_all(terms, ("yl", "z"), 0, 0, tiled=True)
        parts = parts.reshape(8, -1, terms.shape[1])

        def kernel(part_ref, *refs):
            total = part_ref[0].astype(F32)
            for n in range(1, 8):
                total = total + part_ref[n].astype(F32)
            finish(total, refs[: len(extras)], refs[len(extras) :])

        return in_vmem(kernel, [parts] + list(extras), out_shape, deps, weight)

    def gather_tp(self, first, second, deps=(), weight=1):
        pair = join([first, lax.ppermute(first, "yl", SWAP)])
        rest = join([lax.ppermute(second, "z", ring(-k)) for k in (1, 2, 3)])
        pieces = [pair] + [lax.ppermute(pair, "z", ring(-k)) for k in (1, 2, 3)]
        pieces += [second, lax.ppermute(second, "yl", SWAP), rest, lax.ppermute(rest, "yl", SWAP)]
        spots = [(k, (d,), 4 * d + k) for k in range(4) for d in range(2)]
        spots += [(4, (), 8), (5, (), 12)]
        spots += [(6, (k,), k + 9) for k in range(3)] + [(7, (k,), k + 13) for k in range(3)]
        count = first.shape[0] if first.ndim == 3 else 1
        plan = []
        for piece, index, entry in spots:
            for out in range(count):
                at = index + ((out,) if first.ndim == 3 else ())
                plan.append((piece, at or None, out, entry))
        table = self.ztable()
        table = jnp.concatenate([2 * table, 2 * table + 1])
        laid = lay(pieces, plan, table, 16, count, deps, weight)
        return [v.reshape(-1, v.shape[-1]) for v in laid]

    def gather_weights(self, shard):
        pair = jnp.stack([shard, lax.ppermute(shard, "yh", SWAP)])
        mine = [pair] + [lax.ppermute(pair, "x", ring(-k)) for k in (1, 2, 3)]
        return mine + [lax.ppermute(p, "c", SWAP) for p in mine]

    def scatter_weights(self, total, sends, late=False):
        near = [lax.ppermute(sends[n], "x", ring(n + 1)) for n in (0, 2)]
        far = lax.ppermute(tie(sends[1], near) if late else sends[1], "x", ring(2))
        for part in near + [far]:
            total = total + part.astype(F32)
        n = D // 16
        back = lax.ppermute(total[n:].astype(BF16), "yh", SWAP)
        return (total[:n], back), near, far

    def gather_ctx(self, own):
        over = lax.ppermute(own, "yh", SWAP)
        pieces = [own, over, lax.ppermute(own, "c", SWAP), lax.ppermute(over, "c", SWAP)]
        table = jnp.stack(
            [
                self.yh * 2 + self.c,
                (1 - self.yh) * 2 + self.c,
                self.yh * 2 + 1 - self.c,
                (1 - self.yh) * 2 + 1 - self.c,
            ]
        ).astype(jnp.int32)
        plan = [(i, None, 0, i) for i in range(4)]
        return lay(pieces, plan, table, 4)[0].reshape(-1, own.shape[1])

    def scatter_ctx(self, terms, deps):
        give, keep = keys_split(terms, self.c.reshape(1).astype(jnp.int32), deps)
        both = keep + lax.ppermute(give, "c", SWAP).astype(F32)
        give = pick(both, 0, 1 - self.yh).astype(BF16)
        return pick(both, 0, self.yh), lax.ppermute(give, "yh", SWAP)

    def sum_tp(self, value):
        value = value + lax.ppermute(value, "yl", SWAP)
        got = [lax.ppermute(value, "z", ring(k)) for k in (1, 2, 3)]
        parts = jnp.stack([value] + got)
        order = jnp.stack([(self.z - j) % 4 for j in range(4)])
        return jnp.sum(jnp.take(parts, order, axis=0), axis=0)


def per_device(
    tokens,
    cotangent,
    lengths,
    groups,
    query_weight,
    query_m,
    query_v,
    kv_weight,
    kv_m,
    kv_v,
    out_weight,
    out_m,
    out_v,
    gate_weight,
    gate_m,
    gate_v,
    up_weight,
    up_m,
    up_v,
    down_weight,
    down_m,
    down_v,
    norm_gains,
    gains_m,
    gains_v,
):
    here = Here()
    row_count = tokens.shape[0]
    group_rows = row_count * 4
    group_id = here.x
    ctx_id = here.yh * 2 + here.c
    tp_id = here.yl * 4 + here.z
    half = row_count // 2
    part = half // 8
    xtable = here.xtable()

    kv_flat = kv_weight.reshape(D // 16, 2 * HD)
    attn_shard = jnp.concatenate([query_weight, kv_flat, out_weight.T], axis=1).astype(BF16)
    q_cols, kv_cols, o_cols = query_weight.shape[1], 2 * HD, out_weight.shape[0]
    cols = q_cols + kv_cols + o_cols
    gains_low = norm_gains.astype(BF16)
    gain_rows = jnp.zeros((16, cols), BF16).at[:2, : D // 16].set(gains_low)
    attn_pieces = here.gather_weights(jnp.concatenate([attn_shard, gain_rows], axis=0))

    units = gate_weight.shape[1]
    ff_shard = jnp.stack([gate_weight, up_weight, down_weight.T]).astype(BF16)
    w_ff = lax.all_gather(ff_shard, ("x", "yh", "c"), axis=1, tiled=True)

    slots, starts = slot_tables(lengths, groups, group_id, ctx_id * row_count, row_count)
    frequency = ROPE_BASE ** (-2.0 * jnp.arange(HD // 2, dtype=F32) / HD)
    angles = frequency[:, None] * (slots - starts).astype(F32)[None, :]
    cosine, sine = jnp.cos(angles), jnp.sin(angles)
    bounds = block_bounds(slots, starts)
    slot_rows, start_rows = slots.reshape(-1, 1, QB), starts.reshape(-1, 1, QB)

    normed_one, query_raw, kv_local, w_query, w_kv, w_out, gain_values = normed_projections(
        tokens,
        attn_pieces,
        xtable,
        (q_cols, kv_cols, o_cols),
        cosine,
        sine,
        NORM_EPS,
    )
    kv_whole = here.gather_ctx(kv_local)

    mixed, turned, raw, log_total = attention_forward(
        query_raw, kv_whole, bounds, start_rows, slot_rows, cosine, sine, 0, row_count
    )
    own = lambda v: lax.dynamic_slice_in_dim(v, tp_id * 2 * part, 2 * part, axis=0)
    own_inputs, own_upstream = own(tokens), own(cotangent)
    own_wide = jax.ShapeDtypeStruct((2 * part, D), F32)
    own_low = [jax.ShapeDtypeStruct((part, D), BF16)] * 2

    def both(outs, value):
        outs[0][...] = value[:part]
        outs[1][...] = value[part:]

    def close_attention(total, ins, outs):
        value = ins[0][...].astype(F32) + total
        outs[0][...] = value
        both(outs[1:], (value * rms_inverse(value) * ins[1][1:2, :]).astype(BF16))

    term = jnp.einsum("ra,da->rd", mixed, w_out, preferred_element_type=F32).astype(BF16)
    hidden_one, *own_normed = here.scatter_tp(
        term, [own_inputs, gain_values], close_attention, [own_wide] + own_low
    )
    (normed_two,) = here.gather_tp(*own_normed)

    order = here.xtable()
    order = jnp.concatenate([order[8:], order[:8]])
    hidden, d_gate, d_up, d_two, out_term, *turned_inputs = feed_forward(
        normed_two, cotangent, w_ff, order
    )
    normed_give, normed_keep, upstream_give, upstream_keep = turned_inputs
    outer = lambda a, b: jnp.einsum("rd,rf->df", a, b, preferred_element_type=F32).astype(BF16)
    gives = [outer(normed_give, d_gate), outer(normed_give, d_up), outer(upstream_give, hidden)]
    keeps = [outer(normed_keep, d_gate), outer(normed_keep, d_up), outer(upstream_keep, hidden)]
    gots = [lax.ppermute(give, "c", SWAP) for give in gives]

    ff_total, *ff_sends = fold_core(keeps, gots)

    def close_feed_forward(total, ins, outs):
        value = ins[1][...].astype(F32) + through_norm(total, ins[0][...], ins[2][1:2, :])
        outs[0][...] = value
        both(outs[1:], value.astype(BF16))

    d_hidden_one, *own_branch = here.scatter_tp(
        d_two,
        [hidden_one, own_upstream, gain_values],
        close_feed_forward,
        [own_wide] + own_low,
        deps=gots,
        weight=20,
    )
    (d_branch,) = here.gather_tp(*own_branch, deps=[ff_total], weight=20)
    d_mixed = jnp.dot(d_branch, w_out, preferred_element_type=F32).astype(BF16)

    ff_sums, ff_near, ff_far = here.scatter_weights(ff_total, ff_sends, True)

    def close_output(total, ins, outs):
        both(outs, (ins[0][...] + total).astype(BF16))

    own_outputs = here.scatter_tp(
        tie(out_term, [d_branch]), [hidden_one], close_output, own_low
    )

    d_query_low, d_kv = attention_backward(
        d_mixed,
        kv_whole,
        turned,
        raw,
        log_total,
        bounds,
        start_rows,
        slot_rows,
        cosine,
        sine,
    )
    d_kv_low = keys_back(
        *here.scatter_ctx(d_kv, own_outputs[:1]), cosine, sine, deps=ff_near
    )

    give, keep = outer_blocks(
        order,
        [((normed_one, d_query_low),), ((d_branch, mixed),), ((normed_one, d_kv_low),)],
    )
    attn_got = lax.ppermute(give, "c", SWAP)
    attn_total, *attn_sends = fold_core([keep], [attn_got])
    attn_sums, attn_near, attn_far = here.scatter_weights(attn_total, attn_sends)

    def close_inputs(total, ins, outs):
        value = ins[0][...] + through_norm(total, ins[1][...].astype(F32), ins[2][:1, :])
        value = value.astype(BF16)
        for n in range(2):
            outs[n][0] = ins[3 + n][...]
            outs[n][1] = value[n * part : (n + 1) * part]

    term = (
        jnp.einsum("ra,da->rd", d_query_low, w_query, preferred_element_type=F32)
        + jnp.einsum("rc,dc->rd", d_kv_low, w_kv, preferred_element_type=F32)
    ).astype(BF16)
    own_results = here.scatter_tp(
        term,
        [d_hidden_one, own_inputs, gain_values, *own_outputs],
        close_inputs,
        [jax.ShapeDtypeStruct((2, part, D), BF16)] * 2,
        deps=[ff_far],
        weight=50,
    )
    output, tokens_grad = here.gather_tp(*own_results, deps=[attn_far], weight=50)

    flat = lambda v: v.reshape(kv_flat.shape)
    fan = D ** (-0.5)
    out_fan = max(1, 4 * D // group_rows) ** (-0.5)
    query_new = adamw_kernel(query_weight, query_m, query_v, attn_sums, 0, fan, False)
    out_new = adamw_kernel(out_weight, out_m, out_v, attn_sums, q_cols, out_fan, True)
    kv_new = adamw_kernel(
        kv_flat, flat(kv_m), flat(kv_v), attn_sums, q_cols + o_cols, fan, False
    )
    gate_new = adamw_kernel(gate_weight, gate_m, gate_v, ff_sums, 0, fan, False)
    up_new = adamw_kernel(up_weight, up_m, up_v, ff_sums, units, fan, False)
    down_new = adamw_kernel(down_weight, down_m, down_v, ff_sums, 2 * units, FF ** (-0.5), True)

    gain_sums = jnp.stack([query_new[3] + kv_new[3], gate_new[3] + up_new[3]])[:, :, 0]
    grad_gains = here.sum_tp(tie_small(gain_sums, tokens_grad)) / gains_low.astype(F32)
    gains_new = adamw_step(norm_gains, gains_m, gains_v, grad_gains, 0.5, 0.0)
    return (
        output,
        tokens_grad,
        *query_new[:3],
        *[v.reshape(kv_weight.shape) for v in kv_new[:3]],
        *out_new[:3],
        *gate_new[:3],
        *up_new[:3],
        *down_new[:3],
        *gains_new,
    )


def solution(mesh):
    fine = Mesh(mesh.devices.reshape(4, 2, 2, 2, 4), ("x", "yh", "c", "yl", "z"))
    rows = ("x", "yh", "c")
    tp = ("yl", "z")
    by_row, by_col, by_unit = P(rows, None), P(rows, tp), P(tp, rows)
    by_kv, by_gain = P(rows, tp, None), P(None, rows)
    in_specs = (
        (by_row,) * 2
        + (P(),) * 2
        + (by_col,) * 3
        + (by_kv,) * 3
        + (by_unit,) * 3
        + (by_col,) * 6
        + (by_unit,) * 3
        + (by_gain,) * 3
    )
    out_specs = (
        (by_row,) * 2
        + (by_col,) * 3
        + (by_kv,) * 3
        + (by_unit,) * 3
        + (by_col,) * 6
        + (by_unit,) * 3
        + (by_gain,) * 3
    )
    return jax.shard_map(
        per_device, mesh=fine, in_specs=in_specs, out_specs=out_specs, check_vma=False
    )
```

```python
import functools

import jax
import jax.numpy as jnp
from jax import lax
from jax.experimental import pallas as pl
from jax.experimental.pallas import tpu as pltpu
from jax.sharding import Mesh
from jax.sharding import PartitionSpec as P

D = 2048
HD = 64
FF = 8192
STEP = 5


NORM_EPS = 1e-05
BETA_FIRST = 0.9
BETA_SECOND = 0.95
ADAM_EPS = 1e-08
DECAY_RATE = 0.1
ROPE_BASE = 500000.0
MASKED_SCORE = -1e30

F32 = jnp.float32
BF16 = jnp.bfloat16
QB = 128
KB = 512
KB_FORWARD = 1024


SWAP = ((0, 1), (1, 0))


def ring(step):
    return tuple((i, (i + step) % 4) for i in range(4))


def dot(a, b):
    return jnp.dot(a, b, preferred_element_type=F32)


def turn(value, cosine, sine):
    a, b = value[: HD // 2], value[HD // 2 :]
    return jnp.concatenate([a * cosine - b * sine, b * cosine + a * sine], axis=0)


def heads_to_lanes(wide, heads):
    return jnp.concatenate([wide[h * HD : (h + 1) * HD] for h in range(heads)], axis=1)


def lanes_to_heads(tall, heads):
    n = tall.shape[1] // heads
    return jnp.concatenate([tall[:, h * n : (h + 1) * n] for h in range(heads)], axis=0)


def normed_projections(tokens, pieces, table, widths, cosine, sine, eps, deps=()):
    rows, width = tokens.shape
    block, part = 256, D // 16
    q_cols, kv_cols, o_cols = widths
    deps = list(deps)
    count = len(pieces)

    def kernel(table_ref, t_ref, *refs):
        piece_refs, refs = refs[:count], refs[count:]
        cos_ref, sin_ref, n_ref, q_ref, kv_ref, wq_ref, wkv_ref, wo_ref, g_ref = refs

        @pl.when(pl.program_id(0) == 0)
        def _():
            for i in range(count):
                for d in range(2):
                    spot = table_ref[2 * i + d]
                    at = pl.ds(pl.multiple_of(spot * part, part), part)
                    body = piece_refs[i][d, :part, :]
                    wq_ref[at, :] = body[:, :q_cols]
                    wkv_ref[at, :] = body[:, q_cols : q_cols + kv_cols]
                    wo_ref[at, :] = body[:, q_cols + kv_cols :]
                    g_ref[:, at] = piece_refs[i][d, part:, :part].astype(F32)[:8]

        x = t_ref[...].astype(F32)
        inv = lax.rsqrt(jnp.mean(x * x, axis=-1, keepdims=True) + eps)
        normed = (x * inv * g_ref[:1, :]).astype(BF16)
        n_ref[...] = normed
        q_ref[...] = dot(normed, wq_ref[...])
        kv = jnp.transpose(dot(normed, wkv_ref[...]))
        kv = jnp.concatenate([turn(kv[:HD], cos_ref[...], sin_ref[...]), kv[HD:]], axis=0)
        kv_ref[...] = jnp.transpose(kv).astype(BF16)

    whole = lambda *shape: pl.BlockSpec(shape, lambda i: (0,) * len(shape))
    by_row = lambda w: pl.BlockSpec((block, w), lambda i: (i, 0))
    by_lane = pl.BlockSpec((HD // 2, block), lambda i: (0, i))
    return pl.pallas_call(
        after(kernel, 4 + count, deps),
        grid=(rows // block,),
        in_specs=[pl.BlockSpec(memory_space=pltpu.SMEM), by_row(width)]
        + [whole(*p.shape) for p in pieces]
        + [by_lane, by_lane]
        + dep_specs(deps),
        out_specs=[
            by_row(width),
            by_row(q_cols),
            by_row(kv_cols),
            whole(D, q_cols),
            whole(D, kv_cols),
            whole(D, o_cols),
            whole(8, D),
        ],
        out_shape=[
            jax.ShapeDtypeStruct((rows, width), BF16),
            jax.ShapeDtypeStruct((rows, q_cols), F32),
            jax.ShapeDtypeStruct((rows, kv_cols), BF16),
            jax.ShapeDtypeStruct((D, q_cols), BF16),
            jax.ShapeDtypeStruct((D, kv_cols), BF16),
            jax.ShapeDtypeStruct((D, o_cols), BF16),
            jax.ShapeDtypeStruct((8, D), F32),
        ],
        cost_estimate=pl.CostEstimate(
            flops=2 * rows * width * 384, bytes_accessed=12 << 20, transcendentals=0
        ),
        compiler_params=pltpu.CompilerParams(vmem_limit_bytes=24 << 20),
    )(table, tokens, *pieces, cosine, sine, *deps)


def key_ranges(bounds_ref, step):
    return [bounds_ref[step * 4 + n] for n in range(4)]


def attention_forward(query_raw, kv, bounds, starts, slots, cosine, sine, row_offset, rows):
    heads = query_raw.shape[1] // HD
    keys = kv.shape[0]
    wide = heads * QB
    steps, base = rows // QB, row_offset // QB

    def kernel(b_ref, q_ref, kv_ref, start_ref, slot_ref, cos_ref, sin_ref, m_ref, qt_ref, ot_ref, lse_ref, kvt_ref, qp_ref):
        step = pl.program_id(0)

        @pl.when(step == 0)
        def _():
            kvt_ref[...] = jnp.transpose(kv_ref[...].astype(F32)).astype(BF16)

        raw = jnp.transpose(q_ref[...])
        turned = jnp.concatenate(
            [turn(raw[h * HD : (h + 1) * HD], cos_ref[...], sin_ref[...]) for h in range(heads)],
            axis=1,
        ).astype(BF16)
        qt_ref[0] = turned
        scaled = (turned.astype(F32) * HD**-0.5).astype(BF16)
        qp_ref[...] = jnp.concatenate([scaled, jnp.zeros_like(scaled)], axis=0)
        start = jnp.concatenate([start_ref[0]] * heads, axis=1)
        slot = jnp.concatenate([slot_ref[0]] * heads, axis=1)

        def body(masked, j, carry):
            peak, total, acc = carry
            at = pl.multiple_of(j * KB_FORWARD, KB_FORWARD)
            scores = dot(kv_ref[pl.ds(at, KB_FORWARD), :], qp_ref[...])
            if masked:
                key = at + lax.broadcasted_iota(jnp.int32, (KB_FORWARD, wide), 0)
                scores = jnp.where((key >= start) & (key <= slot), scores, MASKED_SCORE)
            new_peak = jnp.maximum(peak, jnp.max(scores, axis=0, keepdims=True))
            powers = jnp.exp(scores - new_peak)
            shrink = jnp.exp(peak - new_peak)
            total = total * shrink + jnp.sum(powers, axis=0, keepdims=True)
            values = kvt_ref[HD:, pl.ds(at, KB_FORWARD)]
            acc = acc * shrink + dot(values, powers.astype(BF16))
            return (new_peak, total, acc)

        first, full_first, full_end, end = key_ranges(b_ref, base + step)
        carry = (
            jnp.full((1, wide), MASKED_SCORE, F32),
            jnp.zeros((1, wide), F32),
            jnp.zeros((HD, wide), F32),
        )
        carry = lax.fori_loop(first, full_first, functools.partial(body, True), carry)
        carry = lax.fori_loop(full_first, full_end, functools.partial(body, False), carry)
        carry = lax.fori_loop(full_end, end, functools.partial(body, True), carry)
        peak, total, acc = carry
        mixed = acc / total
        ot_ref[0] = mixed
        lse_ref[0] = peak + jnp.log(total)
        m_ref[...] = jnp.transpose(lanes_to_heads(mixed, heads)).astype(BF16)

    lane = lambda: pl.BlockSpec((HD // 2, QB), lambda i: (0, base + i))
    row = lambda: pl.BlockSpec((1, 1, QB), lambda i: (base + i, 0, 0))
    return pl.pallas_call(
        kernel,
        grid=(steps,),
        in_specs=[
            pl.BlockSpec(memory_space=pltpu.SMEM),
            pl.BlockSpec((QB, heads * HD), lambda i: (base + i, 0)),
            pl.BlockSpec((keys, 2 * HD), lambda i: (0, 0)),
            row(),
            row(),
            lane(),
            lane(),
        ],
        out_specs=[
            pl.BlockSpec((QB, heads * HD), lambda i: (i, 0)),
            pl.BlockSpec((1, HD, wide), lambda i: (i, 0, 0)),
            pl.BlockSpec((1, HD, wide), lambda i: (i, 0, 0)),
            pl.BlockSpec((1, 1, wide), lambda i: (i, 0, 0)),
        ],
        out_shape=[
            jax.ShapeDtypeStruct((rows, heads * HD), BF16),
            jax.ShapeDtypeStruct((steps, HD, wide), BF16),
            jax.ShapeDtypeStruct((steps, HD, wide), F32),
            jax.ShapeDtypeStruct((steps, 1, wide), F32),
        ],
        scratch_shapes=[pltpu.VMEM((2 * HD, keys), BF16), pltpu.VMEM((2 * HD, wide), BF16)],
        cost_estimate=pl.CostEstimate(
            flops=rows * keys * heads * HD // 8, bytes_accessed=2 << 20, transcendentals=0
        ),
        compiler_params=pltpu.CompilerParams(vmem_limit_bytes=14 << 20),
    )(bounds, query_raw, kv, starts, slots, cosine, sine)


def attention_backward(
    d_mixed, kv, queries, mixed, lse, bounds, starts, slots, cosine, sine, deps=()
):
    rows, width = d_mixed.shape
    heads = width // HD
    keys = kv.shape[0]
    wide = heads * QB
    steps = rows // QB
    deps = list(deps)

    def kernel(b_ref, d_ref, kv_ref, qt_ref, ot_ref, lse_ref, start_ref, slot_ref, cos_ref, sin_ref, dq_ref, dkv_ref, kvt_ref, qp_ref, dp_ref, qr_ref, dr_ref):
        step = pl.program_id(0)

        @pl.when(step == 0)
        def _():
            kvt_ref[...] = jnp.transpose(kv_ref[...].astype(F32)).astype(BF16)
            dkv_ref[...] = jnp.zeros_like(dkv_ref)

        scaled = qt_ref[0].astype(F32) * HD**-0.5
        grads = heads_to_lanes(jnp.transpose(d_ref[...].astype(F32)), heads)
        delta = jnp.sum(grads * ot_ref[0], axis=0, keepdims=True)
        empty = jnp.zeros_like(scaled)
        q_pad = jnp.concatenate([scaled, empty], axis=0)
        d_pad = jnp.concatenate([empty, grads], axis=0)
        qp_ref[...] = q_pad.astype(BF16)
        dp_ref[...] = d_pad.astype(BF16)
        qr_ref[...] = jnp.transpose(q_pad).astype(BF16)
        dr_ref[...] = jnp.transpose(d_pad).astype(BF16)
        start = jnp.concatenate([start_ref[0]] * heads, axis=1)
        slot = jnp.concatenate([slot_ref[0]] * heads, axis=1)
        log_total = lse_ref[0]

        def body(masked, j, d_query):
            at = pl.multiple_of(j * KB, KB)
            block = kv_ref[pl.ds(at, KB), :]
            scores = dot(block, qp_ref[...])
            if masked:
                key = at + lax.broadcasted_iota(jnp.int32, (KB, wide), 0)
                scores = jnp.where((key >= start) & (key <= slot), scores, MASKED_SCORE)
            chances = jnp.exp(scores - log_total)
            d_chances = dot(block, dp_ref[...])
            d_scores = (chances * (d_chances - delta)).astype(BF16)
            dkv_ref[pl.ds(at, KB), :] += dot(chances.astype(BF16), dr_ref[...]) + dot(
                d_scores, qr_ref[...]
            )
            return d_query + dot(kvt_ref[:HD, pl.ds(at, KB)], d_scores)

        first, full_first, full_end, end = key_ranges(b_ref, step)
        d_query = jnp.zeros((HD, wide), F32)
        d_query = lax.fori_loop(first, full_first, functools.partial(body, True), d_query)
        d_query = lax.fori_loop(full_first, full_end, functools.partial(body, False), d_query)
        d_query = lax.fori_loop(full_end, end, functools.partial(body, True), d_query)
        d_query = lanes_to_heads(d_query * HD**-0.5, heads)
        turned = jnp.concatenate(
            [turn(d_query[h * HD : (h + 1) * HD], cos_ref[...], -sin_ref[...]) for h in range(heads)],
            axis=0,
        )
        dq_ref[...] = jnp.transpose(turned).astype(BF16)

    lane = lambda: pl.BlockSpec((HD // 2, QB), lambda i: (0, i))
    row = lambda: pl.BlockSpec((1, 1, QB), lambda i: (i, 0, 0))
    kept = lambda n: pl.BlockSpec((1, n, wide), lambda i: (i, 0, 0))
    return pl.pallas_call(
        after(kernel, 10, deps),
        grid=(steps,),
        in_specs=[
            pl.BlockSpec(memory_space=pltpu.SMEM),
            pl.BlockSpec((QB, width), lambda i: (i, 0)),
            pl.BlockSpec((keys, 2 * HD), lambda i: (0, 0)),
            kept(HD),
            kept(HD),
            kept(1),
            row(),
            row(),
            lane(),
            lane(),
        ]
        + dep_specs(deps),
        out_specs=[
            pl.BlockSpec((QB, width), lambda i: (i, 0)),
            pl.BlockSpec((keys, 2 * HD), lambda i: (0, 0)),
        ],
        out_shape=[
            jax.ShapeDtypeStruct((rows, width), BF16),
            jax.ShapeDtypeStruct((keys, 2 * HD), F32),
        ],
        scratch_shapes=[
            pltpu.VMEM((2 * HD, keys), BF16),
            pltpu.VMEM((2 * HD, wide), BF16),
            pltpu.VMEM((2 * HD, wide), BF16),
            pltpu.VMEM((wide, 2 * HD), BF16),
            pltpu.VMEM((wide, 2 * HD), BF16),
        ],
        cost_estimate=pl.CostEstimate(
            flops=rows * 2 * keys * heads * HD, bytes_accessed=2 << 20, transcendentals=0
        ),
        compiler_params=pltpu.CompilerParams(vmem_limit_bytes=14 << 20),
    )(bounds, d_mixed, kv, queries, mixed, lse, starts, slots, cosine, sine, *deps)


def keys_split(d_kv, core, deps=()):
    rows, width = d_kv.shape
    quarter = rows // 4
    deps = list(deps)

    def kernel(core_ref, d_ref, give_ref, keep_ref):
        core = core_ref[0]
        for n in range(2):
            give_at = pl.multiple_of((2 * n + 1 - core) * quarter, quarter)
            keep_at = pl.multiple_of((2 * n + core) * quarter, quarter)
            give_ref[n] = d_ref[pl.ds(give_at, quarter), :].astype(BF16)
            keep_ref[n] = d_ref[pl.ds(keep_at, quarter), :]

    shape = (2, quarter, width)
    return pl.pallas_call(
        after(kernel, 2, deps),
        out_shape=[jax.ShapeDtypeStruct(shape, BF16), jax.ShapeDtypeStruct(shape, F32)],
        grid=(1,),
        in_specs=[pl.BlockSpec(memory_space=pltpu.SMEM)] + whole_specs([d_kv]) + dep_specs(deps),
        out_specs=whole_specs([jax.ShapeDtypeStruct(shape, BF16)] * 2),
        cost_estimate=pl.CostEstimate(flops=0, bytes_accessed=2 << 20, transcendentals=0),
    )(core, d_kv, *deps)


def keys_back(keep, got, cosine, sine, deps=()):
    deps = list(deps)

    def kernel(keep_ref, got_ref, cos_ref, sin_ref, out_ref):
        total = jnp.transpose(keep_ref[...] + got_ref[...].astype(F32))
        turned = turn(total[:HD], cos_ref[...], -sin_ref[...])
        out_ref[...] = jnp.transpose(jnp.concatenate([turned, total[HD:]], axis=0)).astype(BF16)

    return pl.pallas_call(
        after(kernel, 4, deps),
        out_shape=jax.ShapeDtypeStruct(keep.shape, BF16),
        grid=(1,),
        in_specs=whole_specs([keep, got, cosine, sine]) + dep_specs(deps),
        out_specs=whole_specs([keep])[0],
        cost_estimate=pl.CostEstimate(flops=0, bytes_accessed=2 << 20, transcendentals=0),
    )(keep, got, cosine, sine, *deps)


def slot_tables(lengths, groups, group_id, first_slot, rows):
    seq_count = lengths.shape[0]
    seq_order = jnp.arange(seq_count, dtype=jnp.int32)
    same_group = groups[None, :] == groups[:, None]
    before = seq_order[None, :] < seq_order[:, None]
    begins = jnp.sum(jnp.where(same_group & before, lengths[None, :], 0), axis=1)
    ends = begins + lengths
    slots = first_slot + jnp.arange(rows, dtype=jnp.int32)
    inside = (
        (groups == group_id)[:, None]
        & (slots[None, :] >= begins[:, None])
        & (slots[None, :] < ends[:, None])
    )
    starts = jnp.where(
        jnp.any(inside, axis=0), jnp.sum(jnp.where(inside, begins[:, None], 0), axis=0), slots
    )
    return slots, starts


def block_bounds(slots, starts, size):
    first_row, last_row = slots[::QB], slots[QB - 1 :: QB]
    low, high = starts[::QB], starts[QB - 1 :: QB]
    first = low // size
    end = last_row // size + 1
    full_first = jnp.clip((high + size - 1) // size, first, end)
    full_end = jnp.clip((first_row + 1) // size, full_first, end)
    return jnp.stack([first, full_first, full_end, end], axis=1).reshape(-1).astype(jnp.int32)


def adamw_step(weight, first, second, grad, rate, decay):
    first_new = BETA_FIRST * first + (1.0 - BETA_FIRST) * grad
    second_new = BETA_SECOND * second + (1.0 - BETA_SECOND) * grad * grad
    first_hat = first_new / (1.0 - BETA_FIRST**STEP)
    second_hat = second_new / (1.0 - BETA_SECOND**STEP)
    weight_new = weight - rate * (first_hat / (jnp.sqrt(second_hat) + ADAM_EPS) + decay * weight)
    return (first_new, second_new, weight_new)


def after(kernel, inputs, deps):
    count = len(deps)
    if not count:
        return kernel
    return lambda *refs: kernel(*refs[:inputs], *refs[inputs + count :])


def any_specs(count):
    return [pl.BlockSpec(memory_space=pl.ANY)] * count


def dep_specs(deps):
    return [
        pl.BlockSpec((1,) * (d.ndim - 2) + (16, 128), lambda *at, n=d.ndim: (0,) * n) for d in deps
    ]


def whole_specs(arrays):
    return [pl.BlockSpec(v.shape, lambda *at, n=len(v.shape): (0,) * n) for v in arrays]


def tie(value, deps):
    deps = list(deps)
    return pl.pallas_call(
        lambda *refs: None,
        grid=(1,),
        out_shape=jax.ShapeDtypeStruct(value.shape, value.dtype),
        in_specs=any_specs(1) + dep_specs(deps),
        out_specs=pl.BlockSpec(memory_space=pl.ANY),
        input_output_aliases={0: 0},
    )(value, *deps)


def lay(pieces, plan, table, blocks, outputs=1, deps=(), weight=1):
    deps = list(deps)
    n, w = pieces[0].shape[-2:]
    inputs = 1 + len(pieces)

    def kernel(table_ref, *refs):
        out_refs = refs[len(pieces) :]
        for piece, index, out, entry in plan:
            source = refs[piece]
            out_refs[out][table_ref[entry]] = source[...] if index is None else source[index]

    size = sum(p.size * p.dtype.itemsize for p in pieces)
    return pl.pallas_call(
        after(kernel, inputs, deps),
        out_shape=[jax.ShapeDtypeStruct((blocks, n, w), BF16)] * outputs,
        grid=(1,),
        in_specs=[pl.BlockSpec(memory_space=pltpu.SMEM)] + whole_specs(pieces) + dep_specs(deps),
        out_specs=whole_specs([jax.ShapeDtypeStruct((blocks, n, w), BF16)] * outputs),
        cost_estimate=pl.CostEstimate(flops=0, bytes_accessed=2 * weight * size, transcendentals=0),
        compiler_params=pltpu.CompilerParams(vmem_limit_bytes=3 * size + (3 << 20)),
    )(table, *pieces, *deps)


def tie_small(value, late):
    def kernel(value_ref, out_ref):
        out_ref[...] = value_ref[...]

    return in_vmem(kernel, [value], [jax.ShapeDtypeStruct(value.shape, F32)], [late])[0]


def in_vmem(kernel, inputs, out_shape, deps=(), weight=1):
    deps = list(deps)
    count = len(inputs)
    size = sum(v.size * v.dtype.itemsize for v in list(inputs) + list(out_shape))
    return pl.pallas_call(
        after(kernel, count, deps),
        out_shape=out_shape,
        grid=(1,),
        in_specs=whole_specs(inputs) + dep_specs(deps),
        out_specs=whole_specs(out_shape),
        cost_estimate=pl.CostEstimate(flops=0, bytes_accessed=weight * size, transcendentals=0),
        compiler_params=pltpu.CompilerParams(vmem_limit_bytes=2 * size + (6 << 20)),
    )(*inputs, *deps)


def join(parts, deps=()):
    arrays = []
    for array, _ in parts:
        if not any(array is known for known in arrays):
            arrays.append(array)
    spots = [next(n for n, known in enumerate(arrays) if known is array) for array, _ in parts]
    picked = [array.shape if index is None else array.shape[1:] for array, index in parts]

    def kernel(*refs):
        for n, (spot, (_, index)) in enumerate(zip(spots, parts)):
            refs[-1][n] = refs[spot][...] if index is None else refs[spot][index]

    shape = (len(parts),) + picked[0]
    return in_vmem(kernel, arrays, [jax.ShapeDtypeStruct(shape, BF16)], deps)[0]


def rms_inverse(value):
    return lax.rsqrt(jnp.mean(value * value, axis=-1, keepdims=True) + NORM_EPS)


def through_norm(d_normed, value, gain):
    inverse = rms_inverse(value)
    scaled = d_normed * gain
    pre = value * inverse
    return inverse * (scaled - pre * jnp.mean(scaled * pre, axis=-1, keepdims=True))


def load_weights(piece_refs, plan, table_ref, weights, held, sem, part):
    copies = []
    for n, (piece, index, entry) in enumerate(plan):
        source = piece_refs[piece] if index is None else piece_refs[piece].at[index]
        at = pl.ds(pl.multiple_of(table_ref[entry] * part, part), part)
        source = source.at[pl.ds(weights[0], len(weights))]
        copies.append(pltpu.make_async_copy(source, held.at[:, at, :], sem.at[n]))
    for copy in copies:
        copy.start()
    for copy in copies:
        copy.wait()


def upstream_hidden(upstream, pieces, plan, table, order):
    rows, units, part = upstream.shape[0], pieces[0].shape[-1], D // 16
    count, block = len(pieces), upstream.shape[0] // 2

    def kernel(order_ref, table_ref, u_ref, *refs):
        piece_refs, (dh_ref, ug_ref, uk_ref, w_ref, sem) = refs[:count], refs[count:]

        @pl.when(pl.program_id(0) == 0)
        def _():
            load_weights(piece_refs, plan, table_ref, (2,), w_ref, sem, part)

        for i in range(16):
            at = pl.ds(pl.multiple_of(order_ref[i] * part, part), part)
            to = slice((i % 8) * part, (i % 8 + 1) * part)
            (ug_ref if i < 8 else uk_ref)[:, to] = u_ref[:, at]
        for f in range(0, units, 256):
            at = slice(f, f + 256)
            dh_ref[:, at] = dot(u_ref[...], w_ref[0, :, at])

    by_row = lambda w: pl.BlockSpec((block, w), lambda i: (i, 0))
    shape = lambda w, t: jax.ShapeDtypeStruct((rows, w), t)
    return pl.pallas_call(
        kernel,
        grid=(2,),
        in_specs=[pl.BlockSpec(memory_space=pltpu.SMEM)] * 2 + [by_row(D)] + any_specs(count),
        out_specs=[by_row(units), by_row(D // 2), by_row(D // 2)],
        out_shape=[shape(units, F32), shape(D // 2, BF16), shape(D // 2, BF16)],
        scratch_shapes=[pltpu.VMEM((1, D, units), BF16), pltpu.SemaphoreType.DMA((len(plan),))],
        cost_estimate=pl.CostEstimate(
            flops=2 * rows * D * units, bytes_accessed=12 << 20, transcendentals=0
        ),
        compiler_params=pltpu.CompilerParams(vmem_limit_bytes=22 << 20),
    )(order, table, upstream, *pieces)


def feed_forward(normed, d_hidden, pieces, plan, table, order):
    rows, units, block = normed.shape[0], pieces[0].shape[-1], normed.shape[0] // 2
    count, part = len(pieces), D // 16

    def across(a, b):
        return lax.dot_general(a, b, (((1,), (1,)), ((), ())), preferred_element_type=F32)

    def kernel(order_ref, table_ref, n_ref, dh_ref, *refs):
        piece_refs, refs = refs[:count], refs[count:]
        hid_ref, dg_ref, du_ref, dn_ref, ff_ref, ng_ref, nk_ref, w_ref, sem = refs

        @pl.when(pl.program_id(0) == 0)
        def _():
            load_weights(piece_refs, plan, table_ref, (0, 1, 2), w_ref, sem, part)

        for i in range(16):
            at = pl.ds(pl.multiple_of(order_ref[i] * part, part), part)
            to = slice((i % 8) * part, (i % 8 + 1) * part)
            (ng_ref if i < 8 else nk_ref)[:, to] = n_ref[:, at]
        for f in range(0, units, 256):
            at = slice(f, f + 256)
            gate = dot(n_ref[...], w_ref[0, :, at])
            up = dot(n_ref[...], w_ref[1, :, at])
            d_hidden = dh_ref[:, at]
            sigmoid = jax.nn.sigmoid(gate)
            activated = gate * sigmoid
            hid_ref[:, at] = (activated * up).astype(BF16)
            dg_ref[:, at] = (
                d_hidden * up * sigmoid * (1.0 + gate * (1.0 - sigmoid))
            ).astype(BF16)
            du_ref[:, at] = (d_hidden * activated).astype(BF16)
        for d in range(0, D, 512):
            at = slice(d, d + 512)
            dn_ref[:, at] = (
                across(dg_ref[...], w_ref[0, at, :]) + across(du_ref[...], w_ref[1, at, :])
            ).astype(BF16)
            ff_ref[:, at] = across(hid_ref[...], w_ref[2, at, :]).astype(BF16)

    by_row = lambda w: pl.BlockSpec((block, w), lambda i: (i, 0))
    shape = lambda w: jax.ShapeDtypeStruct((rows, w), BF16)
    return pl.pallas_call(
        kernel,
        grid=(2,),
        in_specs=[pl.BlockSpec(memory_space=pltpu.SMEM)] * 2
        + [by_row(D), by_row(units)]
        + any_specs(count),
        out_specs=[by_row(units)] * 3 + [by_row(D)] * 2 + [by_row(D // 2)] * 2,
        out_shape=[shape(units)] * 3 + [shape(D)] * 2 + [shape(D // 2)] * 2,
        scratch_shapes=[pltpu.VMEM((3, D, units), BF16), pltpu.SemaphoreType.DMA((len(plan),))],
        cost_estimate=pl.CostEstimate(
            flops=10 * rows * D * units, bytes_accessed=24 << 20, transcendentals=0
        ),
        compiler_params=pltpu.CompilerParams(vmem_limit_bytes=56 << 20),
    )(order, table, normed, d_hidden, *pieces)


def outer_blocks(table, groups, deps=()):
    lefts, rights, plan = [], [], []
    for pairs in groups:
        entry = []
        for left, right in pairs:
            spot = next((n for n, known in enumerate(lefts) if known is left), None)
            if spot is None:
                spot = len(lefts)
                lefts.append(left)
            entry.append((spot, len(rights)))
            rights.append(right)
        plan.append(entry)
    width = sum(pairs[0][1].shape[1] for pairs in groups)
    block = D // 16

    def kernel(table_ref, *refs):
        left_refs, refs = refs[: len(lefts)], refs[len(lefts) :]
        right_refs, (give_ref, keep_ref) = refs[: len(rights)], refs[len(rights) :]
        step = pl.program_id(0)
        turned = [jnp.transpose(r[...]) for r in left_refs]
        parts = []
        for entry in plan:
            part = None
            for spot, n in entry:
                term = dot(turned[spot], right_refs[n][...])
                part = term if part is None else part + term
            parts.append(part.astype(BF16))
        whole = parts[0] if len(parts) == 1 else jnp.concatenate(parts, axis=1)

        @pl.when(step < 8)
        def _():
            give_ref[...] = whole

        @pl.when(step >= 8)
        def _():
            keep_ref[...] = whole

    flops = sum(2 * left.shape[0] * D * right.shape[1] for g in groups for left, right in g)
    return pl.pallas_call(
        after(kernel, 1 + len(lefts) + len(rights), deps),
        grid_spec=pltpu.PrefetchScalarGridSpec(
            num_scalar_prefetch=1,
            grid=(16,),
            in_specs=[pl.BlockSpec((v.shape[0], block), lambda i, t: (0, t[i])) for v in lefts]
            + [pl.BlockSpec(v.shape, lambda i, t: (0, 0)) for v in rights]
            + dep_specs(deps),
            out_specs=[
                pl.BlockSpec((block, width), lambda i, t: (jnp.minimum(i, 7), 0)),
                pl.BlockSpec((block, width), lambda i, t: (jnp.maximum(i - 8, 0), 0)),
            ],
        ),
        out_shape=[jax.ShapeDtypeStruct((8 * block, width), BF16)] * 2,
        cost_estimate=pl.CostEstimate(flops=flops, bytes_accessed=4 << 20, transcendentals=0),
        compiler_params=pltpu.CompilerParams(vmem_limit_bytes=12 << 20),
    )(table, *lefts, *rights, *deps)


def fold_core(keeps, gots, deps=()):
    count, pair = len(keeps), D // 8
    widths = [k.shape[1] for k in keeps]
    starts = [sum(widths[:n]) for n in range(count)]
    deps = list(deps)

    def kernel(*refs):
        keep_refs, got_refs, outs = refs[:count], refs[count : 2 * count], refs[2 * count :]
        for k in range(4):

            @pl.when(pl.program_id(0) == k)
            def _():
                for n in range(count):
                    total = keep_refs[n][...].astype(F32) + got_refs[n][...].astype(F32)
                    to = slice(starts[n], starts[n] + widths[n])
                    outs[k][:, to] = total.astype(outs[k].dtype)

    whole = pl.BlockSpec((pair, sum(widths)), lambda i: (0, 0))
    shape = lambda dtype: jax.ShapeDtypeStruct((pair, sum(widths)), dtype)
    return pl.pallas_call(
        after(kernel, 2 * count, deps),
        grid=(4,),
        in_specs=[pl.BlockSpec((pair, w), lambda i: (i, 0)) for w in widths * 2]
        + dep_specs(deps),
        out_specs=[whole] * 4,
        out_shape=[shape(F32)] + [shape(BF16)] * 3,
        cost_estimate=pl.CostEstimate(
            flops=0, bytes_accessed=12 * pair * sum(widths), transcendentals=0
        ),
        compiler_params=pltpu.CompilerParams(vmem_limit_bytes=(28 << 20) if count > 1 else (8 << 20)),
    )(*keeps, *gots, *deps)


def adamw_kernel(weight, first, second, sums, spot, rate, flip, deps=()):
    def kernel(w_ref, m_ref, v_ref, keep_ref, got_ref, m_out, v_out, w_out, sum_ref):
        grad = keep_ref[...] + got_ref[...].astype(F32)
        if flip:
            grad = jnp.transpose(grad)
        weight = w_ref[...]
        first_new, second_new, weight_new = adamw_step(
            weight, m_ref[...], v_ref[...], grad, rate, DECAY_RATE
        )
        m_out[...] = first_new
        v_out[...] = second_new
        w_out[...] = weight_new
        if flip:
            sum_ref[...] = jnp.zeros_like(sum_ref)
        else:
            sum_ref[...] = jnp.sum(weight.astype(BF16).astype(F32) * grad, axis=1, keepdims=True)

    shape = jax.ShapeDtypeStruct(weight.shape, F32)
    columns = weight.shape[0] if flip else weight.shape[1]
    whole = lambda *shape: pl.BlockSpec(shape, lambda i: (0,) * len(shape))
    view = pl.BlockSpec((D // 16, columns), lambda i: (0, spot // columns))
    return pl.pallas_call(
        after(kernel, 5, deps),
        grid=(1,),
        in_specs=[whole(*weight.shape)] * 3 + [view] * 2 + dep_specs(deps),
        out_specs=[whole(*weight.shape)] * 3 + [whole(D // 16, 1)],
        out_shape=[shape] * 3 + [jax.ShapeDtypeStruct((D // 16, 1), F32)],
        cost_estimate=pl.CostEstimate(
            flops=0, bytes_accessed=28 * weight.size, transcendentals=0
        ),
        compiler_params=pltpu.CompilerParams(vmem_limit_bytes=14 << 20),
    )(weight, first, second, *sums, *deps)


def pick(blocks, axis, index):
    return lax.dynamic_index_in_dim(blocks, index, axis, keepdims=False)


class Here:
    def __init__(self):
        self.x, self.yh, self.c, self.yl, self.z = (
            lax.axis_index(a) for a in ("x", "yh", "c", "yl", "z")
        )

    def ztable(self):
        own = [self.yl * 4 + (self.z + k) % 4 for k in range(4)]
        other = [(1 - self.yl) * 4 + (self.z + k) % 4 for k in range(4)]
        return jnp.stack(own + other).astype(jnp.int32)

    def xtable(self):
        table = []
        for dc in range(2):
            core = self.c if dc == 0 else 1 - self.c
            for k in range(4):
                for dy in range(2):
                    yh = self.yh if dy == 0 else 1 - self.yh
                    table.append(((self.x + k) % 4) * 4 + yh * 2 + core)
        return jnp.stack(table).astype(jnp.int32)

    def scatter_tp(self, terms, extras, finish, out_shape, deps=(), weight=1):
        parts = lax.all_to_all(terms, ("yl", "z"), 0, 0, tiled=True)
        return self.sum_tp_parts(parts, extras, finish, out_shape, deps, weight)

    def sum_tp_parts(self, parts, extras, finish, out_shape, deps=(), weight=1):
        parts = parts.reshape(8, -1, parts.shape[1])

        def kernel(part_ref, *refs):
            total = part_ref[0].astype(F32)
            for n in range(1, 8):
                total = total + part_ref[n].astype(F32)
            finish(total, refs[: len(extras)], refs[len(extras) :])

        return in_vmem(kernel, [parts] + list(extras), out_shape, deps, weight)

    def gather_first(self, both, second):
        over = lax.ppermute(both, "yl", SWAP)
        return [both, over] + [lax.ppermute(second, "z", ring(-k)) for k in (1, 2, 3)]

    def gather_join(self, first):
        both, over, *rest = first
        return both, over, join([(both, 0), (over, 0)]), join([(part, None) for part in rest])

    def gather_second(self, joined):
        both, over, pair, rest = joined
        pieces = [pair] + [lax.ppermute(pair, "z", ring(-k)) for k in (1, 2, 3)]
        return pieces + [both, over, rest, lax.ppermute(rest, "yl", SWAP)]

    def gather_last(self, pieces, deps=(), weight=1):
        spots = [(k, (d,), 4 * d + k) for k in range(4) for d in range(2)]
        spots += [(4, (1,), 8), (5, (1,), 12)]
        spots += [(6, (k,), k + 9) for k in range(3)] + [(7, (k,), k + 13) for k in range(3)]
        plan = [(piece, index, 0, entry) for piece, index, entry in spots]
        table = self.ztable()
        table = jnp.concatenate([2 * table, 2 * table + 1])
        (laid,) = lay(pieces, plan, table, 16, 1, deps, weight)
        return laid.reshape(-1, laid.shape[-1])

    def gather_tp(self, both, second, deps=(), weight=1):
        joined = self.gather_join(self.gather_first(both, second))
        return self.gather_last(self.gather_second(joined), deps, weight)

    def gather_weights(self, shard):
        pair = jnp.stack([shard, lax.ppermute(shard, "yh", SWAP)])
        mine = [pair] + [lax.ppermute(pair, "x", ring(-k)) for k in (1, 2, 3)]
        return mine + [lax.ppermute(p, "c", SWAP) for p in mine]

    def gather_large(self, shard, over, deps):
        pair = join([(shard, None), (over, None)], deps)
        near = [lax.ppermute(pair, "x", ring(-1)), lax.ppermute(pair, "x", ring(1))]
        far = [
            lax.ppermute(near[0][0], "x", ring(-1)),
            lax.ppermute(near[1][1], "x", ring(1)),
        ]
        mine = [pair] + near + far
        plan = [(0, 0, 0), (0, 1, 1), (1, 0, 2), (1, 1, 3), (2, 0, 6), (2, 1, 7)]
        plan += [(3, None, 4), (4, None, 5)]
        plan += [(p + 5, i, e + 8) for p, i, e in plan]
        theirs = [lax.ppermute(p, "c", SWAP) for p in mine]
        return mine + theirs, plan, near

    def scatter_weights(self, total, sends, late=False):
        near = [lax.ppermute(sends[n], "x", ring(n + 1)) for n in (0, 2)]
        far = lax.ppermute(tie(sends[1], near) if late else sends[1], "x", ring(2))
        for part in near + [far]:
            total = total + part.astype(F32)
        n = D // 16
        give = total[n:].astype(BF16)
        return [total[:n], lax.ppermute(give, "yh", SWAP)], near, give

    def gather_ctx(self, own):
        over = lax.ppermute(own, "yh", SWAP)
        pieces = [own, over, lax.ppermute(own, "c", SWAP), lax.ppermute(over, "c", SWAP)]
        table = jnp.stack(
            [
                self.yh * 2 + self.c,
                (1 - self.yh) * 2 + self.c,
                self.yh * 2 + 1 - self.c,
                (1 - self.yh) * 2 + 1 - self.c,
            ]
        ).astype(jnp.int32)
        plan = [(i, None, 0, i) for i in range(4)]
        return lay(pieces, plan, table, 4)[0].reshape(-1, own.shape[1])

    def scatter_ctx(self, terms, deps):
        give, keep = keys_split(terms, self.c.reshape(1).astype(jnp.int32), deps)
        both = keep + lax.ppermute(give, "c", SWAP).astype(F32)
        give = pick(both, 0, 1 - self.yh).astype(BF16)
        return pick(both, 0, self.yh), lax.ppermute(give, "yh", SWAP)

    def sum_tp(self, value):
        value = value + lax.ppermute(value, "yl", SWAP)
        got = [lax.ppermute(value, "z", ring(k)) for k in (1, 2, 3)]
        parts = jnp.stack([value] + got)
        order = jnp.stack([(self.z - j) % 4 for j in range(4)])
        return jnp.sum(jnp.take(parts, order, axis=0), axis=0)


def per_device(
    tokens,
    cotangent,
    lengths,
    groups,
    query_weight,
    query_m,
    query_v,
    kv_weight,
    kv_m,
    kv_v,
    out_weight,
    out_m,
    out_v,
    gate_weight,
    gate_m,
    gate_v,
    up_weight,
    up_m,
    up_v,
    down_weight,
    down_m,
    down_v,
    norm_gains,
    gains_m,
    gains_v,
):
    here = Here()
    row_count = tokens.shape[0]
    group_rows = row_count * 4
    group_id = here.x
    ctx_id = here.yh * 2 + here.c
    tp_id = here.yl * 4 + here.z
    half = row_count // 2
    part = half // 8
    xtable = here.xtable()

    kv_flat = kv_weight.reshape(D // 16, 2 * HD)
    attn_shard = jnp.concatenate([query_weight, kv_flat, out_weight.T], axis=1).astype(BF16)
    q_cols, kv_cols, o_cols = query_weight.shape[1], 2 * HD, out_weight.shape[0]
    cols = q_cols + kv_cols + o_cols
    gains_low = norm_gains.astype(BF16)
    gain_rows = jnp.zeros((16, cols), BF16).at[:2, : D // 16].set(gains_low)
    attn_pieces = here.gather_weights(jnp.concatenate([attn_shard, gain_rows], axis=0))

    units = gate_weight.shape[1]
    ff_shard = jnp.stack([gate_weight, up_weight, down_weight.T]).astype(BF16)
    ff_over = lax.ppermute(ff_shard, "yh", SWAP)

    slots, starts = slot_tables(lengths, groups, group_id, ctx_id * row_count, row_count)
    frequency = ROPE_BASE ** (-2.0 * jnp.arange(HD // 2, dtype=F32) / HD)
    angles = frequency[:, None] * (slots - starts).astype(F32)[None, :]
    cosine, sine = jnp.cos(angles), jnp.sin(angles)
    bounds_forward = block_bounds(slots, starts, KB_FORWARD)
    bounds = block_bounds(slots, starts, KB)
    slot_rows, start_rows = slots.reshape(-1, 1, QB), starts.reshape(-1, 1, QB)

    normed_one, query_raw, kv_local, w_query, w_kv, w_out, gain_values = normed_projections(
        tokens,
        attn_pieces,
        xtable,
        (q_cols, kv_cols, o_cols),
        cosine,
        sine,
        NORM_EPS,
        deps=[ff_over],
    )
    kv_whole = here.gather_ctx(kv_local)
    ff_pieces, ff_plan, weights_near = here.gather_large(ff_shard, ff_over, [kv_local])

    mixed, turned, raw, log_total = attention_forward(
        query_raw, kv_whole, bounds_forward, start_rows, slot_rows, cosine, sine, 0, row_count
    )
    mixed = tie(mixed, weights_near)
    own = lambda v: lax.dynamic_slice_in_dim(v, tp_id * 2 * part, 2 * part, axis=0)
    own_inputs, own_upstream = own(tokens), own(cotangent)
    own_wide = jax.ShapeDtypeStruct((2 * part, D), F32)
    own_low = [jax.ShapeDtypeStruct((2, part, D), BF16), jax.ShapeDtypeStruct((part, D), BF16)]

    def both(outs, value):
        outs[0][0] = value[:part]
        outs[0][1] = value[part:]
        outs[1][...] = value[part:]

    def close_attention(total, ins, outs):
        value = ins[0][...].astype(F32) + total
        outs[0][...] = value
        both(outs[1:], (value * rms_inverse(value) * ins[1][1:2, :]).astype(BF16))

    term = jnp.einsum("ra,da->rd", mixed, w_out, preferred_element_type=F32).astype(BF16)
    hidden_one, *own_normed = here.scatter_tp(
        term, [own_inputs, gain_values], close_attention, [own_wide] + own_low, deps=ff_pieces[5:]
    )
    order = here.xtable()
    order = jnp.concatenate([order[8:], order[:8]])
    d_hidden, upstream_give, upstream_keep = upstream_hidden(
        cotangent, ff_pieces, ff_plan, xtable, order
    )
    normed_two = here.gather_tp(*own_normed, deps=[d_hidden])
    hidden, d_gate, d_up, d_two, out_term, normed_give, normed_keep = feed_forward(
        normed_two, d_hidden, ff_pieces, ff_plan, xtable, order
    )
    outer = lambda a, b: jnp.einsum("rd,rf->df", a, b, preferred_element_type=F32).astype(BF16)
    gives = [outer(normed_give, d_gate), outer(normed_give, d_up), outer(upstream_give, hidden)]
    keeps = [outer(normed_keep, d_gate), outer(normed_keep, d_up), outer(upstream_keep, hidden)]
    gots = [lax.ppermute(give, "c", SWAP) for give in gives]

    ff_total, *ff_sends = fold_core(keeps, gots)

    def close_feed_forward(total, ins, outs):
        value = ins[1][...].astype(F32) + through_norm(total, ins[0][...], ins[2][1:2, :])
        outs[0][...] = value
        both(outs[1:], value.astype(BF16))

    d_hidden_one, *own_branch = here.scatter_tp(
        d_two,
        [hidden_one, own_upstream, gain_values],
        close_feed_forward,
        [own_wide] + own_low,
        weight=20,
    )
    d_branch = here.gather_tp(*own_branch, deps=[ff_total], weight=20)
    d_mixed = jnp.dot(d_branch, w_out, preferred_element_type=F32).astype(BF16)


    ff_sums, ff_near, ff_give = here.scatter_weights(ff_total, ff_sends, True)

    def close_output(total, ins, outs):
        both(outs, (ins[0][...] + total).astype(BF16))

    own_output = here.scatter_tp(
        tie(out_term, [d_branch]), [hidden_one], close_output, own_low
    )
    out_joined = here.gather_join(here.gather_first(*own_output))

    d_query_low, d_kv = attention_backward(
        d_mixed,
        kv_whole,
        turned,
        raw,
        log_total,
        bounds,
        start_rows,
        slot_rows,
        cosine,
        sine,
    )
    d_kv_low = keys_back(
        *here.scatter_ctx(d_kv, ff_near), cosine, sine, deps=out_joined[2:]
    )
    out_second = here.gather_second(out_joined)
    output = here.gather_last(out_second)

    term = (
        jnp.einsum("ra,da->rd", d_query_low, w_query, preferred_element_type=F32)
        + jnp.einsum("rc,dc->rd", d_kv_low, w_kv, preferred_element_type=F32)
    ).astype(BF16)

    term = tie(term, out_second[1:4] + out_second[7:])
    give, keep = outer_blocks(
        order,
        [((normed_one, d_query_low),), ((d_branch, mixed),), ((normed_one, d_kv_low),)],
    )
    attn_got = lax.ppermute(give, "c", SWAP)
    attn_total, *attn_sends = fold_core([keep], [attn_got])
    attn_sums, _, attn_give = here.scatter_weights(attn_total, attn_sends)

    def close_inputs(total, ins, outs):
        value = ins[0][...] + through_norm(total, ins[1][...].astype(F32), ins[2][:1, :])
        both(outs, value.astype(BF16))

    own_results = here.scatter_tp(
        term,
        [d_hidden_one, own_inputs, gain_values],
        close_inputs,
        own_low,
        deps=[attn_give, ff_give],
        weight=50,
    )
    last_pieces = here.gather_second(here.gather_join(here.gather_first(*own_results)))
    tokens_grad = here.gather_last(last_pieces, deps=[output], weight=50)

    late = last_pieces[3:4]
    flat = lambda v: v.reshape(kv_flat.shape)
    fan = D ** (-0.5)
    out_fan = max(1, 4 * D // group_rows) ** (-0.5)
    query_new = adamw_kernel(query_weight, query_m, query_v, attn_sums, 0, fan, False, late)
    out_new = adamw_kernel(out_weight, out_m, out_v, attn_sums, q_cols, out_fan, True)
    kv_new = adamw_kernel(
        kv_flat, flat(kv_m), flat(kv_v), attn_sums, q_cols + o_cols, fan, False
    )
    gate_new = adamw_kernel(gate_weight, gate_m, gate_v, ff_sums, 0, fan, False, late)
    up_new = adamw_kernel(up_weight, up_m, up_v, ff_sums, units, fan, False, late)
    down_new = adamw_kernel(down_weight, down_m, down_v, ff_sums, 2 * units, FF ** (-0.5), True, late)

    gain_sums = jnp.stack([query_new[3] + kv_new[3], gate_new[3] + up_new[3]])[:, :, 0]
    grad_gains = here.sum_tp(tie_small(gain_sums, last_pieces[1])) / gains_low.astype(F32)
    gains_new = adamw_step(norm_gains, gains_m, gains_v, grad_gains, 0.5, 0.0)
    return (
        output,
        tokens_grad,
        *query_new[:3],
        *[v.reshape(kv_weight.shape) for v in kv_new[:3]],
        *out_new[:3],
        *gate_new[:3],
        *up_new[:3],
        *down_new[:3],
        *gains_new,
    )


def solution(mesh):
    fine = Mesh(mesh.devices.reshape(4, 2, 2, 2, 4), ("x", "yh", "c", "yl", "z"))
    rows = ("x", "yh", "c")
    tp = ("yl", "z")
    by_row, by_col, by_unit = P(rows, None), P(rows, tp), P(tp, rows)
    by_kv, by_gain = P(rows, tp, None), P(None, rows)
    in_specs = (
        (by_row,) * 2
        + (P(),) * 2
        + (by_col,) * 3
        + (by_kv,) * 3
        + (by_unit,) * 3
        + (by_col,) * 6
        + (by_unit,) * 3
        + (by_gain,) * 3
    )
    out_specs = (
        (by_row,) * 2
        + (by_col,) * 3
        + (by_kv,) * 3
        + (by_unit,) * 3
        + (by_col,) * 6
        + (by_unit,) * 3
        + (by_gain,) * 3
    )
    return jax.shard_map(
        per_device, mesh=fine, in_specs=in_specs, out_specs=out_specs, check_vma=False
    )
```

```python
import functools

import jax
import jax.numpy as jnp
from jax import lax
from jax.experimental import pallas as pl
from jax.experimental.pallas import tpu as pltpu
from jax.sharding import Mesh
from jax.sharding import PartitionSpec as P

D = 2048
HD = 64
FF = 8192
STEP = 5


NORM_EPS = 1e-05
BETA_FIRST = 0.9
BETA_SECOND = 0.95
ADAM_EPS = 1e-08
DECAY_RATE = 0.1
ROPE_BASE = 500000.0
MASKED_SCORE = -1e30

F32 = jnp.float32
BF16 = jnp.bfloat16
QB = 128
KB = 512
KB_FORWARD = 1024


SWAP = ((0, 1), (1, 0))


def ring(step):
    return tuple((i, (i + step) % 4) for i in range(4))


def dot(a, b):
    return jnp.dot(a, b, preferred_element_type=F32)


def across(a, b):
    return lax.dot_general(a, b, (((1,), (1,)), ((), ())), preferred_element_type=F32)


def turn(value, cosine, sine):
    a, b = value[: HD // 2], value[HD // 2 :]
    return jnp.concatenate([a * cosine - b * sine, b * cosine + a * sine], axis=0)


def heads_to_lanes(wide, heads):
    return jnp.concatenate([wide[h * HD : (h + 1) * HD] for h in range(heads)], axis=1)


def lanes_to_heads(tall, heads):
    n = tall.shape[1] // heads
    return jnp.concatenate([tall[:, h * n : (h + 1) * n] for h in range(heads)], axis=0)


def normed_projections(tokens, pieces, table, widths, cosine, sine, eps, deps=()):
    rows, width = tokens.shape
    block, part = 256, D // 16
    q_cols, kv_cols, o_cols = widths
    deps = list(deps)
    count = len(pieces)

    def kernel(table_ref, t_ref, *refs):
        piece_refs, refs = refs[:count], refs[count:]
        cos_ref, sin_ref, n_ref, q_ref, kv_ref, w_ref, wo_ref, g_ref = refs

        @pl.when(pl.program_id(0) == 0)
        def _():
            for i in range(count):
                for d in range(2):
                    spot = table_ref[2 * i + d]
                    at = pl.ds(pl.multiple_of(spot * part, part), part)
                    body = piece_refs[i][d, :part, :]
                    w_ref[at, :] = body[:, : q_cols + kv_cols]
                    wo_ref[at, :] = body[:, q_cols + kv_cols :]
                    g_ref[:, at] = piece_refs[i][d, part:, :part].astype(F32)[:8]

        x = t_ref[...].astype(F32)
        inv = lax.rsqrt(jnp.mean(x * x, axis=-1, keepdims=True) + eps)
        normed = (x * inv * g_ref[:1, :]).astype(BF16)
        n_ref[...] = normed
        joint = dot(normed, w_ref[...])
        q_ref[...] = joint[:, :q_cols]
        kv = jnp.transpose(joint[:, q_cols:])
        kv = jnp.concatenate([turn(kv[:HD], cos_ref[...], sin_ref[...]), kv[HD:]], axis=0)
        kv_ref[...] = jnp.transpose(kv).astype(BF16)

    whole = lambda *shape: pl.BlockSpec(shape, lambda i: (0,) * len(shape))
    by_row = lambda w: pl.BlockSpec((block, w), lambda i: (i, 0))
    by_lane = pl.BlockSpec((HD // 2, block), lambda i: (0, i))
    return pl.pallas_call(
        after(kernel, 4 + count, deps),
        grid=(rows // block,),
        in_specs=[pl.BlockSpec(memory_space=pltpu.SMEM), by_row(width)]
        + [whole(*p.shape) for p in pieces]
        + [by_lane, by_lane]
        + dep_specs(deps),
        out_specs=[
            by_row(width),
            by_row(q_cols),
            by_row(kv_cols),
            whole(D, q_cols + kv_cols),
            whole(D, o_cols),
            whole(8, D),
        ],
        out_shape=[
            jax.ShapeDtypeStruct((rows, width), BF16),
            jax.ShapeDtypeStruct((rows, q_cols), F32),
            jax.ShapeDtypeStruct((rows, kv_cols), BF16),
            jax.ShapeDtypeStruct((D, q_cols + kv_cols), BF16),
            jax.ShapeDtypeStruct((D, o_cols), BF16),
            jax.ShapeDtypeStruct((8, D), F32),
        ],
        cost_estimate=pl.CostEstimate(
            flops=2 * rows * width * 384, bytes_accessed=12 << 20, transcendentals=0
        ),
        compiler_params=pltpu.CompilerParams(vmem_limit_bytes=24 << 20),
    )(table, tokens, *pieces, cosine, sine, *deps)


def key_ranges(bounds_ref, step):
    return [bounds_ref[step * 4 + n] for n in range(4)]


def attention_forward(query_raw, kv, bounds, starts, slots, cosine, sine, row_offset, rows):
    heads = query_raw.shape[1] // HD
    keys = kv.shape[0]
    wide = heads * QB
    steps, base = rows // QB, row_offset // QB

    def kernel(b_ref, q_ref, kv_ref, start_ref, slot_ref, cos_ref, sin_ref, m_ref, qt_ref, ot_ref, lse_ref, kvt_ref, qp_ref):
        step = pl.program_id(0)

        @pl.when(step == 0)
        def _():
            kvt_ref[...] = jnp.transpose(kv_ref[...].astype(F32)).astype(BF16)

        raw = jnp.transpose(q_ref[...])
        turned = jnp.concatenate(
            [turn(raw[h * HD : (h + 1) * HD], cos_ref[...], sin_ref[...]) for h in range(heads)],
            axis=1,
        ).astype(BF16)
        qt_ref[0] = turned
        scaled = (turned.astype(F32) * HD**-0.5).astype(BF16)
        qp_ref[...] = jnp.concatenate([scaled, jnp.zeros_like(scaled)], axis=0)
        start = jnp.concatenate([start_ref[0]] * heads, axis=1)
        slot = jnp.concatenate([slot_ref[0]] * heads, axis=1)

        def body(masked, j, carry):
            peak, total, acc = carry
            at = pl.multiple_of(j * KB_FORWARD, KB_FORWARD)
            scores = dot(kv_ref[pl.ds(at, KB_FORWARD), :], qp_ref[...])
            if masked:
                key = at + lax.broadcasted_iota(jnp.int32, (KB_FORWARD, wide), 0)
                scores = jnp.where((key >= start) & (key <= slot), scores, MASKED_SCORE)
            new_peak = jnp.maximum(peak, jnp.max(scores, axis=0, keepdims=True))
            powers = jnp.exp(scores - new_peak)
            shrink = jnp.exp(peak - new_peak)
            total = total * shrink + jnp.sum(powers, axis=0, keepdims=True)
            values = kvt_ref[HD:, pl.ds(at, KB_FORWARD)]
            acc = acc * shrink + dot(values, powers.astype(BF16))
            return (new_peak, total, acc)

        first, full_first, full_end, end = key_ranges(b_ref, base + step)
        carry = (
            jnp.full((1, wide), MASKED_SCORE, F32),
            jnp.zeros((1, wide), F32),
            jnp.zeros((HD, wide), F32),
        )
        carry = lax.fori_loop(first, full_first, functools.partial(body, True), carry)
        carry = lax.fori_loop(full_first, full_end, functools.partial(body, False), carry)
        carry = lax.fori_loop(full_end, end, functools.partial(body, True), carry)
        peak, total, acc = carry
        mixed = acc / total
        ot_ref[0] = mixed
        lse_ref[0] = peak + jnp.log(total)
        m_ref[...] = jnp.transpose(lanes_to_heads(mixed, heads)).astype(BF16)

    lane = lambda: pl.BlockSpec((HD // 2, QB), lambda i: (0, base + i))
    row = lambda: pl.BlockSpec((1, 1, QB), lambda i: (base + i, 0, 0))
    return pl.pallas_call(
        kernel,
        grid=(steps,),
        in_specs=[
            pl.BlockSpec(memory_space=pltpu.SMEM),
            pl.BlockSpec((QB, heads * HD), lambda i: (base + i, 0)),
            pl.BlockSpec((keys, 2 * HD), lambda i: (0, 0)),
            row(),
            row(),
            lane(),
            lane(),
        ],
        out_specs=[
            pl.BlockSpec((QB, heads * HD), lambda i: (i, 0)),
            pl.BlockSpec((1, HD, wide), lambda i: (i, 0, 0)),
            pl.BlockSpec((1, HD, wide), lambda i: (i, 0, 0)),
            pl.BlockSpec((1, 1, wide), lambda i: (i, 0, 0)),
        ],
        out_shape=[
            jax.ShapeDtypeStruct((rows, heads * HD), BF16),
            jax.ShapeDtypeStruct((steps, HD, wide), BF16),
            jax.ShapeDtypeStruct((steps, HD, wide), F32),
            jax.ShapeDtypeStruct((steps, 1, wide), F32),
        ],
        scratch_shapes=[pltpu.VMEM((2 * HD, keys), BF16), pltpu.VMEM((2 * HD, wide), BF16)],
        cost_estimate=pl.CostEstimate(
            flops=rows * keys * heads * HD // 8, bytes_accessed=2 << 20, transcendentals=0
        ),
        compiler_params=pltpu.CompilerParams(vmem_limit_bytes=14 << 20),
    )(bounds, query_raw, kv, starts, slots, cosine, sine)


def attention_backward(
    d_mixed, kv, queries, mixed, lse, bounds, starts, slots, cosine, sine, deps=()
):
    rows, width = d_mixed.shape
    heads = width // HD
    keys = kv.shape[0]
    wide = heads * QB
    steps = rows // QB
    deps = list(deps)

    def kernel(b_ref, d_ref, kv_ref, qt_ref, ot_ref, lse_ref, start_ref, slot_ref, cos_ref, sin_ref, dq_ref, dkv_ref, kvt_ref, qp_ref, dp_ref, qr_ref, dr_ref):
        step = pl.program_id(0)

        @pl.when(step == 0)
        def _():
            kvt_ref[...] = jnp.transpose(kv_ref[...].astype(F32)).astype(BF16)
            dkv_ref[...] = jnp.zeros_like(dkv_ref)

        scaled = qt_ref[0].astype(F32) * HD**-0.5
        grads = heads_to_lanes(jnp.transpose(d_ref[...].astype(F32)), heads)
        delta = jnp.sum(grads * ot_ref[0], axis=0, keepdims=True)
        empty = jnp.zeros_like(scaled)
        q_pad = jnp.concatenate([scaled, empty], axis=0)
        d_pad = jnp.concatenate([empty, grads], axis=0)
        qp_ref[...] = q_pad.astype(BF16)
        dp_ref[...] = d_pad.astype(BF16)
        qr_ref[...] = jnp.transpose(q_pad).astype(BF16)
        dr_ref[...] = jnp.transpose(d_pad).astype(BF16)
        start = jnp.concatenate([start_ref[0]] * heads, axis=1)
        slot = jnp.concatenate([slot_ref[0]] * heads, axis=1)
        log_total = lse_ref[0]

        def body(masked, j, d_query):
            at = pl.multiple_of(j * KB, KB)
            block = kv_ref[pl.ds(at, KB), :]
            scores = dot(block, qp_ref[...])
            if masked:
                key = at + lax.broadcasted_iota(jnp.int32, (KB, wide), 0)
                scores = jnp.where((key >= start) & (key <= slot), scores, MASKED_SCORE)
            chances = jnp.exp(scores - log_total)
            d_chances = dot(block, dp_ref[...])
            d_scores = (chances * (d_chances - delta)).astype(BF16)
            dkv_ref[pl.ds(at, KB), :] += dot(chances.astype(BF16), dr_ref[...]) + dot(
                d_scores, qr_ref[...]
            )
            return d_query + dot(kvt_ref[:HD, pl.ds(at, KB)], d_scores)

        first, full_first, full_end, end = key_ranges(b_ref, step)
        d_query = jnp.zeros((HD, wide), F32)
        d_query = lax.fori_loop(first, full_first, functools.partial(body, True), d_query)
        d_query = lax.fori_loop(full_first, full_end, functools.partial(body, False), d_query)
        d_query = lax.fori_loop(full_end, end, functools.partial(body, True), d_query)
        d_query = lanes_to_heads(d_query * HD**-0.5, heads)
        turned = jnp.concatenate(
            [turn(d_query[h * HD : (h + 1) * HD], cos_ref[...], -sin_ref[...]) for h in range(heads)],
            axis=0,
        )
        dq_ref[...] = jnp.transpose(turned).astype(BF16)

    lane = lambda: pl.BlockSpec((HD // 2, QB), lambda i: (0, i))
    row = lambda: pl.BlockSpec((1, 1, QB), lambda i: (i, 0, 0))
    kept = lambda n: pl.BlockSpec((1, n, wide), lambda i: (i, 0, 0))
    return pl.pallas_call(
        after(kernel, 10, deps),
        grid=(steps,),
        in_specs=[
            pl.BlockSpec(memory_space=pltpu.SMEM),
            pl.BlockSpec((QB, width), lambda i: (i, 0)),
            pl.BlockSpec((keys, 2 * HD), lambda i: (0, 0)),
            kept(HD),
            kept(HD),
            kept(1),
            row(),
            row(),
            lane(),
            lane(),
        ]
        + dep_specs(deps),
        out_specs=[
            pl.BlockSpec((QB, width), lambda i: (i, 0)),
            pl.BlockSpec((keys, 2 * HD), lambda i: (0, 0)),
        ],
        out_shape=[
            jax.ShapeDtypeStruct((rows, width), BF16),
            jax.ShapeDtypeStruct((keys, 2 * HD), F32),
        ],
        scratch_shapes=[
            pltpu.VMEM((2 * HD, keys), BF16),
            pltpu.VMEM((2 * HD, wide), BF16),
            pltpu.VMEM((2 * HD, wide), BF16),
            pltpu.VMEM((wide, 2 * HD), BF16),
            pltpu.VMEM((wide, 2 * HD), BF16),
        ],
        cost_estimate=pl.CostEstimate(
            flops=rows * 2 * keys * heads * HD, bytes_accessed=2 << 20, transcendentals=0
        ),
        compiler_params=pltpu.CompilerParams(vmem_limit_bytes=14 << 20),
    )(bounds, d_mixed, kv, queries, mixed, lse, starts, slots, cosine, sine, *deps)


def keys_split(d_kv, core, deps=()):
    rows, width = d_kv.shape
    quarter = rows // 4
    deps = list(deps)

    def kernel(core_ref, d_ref, give_ref, keep_ref):
        core = core_ref[0]
        for n in range(2):
            give_at = pl.multiple_of((2 * n + 1 - core) * quarter, quarter)
            keep_at = pl.multiple_of((2 * n + core) * quarter, quarter)
            give_ref[n] = d_ref[pl.ds(give_at, quarter), :].astype(BF16)
            keep_ref[n] = d_ref[pl.ds(keep_at, quarter), :]

    shape = (2, quarter, width)
    return pl.pallas_call(
        after(kernel, 2, deps),
        out_shape=[jax.ShapeDtypeStruct(shape, BF16), jax.ShapeDtypeStruct(shape, F32)],
        grid=(1,),
        in_specs=[pl.BlockSpec(memory_space=pltpu.SMEM)] + whole_specs([d_kv]) + dep_specs(deps),
        out_specs=whole_specs([jax.ShapeDtypeStruct(shape, BF16)] * 2),
        cost_estimate=pl.CostEstimate(flops=0, bytes_accessed=2 << 20, transcendentals=0),
    )(core, d_kv, *deps)


def keys_middle(keep, got, row):
    _, rows, width = keep.shape

    def kernel(row_ref, keep_ref, got_ref, give_out, keep_out):
        row = row_ref[0]
        give_out[...] = (keep_ref[1 - row] + got_ref[1 - row].astype(F32)).astype(BF16)
        keep_out[...] = keep_ref[row] + got_ref[row].astype(F32)

    shapes = [jax.ShapeDtypeStruct((rows, width), t) for t in (BF16, F32)]
    return pl.pallas_call(
        kernel,
        grid=(1,),
        out_shape=shapes,
        in_specs=[pl.BlockSpec(memory_space=pltpu.SMEM)] + whole_specs([keep, got]),
        out_specs=whole_specs(shapes),
        cost_estimate=pl.CostEstimate(flops=0, bytes_accessed=2 << 20, transcendentals=0),
    )(row, keep, got)


def keys_back(queries, keep, got, w_joint, cosine, sine, deps=()):
    deps = list(deps)

    rows, q_cols = queries.shape
    shapes = [jax.ShapeDtypeStruct((rows, n), BF16) for n in (q_cols + 2 * HD, D)]

    def kernel(q_ref, keep_ref, got_ref, w_ref, cos_ref, sin_ref, out_ref, term_ref):
        out_ref[:, :q_cols] = q_ref[...]
        total = jnp.transpose(keep_ref[...] + got_ref[...].astype(F32))
        turned = turn(total[:HD], cos_ref[...], -sin_ref[...])
        both = jnp.concatenate([turned, total[HD:]], axis=0)
        out_ref[:, q_cols:] = jnp.transpose(both).astype(BF16)
        for n in range(0, rows, 256):
            at = slice(n, n + 256)
            term_ref[at, :] = across(out_ref[at, :], w_ref[...]).astype(BF16)

    return pl.pallas_call(
        after(kernel, 6, deps),
        out_shape=shapes,
        grid=(1,),
        in_specs=whole_specs([queries, keep, got, w_joint, cosine, sine]) + dep_specs(deps),
        out_specs=whole_specs(shapes),
        cost_estimate=pl.CostEstimate(flops=0, bytes_accessed=2 << 20, transcendentals=0),
        compiler_params=pltpu.CompilerParams(vmem_limit_bytes=24 << 20),
    )(queries, keep, got, w_joint, cosine, sine, *deps)


def slot_tables(lengths, groups, group_id, first_slot, rows):
    seq_count = lengths.shape[0]
    seq_order = jnp.arange(seq_count, dtype=jnp.int32)
    same_group = groups[None, :] == groups[:, None]
    before = seq_order[None, :] < seq_order[:, None]
    begins = jnp.sum(jnp.where(same_group & before, lengths[None, :], 0), axis=1)
    ends = begins + lengths
    slots = first_slot + jnp.arange(rows, dtype=jnp.int32)
    inside = (
        (groups == group_id)[:, None]
        & (slots[None, :] >= begins[:, None])
        & (slots[None, :] < ends[:, None])
    )
    starts = jnp.where(
        jnp.any(inside, axis=0), jnp.sum(jnp.where(inside, begins[:, None], 0), axis=0), slots
    )
    return slots, starts


def block_bounds(slots, starts, size):
    first_row, last_row = slots[::QB], slots[QB - 1 :: QB]
    low, high = starts[::QB], starts[QB - 1 :: QB]
    first = low // size
    end = last_row // size + 1
    full_first = jnp.clip((high + size - 1) // size, first, end)
    full_end = jnp.clip((first_row + 1) // size, full_first, end)
    return jnp.stack([first, full_first, full_end, end], axis=1).reshape(-1).astype(jnp.int32)


def adamw_step(weight, first, second, grad, rate, decay):
    first_new = BETA_FIRST * first + (1.0 - BETA_FIRST) * grad
    second_new = BETA_SECOND * second + (1.0 - BETA_SECOND) * grad * grad
    first_hat = first_new / (1.0 - BETA_FIRST**STEP)
    second_hat = second_new / (1.0 - BETA_SECOND**STEP)
    weight_new = weight - rate * (first_hat / (jnp.sqrt(second_hat) + ADAM_EPS) + decay * weight)
    return (first_new, second_new, weight_new)


def after(kernel, inputs, deps):
    count = len(deps)
    if not count:
        return kernel
    return lambda *refs: kernel(*refs[:inputs], *refs[inputs + count :])


def any_specs(count):
    return [pl.BlockSpec(memory_space=pl.ANY)] * count


def dep_specs(deps):
    return [
        pl.BlockSpec((1,) * (d.ndim - 2) + (16, 128), lambda *at, n=d.ndim: (0,) * n) for d in deps
    ]


def whole_specs(arrays):
    return [pl.BlockSpec(v.shape, lambda *at, n=len(v.shape): (0,) * n) for v in arrays]


def tie(value, deps):
    deps = list(deps)
    return pl.pallas_call(
        lambda *refs: None,
        grid=(1,),
        out_shape=jax.ShapeDtypeStruct(value.shape, value.dtype),
        in_specs=any_specs(1) + dep_specs(deps),
        out_specs=pl.BlockSpec(memory_space=pl.ANY),
        input_output_aliases={0: 0},
    )(value, *deps)


def lay(pieces, plan, table, blocks, deps=(), weight=1):
    deps = list(deps)
    n, w = pieces[0].shape[-2:]
    inputs = 1 + len(pieces)
    shapes = [jax.ShapeDtypeStruct((blocks, n, w), BF16), jax.ShapeDtypeStruct((16, 128), BF16)]

    def kernel(table_ref, *refs):
        out_ref, sign_ref = refs[len(pieces) :]
        for piece, index, _, entry in plan:
            source = refs[piece]
            out_ref[table_ref[entry]] = source[...] if index is None else source[index]
        sign_ref[...] = jnp.zeros_like(sign_ref)

    size = sum(p.size * p.dtype.itemsize for p in pieces)
    return pl.pallas_call(
        after(kernel, inputs, deps),
        out_shape=shapes,
        grid=(1,),
        in_specs=[pl.BlockSpec(memory_space=pltpu.SMEM)] + whole_specs(pieces) + dep_specs(deps),
        out_specs=whole_specs(shapes),
        cost_estimate=pl.CostEstimate(flops=0, bytes_accessed=2 * weight * size, transcendentals=0),
        compiler_params=pltpu.CompilerParams(vmem_limit_bytes=3 * size + (3 << 20)),
    )(table, *pieces, *deps)


def tie_small(value, late):
    def kernel(value_ref, out_ref):
        out_ref[...] = value_ref[...]

    return in_vmem(kernel, [value], [jax.ShapeDtypeStruct(value.shape, F32)], [late])[0]


def in_vmem(kernel, inputs, out_shape, deps=(), weight=1):
    deps = list(deps)
    count = len(inputs)
    size = sum(v.size * v.dtype.itemsize for v in list(inputs) + list(out_shape))
    return pl.pallas_call(
        after(kernel, count, deps),
        out_shape=out_shape,
        grid=(1,),
        in_specs=whole_specs(inputs) + dep_specs(deps),
        out_specs=whole_specs(out_shape),
        cost_estimate=pl.CostEstimate(flops=0, bytes_accessed=weight * size, transcendentals=0),
        compiler_params=pltpu.CompilerParams(vmem_limit_bytes=2 * size + (6 << 20)),
    )(*inputs, *deps)


def join(parts, deps=()):
    arrays = []
    for array, _ in parts:
        if not any(array is known for known in arrays):
            arrays.append(array)
    spots = [next(n for n, known in enumerate(arrays) if known is array) for array, _ in parts]
    picked = [array.shape if index is None else array.shape[1:] for array, index in parts]

    def kernel(*refs):
        for n, (spot, (_, index)) in enumerate(zip(spots, parts)):
            refs[-1][n] = refs[spot][...] if index is None else refs[spot][index]

    shape = (len(parts),) + picked[0]
    return in_vmem(kernel, arrays, [jax.ShapeDtypeStruct(shape, BF16)], deps)[0]


def rms_inverse(value):
    return lax.rsqrt(jnp.mean(value * value, axis=-1, keepdims=True) + NORM_EPS)


def through_norm(d_normed, value, gain):
    inverse = rms_inverse(value)
    scaled = d_normed * gain
    pre = value * inverse
    return inverse * (scaled - pre * jnp.mean(scaled * pre, axis=-1, keepdims=True))


def load_weights(piece_refs, plan, table_ref, weights, held, sem, part, meanwhile=None):
    copies = []
    for n, (piece, index, entry) in enumerate(plan):
        source = piece_refs[piece] if index is None else piece_refs[piece].at[index]
        at = pl.ds(pl.multiple_of(table_ref[entry] * part, part), part)
        source = source.at[pl.ds(weights[0], len(weights))]
        copies.append(pltpu.make_async_copy(source, held.at[:, at, :], sem.at[n]))
    for copy in copies:
        copy.start()
    if meanwhile is not None:
        meanwhile()
    for copy in copies:
        copy.wait()


def upstream_hidden(upstream, pieces, plan, table, order):
    rows, units, part = upstream.shape[0], pieces[0].shape[-1], D // 16
    count, block = len(pieces), upstream.shape[0] // 2

    def kernel(order_ref, table_ref, u_ref, *refs):
        piece_refs, (dh_ref, ug_ref, uk_ref, w_ref, sem) = refs[:count], refs[count:]

        @pl.when(pl.program_id(0) == 0)
        def _():
            load_weights(piece_refs, plan, table_ref, (2,), w_ref, sem, part)

        for i in range(16):
            at = pl.ds(pl.multiple_of(order_ref[i] * part, part), part)
            to = slice((i % 8) * part, (i % 8 + 1) * part)
            (ug_ref if i < 8 else uk_ref)[:, to] = u_ref[:, at]
        for f in range(0, units, 256):
            at = slice(f, f + 256)
            dh_ref[:, at] = dot(u_ref[...], w_ref[0, :, at])

    by_row = lambda w: pl.BlockSpec((block, w), lambda i: (i, 0))
    shape = lambda w, t: jax.ShapeDtypeStruct((rows, w), t)
    return pl.pallas_call(
        kernel,
        grid=(2,),
        in_specs=[pl.BlockSpec(memory_space=pltpu.SMEM)] * 2 + [by_row(D)] + any_specs(count),
        out_specs=[by_row(units), by_row(D // 2), by_row(D // 2)],
        out_shape=[shape(units, F32), shape(D // 2, BF16), shape(D // 2, BF16)],
        scratch_shapes=[pltpu.VMEM((1, D, units), BF16), pltpu.SemaphoreType.DMA((len(plan),))],
        cost_estimate=pl.CostEstimate(
            flops=2 * rows * D * units, bytes_accessed=12 << 20, transcendentals=0
        ),
        compiler_params=pltpu.CompilerParams(vmem_limit_bytes=22 << 20),
    )(order, table, upstream, *pieces)


def feed_forward(row_pieces, row_plan, row_table, d_hidden, pieces, plan, table, order):
    rows, units, block = d_hidden.shape[0], pieces[0].shape[-1], d_hidden.shape[0] // 2
    count, part, own = len(pieces), D // 16, rows // 16
    row_count = len(row_pieces)

    def kernel(order_ref, table_ref, row_ref, dh_ref, *refs):
        piece_refs, refs = refs[:count], refs[count:]
        row_refs, refs = refs[:row_count], refs[row_count:]
        hid_ref, dg_ref, du_ref, dn_ref, ff_ref, ng_ref, nk_ref, w_ref, all_ref, sem = refs

        @pl.when(pl.program_id(0) == 0)
        def _():
            def lay_rows():
                for piece, index, _, entry in row_plan:
                    at = pl.ds(pl.multiple_of(row_ref[entry] * own, own), own)
                    all_ref[at, :] = row_refs[piece][index]

            load_weights(piece_refs, plan, table_ref, (0, 1, 2), w_ref, sem, part, lay_rows)

        n_ref = all_ref.at[pl.ds(pl.multiple_of(pl.program_id(0) * block, block), block), :]

        for i in range(16):
            at = pl.ds(pl.multiple_of(order_ref[i] * part, part), part)
            to = slice((i % 8) * part, (i % 8 + 1) * part)
            (ng_ref if i < 8 else nk_ref)[:, to] = n_ref[:, at]
        for f in range(0, units, 256):
            at = slice(f, f + 256)
            gate = dot(n_ref[...], w_ref[0, :, at])
            up = dot(n_ref[...], w_ref[1, :, at])
            d_hidden = dh_ref[:, at]
            sigmoid = jax.nn.sigmoid(gate)
            activated = gate * sigmoid
            hid_ref[:, at] = (activated * up).astype(BF16)
            dg_ref[:, at] = (
                d_hidden * up * sigmoid * (1.0 + gate * (1.0 - sigmoid))
            ).astype(BF16)
            du_ref[:, at] = (d_hidden * activated).astype(BF16)
        for d in range(0, D, 512):
            at = slice(d, d + 512)
            dn_ref[:, at] = (
                across(dg_ref[...], w_ref[0, at, :]) + across(du_ref[...], w_ref[1, at, :])
            ).astype(BF16)
            ff_ref[:, at] = across(hid_ref[...], w_ref[2, at, :]).astype(BF16)

    by_row = lambda w: pl.BlockSpec((block, w), lambda i: (i, 0))
    shape = lambda w: jax.ShapeDtypeStruct((rows, w), BF16)
    return pl.pallas_call(
        kernel,
        grid=(2,),
        in_specs=[pl.BlockSpec(memory_space=pltpu.SMEM)] * 3
        + [by_row(units)]
        + any_specs(count)
        + whole_specs(row_pieces),
        out_specs=[by_row(units)] * 3 + [by_row(D)] * 2 + [by_row(D // 2)] * 2,
        out_shape=[shape(units)] * 3 + [shape(D)] * 2 + [shape(D // 2)] * 2,
        scratch_shapes=[
            pltpu.VMEM((3, D, units), BF16),
            pltpu.VMEM((rows, D), BF16),
            pltpu.SemaphoreType.DMA((len(plan),)),
        ],
        cost_estimate=pl.CostEstimate(
            flops=10 * rows * D * units, bytes_accessed=24 << 20, transcendentals=0
        ),
        compiler_params=pltpu.CompilerParams(vmem_limit_bytes=58 << 20),
    )(order, table, row_table, d_hidden, *pieces, *row_pieces)


def outer_blocks(table, groups, deps=()):
    lefts, rights, plan = [], [], []
    for pairs in groups:
        entry = []
        for left, right in pairs:
            spot = next((n for n, known in enumerate(lefts) if known is left), None)
            if spot is None:
                spot = len(lefts)
                lefts.append(left)
            entry.append((spot, len(rights)))
            rights.append(right)
        plan.append(entry)
    width = sum(pairs[0][1].shape[1] for pairs in groups)
    block = D // 16

    def kernel(table_ref, *refs):
        left_refs, refs = refs[: len(lefts)], refs[len(lefts) :]
        right_refs, (give_ref, keep_ref) = refs[: len(rights)], refs[len(rights) :]
        step = pl.program_id(0)
        turned = [jnp.transpose(r[...]) for r in left_refs]
        parts = []
        for entry in plan:
            part = None
            for spot, n in entry:
                term = dot(turned[spot], right_refs[n][...])
                part = term if part is None else part + term
            parts.append(part.astype(BF16))
        whole = parts[0] if len(parts) == 1 else jnp.concatenate(parts, axis=1)

        @pl.when(step < 8)
        def _():
            give_ref[...] = whole

        @pl.when(step >= 8)
        def _():
            keep_ref[...] = whole

    flops = sum(2 * left.shape[0] * D * right.shape[1] for g in groups for left, right in g)
    return pl.pallas_call(
        after(kernel, 1 + len(lefts) + len(rights), deps),
        grid_spec=pltpu.PrefetchScalarGridSpec(
            num_scalar_prefetch=1,
            grid=(16,),
            in_specs=[pl.BlockSpec((v.shape[0], block), lambda i, t: (0, t[i])) for v in lefts]
            + [pl.BlockSpec(v.shape, lambda i, t: (0, 0)) for v in rights]
            + dep_specs(deps),
            out_specs=[
                pl.BlockSpec((block, width), lambda i, t: (jnp.minimum(i, 7), 0)),
                pl.BlockSpec((block, width), lambda i, t: (jnp.maximum(i - 8, 0), 0)),
            ],
        ),
        out_shape=[jax.ShapeDtypeStruct((8 * block, width), BF16)] * 2,
        cost_estimate=pl.CostEstimate(flops=flops, bytes_accessed=4 << 20, transcendentals=0),
        compiler_params=pltpu.CompilerParams(vmem_limit_bytes=12 << 20),
    )(table, *lefts, *rights, *deps)


def fold_core(keeps, gots, deps=()):
    count, pair = len(keeps), D // 8
    widths = [k.shape[1] for k in keeps]
    starts = [sum(widths[:n]) for n in range(count)]
    deps = list(deps)

    def kernel(*refs):
        keep_refs, got_refs, outs = refs[:count], refs[count : 2 * count], refs[2 * count :]
        for k in range(4):

            @pl.when(pl.program_id(0) == k)
            def _():
                for n in range(count):
                    total = keep_refs[n][...].astype(F32) + got_refs[n][...].astype(F32)
                    to = slice(starts[n], starts[n] + widths[n])
                    outs[k][:, to] = total.astype(outs[k].dtype)

    whole = pl.BlockSpec((pair, sum(widths)), lambda i: (0, 0))
    shape = lambda dtype: jax.ShapeDtypeStruct((pair, sum(widths)), dtype)
    return pl.pallas_call(
        after(kernel, 2 * count, deps),
        grid=(4,),
        in_specs=[pl.BlockSpec((pair, w), lambda i: (i, 0)) for w in widths * 2]
        + dep_specs(deps),
        out_specs=[whole] * 4,
        out_shape=[shape(F32)] + [shape(BF16)] * 3,
        cost_estimate=pl.CostEstimate(
            flops=0, bytes_accessed=12 * pair * sum(widths), transcendentals=0
        ),
        compiler_params=pltpu.CompilerParams(vmem_limit_bytes=(28 << 20) if count > 1 else (8 << 20)),
    )(*keeps, *gots, *deps)


def adamw_kernel(weight, first, second, sums, spot, rate, flip, deps=()):
    def kernel(w_ref, m_ref, v_ref, keep_ref, got_ref, m_out, v_out, w_out, sum_ref):
        grad = keep_ref[...] + got_ref[...].astype(F32)
        if flip:
            grad = jnp.transpose(grad)
        weight = w_ref[...]
        first_new, second_new, weight_new = adamw_step(
            weight, m_ref[...], v_ref[...], grad, rate, DECAY_RATE
        )
        m_out[...] = first_new
        v_out[...] = second_new
        w_out[...] = weight_new
        if flip:
            sum_ref[...] = jnp.zeros_like(sum_ref)
        else:
            sum_ref[...] = jnp.sum(weight.astype(BF16).astype(F32) * grad, axis=1, keepdims=True)

    shape = jax.ShapeDtypeStruct(weight.shape, F32)
    columns = weight.shape[0] if flip else weight.shape[1]
    whole = lambda *shape: pl.BlockSpec(shape, lambda i: (0,) * len(shape))
    view = pl.BlockSpec((D // 16, columns), lambda i: (0, spot // columns))
    return pl.pallas_call(
        after(kernel, 5, deps),
        grid=(1,),
        in_specs=[whole(*weight.shape)] * 3 + [view] * 2 + dep_specs(deps),
        out_specs=[whole(*weight.shape)] * 3 + [whole(D // 16, 1)],
        out_shape=[shape] * 3 + [jax.ShapeDtypeStruct((D // 16, 1), F32)],
        cost_estimate=pl.CostEstimate(
            flops=0, bytes_accessed=28 * weight.size, transcendentals=0
        ),
        compiler_params=pltpu.CompilerParams(vmem_limit_bytes=14 << 20),
    )(weight, first, second, *sums, *deps)


def pick(blocks, axis, index):
    return lax.dynamic_index_in_dim(blocks, index, axis, keepdims=False)


class Here:
    def __init__(self):
        self.x, self.yh, self.c, self.yl, self.z = (
            lax.axis_index(a) for a in ("x", "yh", "c", "yl", "z")
        )

    def ztable(self):
        own = [self.yl * 4 + (self.z + k) % 4 for k in range(4)]
        other = [(1 - self.yl) * 4 + (self.z + k) % 4 for k in range(4)]
        return jnp.stack(own + other).astype(jnp.int32)

    def xtable(self):
        table = []
        for dc in range(2):
            core = self.c if dc == 0 else 1 - self.c
            for k in range(4):
                for dy in range(2):
                    yh = self.yh if dy == 0 else 1 - self.yh
                    table.append(((self.x + k) % 4) * 4 + yh * 2 + core)
        return jnp.stack(table).astype(jnp.int32)

    def scatter_tp(self, terms, extras, finish, out_shape, deps=(), weight=1):
        parts = lax.all_to_all(terms, ("yl", "z"), 0, 0, tiled=True)
        return self.sum_tp_parts(parts, extras, finish, out_shape, deps, weight)

    def sum_tp_parts(self, parts, extras, finish, out_shape, deps=(), weight=1):
        parts = parts.reshape(8, -1, parts.shape[1])

        def kernel(part_ref, *refs):
            total = part_ref[0].astype(F32)
            for n in range(1, 8):
                total = total + part_ref[n].astype(F32)
            finish(total, refs[: len(extras)], refs[len(extras) :])

        return in_vmem(kernel, [parts] + list(extras), out_shape, deps, weight)

    def gather_first(self, both, second):
        over = lax.ppermute(both, "yl", SWAP)
        return [both, over] + [lax.ppermute(second, "z", ring(-k)) for k in (1, 2, 3)]

    def gather_join(self, first, deps=()):
        both, over, *rest = first
        rest = join([(part, None) for part in rest], deps)
        return both, over, join([(both, 0), (over, 0)]), rest

    def gather_second(self, joined):
        both, over, pair, rest = joined
        pieces = [pair] + [lax.ppermute(pair, "z", ring(-k)) for k in (1, 2, 3)]
        return pieces + [both, over, rest, lax.ppermute(rest, "yl", SWAP)]

    def gather_plan(self):
        spots = [(k, (d,), 4 * d + k) for k in range(4) for d in range(2)]
        spots += [(4, (1,), 8), (5, (1,), 12)]
        spots += [(6, (k,), k + 9) for k in range(3)] + [(7, (k,), k + 13) for k in range(3)]
        plan = [(piece, index, 0, entry) for piece, index, entry in spots]
        table = self.ztable()
        return plan, jnp.concatenate([2 * table, 2 * table + 1])

    def gather_last(self, pieces, deps=(), weight=1):
        plan, table = self.gather_plan()
        laid, sign = lay(pieces, plan, table, 16, deps, weight)
        return laid.reshape(-1, laid.shape[-1]), sign

    def gather_tp(self, both, second, deps=(), weight=1):
        joined = self.gather_join(self.gather_first(both, second))
        return self.gather_last(self.gather_second(joined), deps, weight)[0]

    def gather_weights(self, shard):
        pair = jnp.stack([shard, lax.ppermute(shard, "yh", SWAP)])
        mine = [pair] + [lax.ppermute(pair, "x", ring(-k)) for k in (1, 2, 3)]
        return mine + [lax.ppermute(p, "c", SWAP) for p in mine]

    def gather_large(self, shard, over, deps):
        pair = join([(shard, None), (over, None)], deps)
        near = [lax.ppermute(pair, "x", ring(-1)), lax.ppermute(pair, "x", ring(1))]
        far = [
            lax.ppermute(near[0][0], "x", ring(-1)),
            lax.ppermute(near[1][1], "x", ring(1)),
        ]
        mine = [pair] + near + far
        plan = [(0, 0, 0), (0, 1, 1), (1, 0, 2), (1, 1, 3), (2, 0, 6), (2, 1, 7)]
        plan += [(3, None, 4), (4, None, 5)]
        plan += [(p + 5, i, e + 8) for p, i, e in plan]
        theirs = [lax.ppermute(p, "c", SWAP) for p in mine]
        return mine + theirs, plan, near

    def scatter_weights(self, total, sends, late=False):
        near = [lax.ppermute(sends[n], "x", ring(n + 1)) for n in (0, 2)]
        far = lax.ppermute(tie(sends[1], near) if late else sends[1], "x", ring(2))
        for part in near + [far]:
            total = total + part.astype(F32)
        n = D // 16
        give = total[n:].astype(BF16)
        return [total[:n], lax.ppermute(give, "yh", SWAP)], near, give

    def gather_ctx(self, own):
        over = lax.ppermute(own, "yh", SWAP)
        pieces = [own, over, lax.ppermute(own, "c", SWAP), lax.ppermute(over, "c", SWAP)]
        table = jnp.stack(
            [
                self.yh * 2 + self.c,
                (1 - self.yh) * 2 + self.c,
                self.yh * 2 + 1 - self.c,
                (1 - self.yh) * 2 + 1 - self.c,
            ]
        ).astype(jnp.int32)
        plan = [(i, None, 0, i) for i in range(4)]
        return lay(pieces, plan, table, 4)[0].reshape(-1, own.shape[1])

    def scatter_ctx(self, terms, deps):
        give, keep = keys_split(terms, self.c.reshape(1).astype(jnp.int32), deps)
        got = lax.ppermute(give, "c", SWAP)
        give, keep = keys_middle(keep, got, self.yh.reshape(1).astype(jnp.int32))
        return keep, lax.ppermute(give, "yh", SWAP)

    def sum_tp(self, value):
        value = value + lax.ppermute(value, "yl", SWAP)
        got = [lax.ppermute(value, "z", ring(k)) for k in (1, 2, 3)]
        parts = jnp.stack([value] + got)
        order = jnp.stack([(self.z - j) % 4 for j in range(4)])
        return jnp.sum(jnp.take(parts, order, axis=0), axis=0)


def per_device(
    tokens,
    cotangent,
    lengths,
    groups,
    query_weight,
    query_m,
    query_v,
    kv_weight,
    kv_m,
    kv_v,
    out_weight,
    out_m,
    out_v,
    gate_weight,
    gate_m,
    gate_v,
    up_weight,
    up_m,
    up_v,
    down_weight,
    down_m,
    down_v,
    norm_gains,
    gains_m,
    gains_v,
):
    here = Here()
    row_count = tokens.shape[0]
    group_rows = row_count * 4
    group_id = here.x
    ctx_id = here.yh * 2 + here.c
    tp_id = here.yl * 4 + here.z
    half = row_count // 2
    part = half // 8
    xtable = here.xtable()

    kv_flat = kv_weight.reshape(D // 16, 2 * HD)
    attn_shard = jnp.concatenate([query_weight, kv_flat, out_weight.T], axis=1).astype(BF16)
    q_cols, kv_cols, o_cols = query_weight.shape[1], 2 * HD, out_weight.shape[0]
    cols = q_cols + kv_cols + o_cols
    gains_low = norm_gains.astype(BF16)
    gain_rows = jnp.zeros((16, cols), BF16).at[:2, : D // 16].set(gains_low)
    attn_pieces = here.gather_weights(jnp.concatenate([attn_shard, gain_rows], axis=0))

    units = gate_weight.shape[1]
    ff_shard = jnp.stack([gate_weight, up_weight, down_weight.T]).astype(BF16)
    ff_over = lax.ppermute(ff_shard, "yh", SWAP)

    slots, starts = slot_tables(lengths, groups, group_id, ctx_id * row_count, row_count)
    frequency = ROPE_BASE ** (-2.0 * jnp.arange(HD // 2, dtype=F32) / HD)
    angles = frequency[:, None] * (slots - starts).astype(F32)[None, :]
    cosine, sine = jnp.cos(angles), jnp.sin(angles)
    bounds_forward = block_bounds(slots, starts, KB_FORWARD)
    bounds = block_bounds(slots, starts, KB)
    slot_rows, start_rows = slots.reshape(-1, 1, QB), starts.reshape(-1, 1, QB)

    normed_one, query_raw, kv_local, w_joint, w_out, gain_values = normed_projections(
        tokens,
        attn_pieces,
        xtable,
        (q_cols, kv_cols, o_cols),
        cosine,
        sine,
        NORM_EPS,
        deps=[ff_over],
    )
    kv_whole = here.gather_ctx(kv_local)
    ff_pieces, ff_plan, weights_near = here.gather_large(ff_shard, ff_over, [kv_local])

    mixed, turned, raw, log_total = attention_forward(
        query_raw, kv_whole, bounds_forward, start_rows, slot_rows, cosine, sine, 0, row_count
    )
    mixed = tie(mixed, weights_near)
    own = lambda v: lax.dynamic_slice_in_dim(v, tp_id * 2 * part, 2 * part, axis=0)
    own_inputs, own_upstream = own(tokens), own(cotangent)
    own_wide = jax.ShapeDtypeStruct((2 * part, D), F32)
    own_low = [jax.ShapeDtypeStruct((2, part, D), BF16), jax.ShapeDtypeStruct((part, D), BF16)]

    def both(outs, value):
        outs[0][0] = value[:part]
        outs[0][1] = value[part:]
        outs[1][...] = value[part:]

    def close_attention(total, ins, outs):
        value = ins[0][...].astype(F32) + total
        outs[0][...] = value
        both(outs[1:], (value * rms_inverse(value) * ins[1][1:2, :]).astype(BF16))

    term = jnp.einsum("ra,da->rd", mixed, w_out, preferred_element_type=F32).astype(BF16)
    hidden_one, *own_normed = here.scatter_tp(
        term, [own_inputs, gain_values], close_attention, [own_wide] + own_low, deps=ff_pieces[5:]
    )
    order = here.xtable()
    order = jnp.concatenate([order[8:], order[:8]])
    d_hidden, upstream_give, upstream_keep = upstream_hidden(
        cotangent, ff_pieces, ff_plan, xtable, order
    )
    joined = here.gather_join(here.gather_first(*own_normed), [d_hidden])
    row_pieces = here.gather_second(joined)
    hidden, d_gate, d_up, d_two, out_term, normed_give, normed_keep = feed_forward(
        row_pieces, *here.gather_plan(), d_hidden, ff_pieces, ff_plan, xtable, order
    )
    outer = lambda a, b: jnp.einsum("rd,rf->df", a, b, preferred_element_type=F32).astype(BF16)
    gives = [outer(normed_give, d_gate), outer(normed_give, d_up), outer(upstream_give, hidden)]
    keeps = [outer(normed_keep, d_gate), outer(normed_keep, d_up), outer(upstream_keep, hidden)]
    gots = [lax.ppermute(give, "c", SWAP) for give in gives]

    ff_total, *ff_sends = fold_core(keeps, gots)

    def close_feed_forward(total, ins, outs):
        value = ins[1][...].astype(F32) + through_norm(total, ins[0][...], ins[2][1:2, :])
        outs[0][...] = value
        both(outs[1:], value.astype(BF16))

    d_hidden_one, *own_branch = here.scatter_tp(
        d_two,
        [hidden_one, own_upstream, gain_values],
        close_feed_forward,
        [own_wide] + own_low,
        weight=20,
    )
    d_branch = here.gather_tp(*own_branch, deps=[ff_total], weight=20)
    d_mixed = jnp.dot(d_branch, w_out, preferred_element_type=F32).astype(BF16)


    ff_sums, ff_near, ff_give = here.scatter_weights(ff_total, ff_sends, True)

    def close_output(total, ins, outs):
        both(outs, (ins[0][...] + total).astype(BF16))

    own_output = here.scatter_tp(
        tie(out_term, [d_branch]), [hidden_one], close_output, own_low
    )
    out_joined = here.gather_join(here.gather_first(*own_output))

    d_query_low, d_kv = attention_backward(
        d_mixed,
        kv_whole,
        turned,
        raw,
        log_total,
        bounds,
        start_rows,
        slot_rows,
        cosine,
        sine,
    )
    d_joint, term = keys_back(
        d_query_low, *here.scatter_ctx(d_kv, ff_near), w_joint, cosine, sine, deps=out_joined[2:]
    )
    out_second = here.gather_second(out_joined)
    output, out_sign = here.gather_last(out_second)

    term = tie(term, [])

    give, keep = outer_blocks(
        order,
        [((d_branch, mixed),), ((normed_one, d_joint),)],
        deps=[term],
    )
    attn_got = lax.ppermute(give, "c", SWAP)
    attn_total, *attn_sends = fold_core([keep], [attn_got])
    attn_sums, _, attn_give = here.scatter_weights(attn_total, attn_sends)

    def close_inputs(total, ins, outs):
        value = ins[0][...] + through_norm(total, ins[1][...].astype(F32), ins[2][:1, :])
        both(outs, value.astype(BF16))

    own_results = here.scatter_tp(
        term,
        [d_hidden_one, own_inputs, gain_values],
        close_inputs,
        own_low,
        deps=[ff_give, out_sign],
        weight=50,
    )
    last_pieces = here.gather_second(here.gather_join(here.gather_first(*own_results)))
    tokens_grad, _ = here.gather_last(last_pieces, deps=attn_sums[1:], weight=50)

    late = own_results[1:2]
    flat = lambda v: v.reshape(kv_flat.shape)
    fan = D ** (-0.5)
    out_fan = max(1, 4 * D // group_rows) ** (-0.5)
    query_new = adamw_kernel(query_weight, query_m, query_v, attn_sums, o_cols, fan, False, late)
    out_new = adamw_kernel(out_weight, out_m, out_v, attn_sums, 0, out_fan, True)
    kv_new = adamw_kernel(
        kv_flat, flat(kv_m), flat(kv_v), attn_sums, q_cols + o_cols, fan, False
    )
    gate_new = adamw_kernel(gate_weight, gate_m, gate_v, ff_sums, 0, fan, False, late)
    up_new = adamw_kernel(up_weight, up_m, up_v, ff_sums, units, fan, False, late)
    down_new = adamw_kernel(down_weight, down_m, down_v, ff_sums, 2 * units, FF ** (-0.5), True, late)

    gain_sums = jnp.stack([query_new[3] + kv_new[3], gate_new[3] + up_new[3]])[:, :, 0]
    grad_gains = here.sum_tp(tie_small(gain_sums, last_pieces[1])) / gains_low.astype(F32)
    gains_new = adamw_step(norm_gains, gains_m, gains_v, grad_gains, 0.5, 0.0)
    return (
        output,
        tokens_grad,
        *query_new[:3],
        *[v.reshape(kv_weight.shape) for v in kv_new[:3]],
        *out_new[:3],
        *gate_new[:3],
        *up_new[:3],
        *down_new[:3],
        *gains_new,
    )


def solution(mesh):
    fine = Mesh(mesh.devices.reshape(4, 2, 2, 2, 4), ("x", "yh", "c", "yl", "z"))
    rows = ("x", "yh", "c")
    tp = ("yl", "z")
    by_row, by_col, by_unit = P(rows, None), P(rows, tp), P(tp, rows)
    by_kv, by_gain = P(rows, tp, None), P(None, rows)
    in_specs = (
        (by_row,) * 2
        + (P(),) * 2
        + (by_col,) * 3
        + (by_kv,) * 3
        + (by_unit,) * 3
        + (by_col,) * 6
        + (by_unit,) * 3
        + (by_gain,) * 3
    )
    out_specs = (
        (by_row,) * 2
        + (by_col,) * 3
        + (by_kv,) * 3
        + (by_unit,) * 3
        + (by_col,) * 6
        + (by_unit,) * 3
        + (by_gain,) * 3
    )
    return jax.shard_map(
        per_device, mesh=fine, in_specs=in_specs, out_specs=out_specs, check_vma=False
    )
```

```python
import functools

import jax
import jax.numpy as jnp
from jax import lax
from jax.experimental import pallas as pl
from jax.experimental.pallas import tpu as pltpu
from jax.sharding import Mesh
from jax.sharding import PartitionSpec as P

D = 2048
HD = 64
FF = 8192
STEP = 5


NORM_EPS = 1e-05
BETA_FIRST = 0.9
BETA_SECOND = 0.95
ADAM_EPS = 1e-08
DECAY_RATE = 0.1
ROPE_BASE = 500000.0
MASKED_SCORE = -1e30

F32 = jnp.float32
BF16 = jnp.bfloat16
QB = 128
KB = 512
KB_FORWARD = 1024


SWAP = ((0, 1), (1, 0))


def ring(step):
    return tuple((i, (i + step) % 4) for i in range(4))


def dot(a, b):
    return jnp.dot(a, b, preferred_element_type=F32)


def across(a, b):
    return lax.dot_general(a, b, (((1,), (1,)), ((), ())), preferred_element_type=F32)


def turn(value, cosine, sine):
    a, b = value[: HD // 2], value[HD // 2 :]
    return jnp.concatenate([a * cosine - b * sine, b * cosine + a * sine], axis=0)


def heads_to_lanes(wide, heads):
    return jnp.concatenate([wide[h * HD : (h + 1) * HD] for h in range(heads)], axis=1)


def lanes_to_heads(tall, heads):
    n = tall.shape[1] // heads
    return jnp.concatenate([tall[:, h * n : (h + 1) * n] for h in range(heads)], axis=0)


def normed_projections(tokens, pieces, table, widths, cosine, sine, eps, deps=()):
    rows, width = tokens.shape
    block, part = 256, D // 16
    q_cols, kv_cols, o_cols = widths
    deps = list(deps)
    count = len(pieces)

    def kernel(table_ref, t_ref, *refs):
        piece_refs, refs = refs[:count], refs[count:]
        cos_ref, sin_ref, n_ref, q_ref, kv_ref, w_ref, wo_ref, g_ref = refs

        @pl.when(pl.program_id(0) == 0)
        def _():
            for i in range(count):
                for d in range(2):
                    spot = table_ref[2 * i + d]
                    at = pl.ds(pl.multiple_of(spot * part, part), part)
                    body = piece_refs[i][d, :part, :]
                    w_ref[at, :] = body[:, : q_cols + kv_cols]
                    wo_ref[at, :] = body[:, q_cols + kv_cols :]
                    g_ref[:, at] = piece_refs[i][d, part:, :part].astype(F32)[:8]

        x = t_ref[...].astype(F32)
        inv = lax.rsqrt(jnp.mean(x * x, axis=-1, keepdims=True) + eps)
        normed = (x * inv * g_ref[:1, :]).astype(BF16)
        n_ref[...] = normed
        joint = dot(normed, w_ref[...])
        q_ref[...] = joint[:, :q_cols]
        kv = jnp.transpose(joint[:, q_cols:])
        kv = jnp.concatenate([turn(kv[:HD], cos_ref[...], sin_ref[...]), kv[HD:]], axis=0)
        kv_ref[...] = jnp.transpose(kv).astype(BF16)

    whole = lambda *shape: pl.BlockSpec(shape, lambda i: (0,) * len(shape))
    by_row = lambda w: pl.BlockSpec((block, w), lambda i: (i, 0))
    by_lane = pl.BlockSpec((HD // 2, block), lambda i: (0, i))
    return pl.pallas_call(
        after(kernel, 4 + count, deps),
        grid=(rows // block,),
        in_specs=[pl.BlockSpec(memory_space=pltpu.SMEM), by_row(width)]
        + [whole(*p.shape) for p in pieces]
        + [by_lane, by_lane]
        + dep_specs(deps),
        out_specs=[
            by_row(width),
            by_row(q_cols),
            by_row(kv_cols),
            whole(D, q_cols + kv_cols),
            whole(D, o_cols),
            whole(8, D),
        ],
        out_shape=[
            jax.ShapeDtypeStruct((rows, width), BF16),
            jax.ShapeDtypeStruct((rows, q_cols), F32),
            jax.ShapeDtypeStruct((rows, kv_cols), BF16),
            jax.ShapeDtypeStruct((D, q_cols + kv_cols), BF16),
            jax.ShapeDtypeStruct((D, o_cols), BF16),
            jax.ShapeDtypeStruct((8, D), F32),
        ],
        cost_estimate=pl.CostEstimate(
            flops=2 * rows * width * 384, bytes_accessed=12 << 20, transcendentals=0
        ),
        compiler_params=pltpu.CompilerParams(vmem_limit_bytes=24 << 20),
    )(table, tokens, *pieces, cosine, sine, *deps)


def key_ranges(bounds_ref, step):
    return [bounds_ref[step * 4 + n] for n in range(4)]


def attention_forward(query_raw, kv, bounds, starts, slots, cosine, sine, row_offset, rows):
    heads = query_raw.shape[1] // HD
    keys = kv.shape[0]
    wide = heads * QB
    steps, base = rows // QB, row_offset // QB

    def kernel(b_ref, q_ref, kv_ref, start_ref, slot_ref, cos_ref, sin_ref, m_ref, qt_ref, ot_ref, lse_ref, kvt_ref, qp_ref):
        step = pl.program_id(0)

        @pl.when(step == 0)
        def _():
            kvt_ref[...] = jnp.transpose(kv_ref[...].astype(F32)).astype(BF16)

        raw = jnp.transpose(q_ref[...])
        turned = jnp.concatenate(
            [turn(raw[h * HD : (h + 1) * HD], cos_ref[...], sin_ref[...]) for h in range(heads)],
            axis=1,
        ).astype(BF16)
        qt_ref[0] = turned
        scaled = (turned.astype(F32) * HD**-0.5).astype(BF16)
        qp_ref[...] = jnp.concatenate([scaled, jnp.zeros_like(scaled)], axis=0)
        start = jnp.concatenate([start_ref[0]] * heads, axis=1)
        slot = jnp.concatenate([slot_ref[0]] * heads, axis=1)

        def body(masked, j, carry):
            peak, total, acc = carry
            at = pl.multiple_of(j * KB_FORWARD, KB_FORWARD)
            scores = dot(kv_ref[pl.ds(at, KB_FORWARD), :], qp_ref[...])
            if masked:
                key = at + lax.broadcasted_iota(jnp.int32, (KB_FORWARD, wide), 0)
                scores = jnp.where((key >= start) & (key <= slot), scores, MASKED_SCORE)
            new_peak = jnp.maximum(peak, jnp.max(scores, axis=0, keepdims=True))
            powers = jnp.exp(scores - new_peak)
            shrink = jnp.exp(peak - new_peak)
            total = total * shrink + jnp.sum(powers, axis=0, keepdims=True)
            values = kvt_ref[HD:, pl.ds(at, KB_FORWARD)]
            acc = acc * shrink + dot(values, powers.astype(BF16))
            return (new_peak, total, acc)

        first, full_first, full_end, end = key_ranges(b_ref, base + step)
        carry = (
            jnp.full((1, wide), MASKED_SCORE, F32),
            jnp.zeros((1, wide), F32),
            jnp.zeros((HD, wide), F32),
        )
        carry = lax.fori_loop(first, full_first, functools.partial(body, True), carry)
        carry = lax.fori_loop(full_first, full_end, functools.partial(body, False), carry)
        carry = lax.fori_loop(full_end, end, functools.partial(body, True), carry)
        peak, total, acc = carry
        mixed = acc / total
        ot_ref[0] = mixed
        lse_ref[0] = peak + jnp.log(total)
        m_ref[...] = jnp.transpose(lanes_to_heads(mixed, heads)).astype(BF16)

    lane = lambda: pl.BlockSpec((HD // 2, QB), lambda i: (0, base + i))
    row = lambda: pl.BlockSpec((1, 1, QB), lambda i: (base + i, 0, 0))
    return pl.pallas_call(
        kernel,
        grid=(steps,),
        in_specs=[
            pl.BlockSpec(memory_space=pltpu.SMEM),
            pl.BlockSpec((QB, heads * HD), lambda i: (base + i, 0)),
            pl.BlockSpec((keys, 2 * HD), lambda i: (0, 0)),
            row(),
            row(),
            lane(),
            lane(),
        ],
        out_specs=[
            pl.BlockSpec((QB, heads * HD), lambda i: (i, 0)),
            pl.BlockSpec((1, HD, wide), lambda i: (i, 0, 0)),
            pl.BlockSpec((1, HD, wide), lambda i: (i, 0, 0)),
            pl.BlockSpec((1, 1, wide), lambda i: (i, 0, 0)),
        ],
        out_shape=[
            jax.ShapeDtypeStruct((rows, heads * HD), BF16),
            jax.ShapeDtypeStruct((steps, HD, wide), BF16),
            jax.ShapeDtypeStruct((steps, HD, wide), F32),
            jax.ShapeDtypeStruct((steps, 1, wide), F32),
        ],
        scratch_shapes=[pltpu.VMEM((2 * HD, keys), BF16), pltpu.VMEM((2 * HD, wide), BF16)],
        cost_estimate=pl.CostEstimate(
            flops=rows * keys * heads * HD // 8, bytes_accessed=2 << 20, transcendentals=0
        ),
        compiler_params=pltpu.CompilerParams(vmem_limit_bytes=14 << 20),
    )(bounds, query_raw, kv, starts, slots, cosine, sine)


def attention_backward(
    d_mixed, kv, queries, mixed, lse, bounds, starts, slots, cosine, sine, core, deps=()
):
    rows, width = d_mixed.shape
    heads = width // HD
    keys = kv.shape[0]
    wide = heads * QB
    steps = rows // QB
    deps = list(deps)

    def kernel(b_ref, core_ref, d_ref, kv_ref, qt_ref, ot_ref, lse_ref, start_ref, slot_ref, cos_ref, sin_ref, dq_ref, give_ref, keep_ref, dkv_ref, kvt_ref, qp_ref, dp_ref, qr_ref, dr_ref):
        step = pl.program_id(0)

        @pl.when(step == 0)
        def _():
            kvt_ref[...] = jnp.transpose(kv_ref[...].astype(F32)).astype(BF16)
            dkv_ref[...] = jnp.zeros_like(dkv_ref)

        scaled = qt_ref[0].astype(F32) * HD**-0.5
        grads = heads_to_lanes(jnp.transpose(d_ref[...].astype(F32)), heads)
        delta = jnp.sum(grads * ot_ref[0], axis=0, keepdims=True)
        empty = jnp.zeros_like(scaled)
        q_pad = jnp.concatenate([scaled, empty], axis=0)
        d_pad = jnp.concatenate([empty, grads], axis=0)
        qp_ref[...] = q_pad.astype(BF16)
        dp_ref[...] = d_pad.astype(BF16)
        qr_ref[...] = jnp.transpose(q_pad).astype(BF16)
        dr_ref[...] = jnp.transpose(d_pad).astype(BF16)
        start = jnp.concatenate([start_ref[0]] * heads, axis=1)
        slot = jnp.concatenate([slot_ref[0]] * heads, axis=1)
        log_total = lse_ref[0]

        def body(masked, j, d_query):
            at = pl.multiple_of(j * KB, KB)
            block = kv_ref[pl.ds(at, KB), :]
            scores = dot(block, qp_ref[...])
            if masked:
                key = at + lax.broadcasted_iota(jnp.int32, (KB, wide), 0)
                scores = jnp.where((key >= start) & (key <= slot), scores, MASKED_SCORE)
            chances = jnp.exp(scores - log_total)
            d_chances = dot(block, dp_ref[...])
            d_scores = (chances * (d_chances - delta)).astype(BF16)
            dkv_ref[pl.ds(at, KB), :] += dot(chances.astype(BF16), dr_ref[...]) + dot(
                d_scores, qr_ref[...]
            )
            return d_query + dot(kvt_ref[:HD, pl.ds(at, KB)], d_scores)

        first, full_first, full_end, end = key_ranges(b_ref, step)
        d_query = jnp.zeros((HD, wide), F32)
        d_query = lax.fori_loop(first, full_first, functools.partial(body, True), d_query)
        d_query = lax.fori_loop(full_first, full_end, functools.partial(body, False), d_query)
        d_query = lax.fori_loop(full_end, end, functools.partial(body, True), d_query)
        d_query = lanes_to_heads(d_query * HD**-0.5, heads)
        turned = jnp.concatenate(
            [turn(d_query[h * HD : (h + 1) * HD], cos_ref[...], -sin_ref[...]) for h in range(heads)],
            axis=0,
        )
        dq_ref[...] = jnp.transpose(turned).astype(BF16)

        @pl.when(step == steps - 1)
        def _():
            for n in range(2):
                give_at = pl.multiple_of((2 * n + 1 - core_ref[0]) * rows, rows)
                keep_at = pl.multiple_of((2 * n + core_ref[0]) * rows, rows)
                give_ref[n] = dkv_ref[pl.ds(give_at, rows), :].astype(BF16)
                keep_ref[n] = dkv_ref[pl.ds(keep_at, rows), :]

    lane = lambda: pl.BlockSpec((HD // 2, QB), lambda i: (0, i))
    row = lambda: pl.BlockSpec((1, 1, QB), lambda i: (i, 0, 0))
    kept = lambda n: pl.BlockSpec((1, n, wide), lambda i: (i, 0, 0))
    return pl.pallas_call(
        after(kernel, 11, deps),
        grid=(steps,),
        in_specs=[
            pl.BlockSpec(memory_space=pltpu.SMEM),
            pl.BlockSpec(memory_space=pltpu.SMEM),
            pl.BlockSpec((QB, width), lambda i: (i, 0)),
            pl.BlockSpec((keys, 2 * HD), lambda i: (0, 0)),
            kept(HD),
            kept(HD),
            kept(1),
            row(),
            row(),
            lane(),
            lane(),
        ]
        + dep_specs(deps),
        out_specs=[
            pl.BlockSpec((QB, width), lambda i: (i, 0)),
            pl.BlockSpec((2, rows, 2 * HD), lambda i: (0, 0, 0)),
            pl.BlockSpec((2, rows, 2 * HD), lambda i: (0, 0, 0)),
        ],
        out_shape=[
            jax.ShapeDtypeStruct((rows, width), BF16),
            jax.ShapeDtypeStruct((2, rows, 2 * HD), BF16),
            jax.ShapeDtypeStruct((2, rows, 2 * HD), F32),
        ],
        scratch_shapes=[
            pltpu.VMEM((keys, 2 * HD), F32),
            pltpu.VMEM((2 * HD, keys), BF16),
            pltpu.VMEM((2 * HD, wide), BF16),
            pltpu.VMEM((2 * HD, wide), BF16),
            pltpu.VMEM((wide, 2 * HD), BF16),
            pltpu.VMEM((wide, 2 * HD), BF16),
        ],
        cost_estimate=pl.CostEstimate(
            flops=rows * 2 * keys * heads * HD, bytes_accessed=2 << 20, transcendentals=0
        ),
        compiler_params=pltpu.CompilerParams(vmem_limit_bytes=60 << 20),
    )(bounds, core, d_mixed, kv, queries, mixed, lse, starts, slots, cosine, sine, *deps)


def keys_middle(keep, got, row, deps=()):
    _, rows, width = keep.shape

    def kernel(row_ref, keep_ref, got_ref, give_out, keep_out):
        row = row_ref[0]
        give_out[...] = (keep_ref[1 - row] + got_ref[1 - row].astype(F32)).astype(BF16)
        keep_out[...] = keep_ref[row] + got_ref[row].astype(F32)

    shapes = [jax.ShapeDtypeStruct((rows, width), t) for t in (BF16, F32)]
    deps = list(deps)
    return pl.pallas_call(
        after(kernel, 3, deps),
        grid=(1,),
        out_shape=shapes,
        in_specs=[pl.BlockSpec(memory_space=pltpu.SMEM)] + whole_specs([keep, got])
        + dep_specs(deps),
        out_specs=whole_specs(shapes),
        cost_estimate=pl.CostEstimate(flops=0, bytes_accessed=2 << 20, transcendentals=0),
    )(row, keep, got, *deps)


def keys_back(queries, keep, got, w_joint, cosine, sine, deps=()):
    deps = list(deps)

    rows, q_cols = queries.shape
    shapes = [jax.ShapeDtypeStruct((rows, n), BF16) for n in (q_cols + 2 * HD, D)]

    def kernel(q_ref, keep_ref, got_ref, w_ref, cos_ref, sin_ref, out_ref, term_ref):
        out_ref[:, :q_cols] = q_ref[...]
        total = jnp.transpose(keep_ref[...] + got_ref[...].astype(F32))
        turned = turn(total[:HD], cos_ref[...], -sin_ref[...])
        both = jnp.concatenate([turned, total[HD:]], axis=0)
        out_ref[:, q_cols:] = jnp.transpose(both).astype(BF16)
        for n in range(0, rows, 256):
            at = slice(n, n + 256)
            term_ref[at, :] = across(out_ref[at, :], w_ref[...]).astype(BF16)

    return pl.pallas_call(
        after(kernel, 6, deps),
        out_shape=shapes,
        grid=(1,),
        in_specs=whole_specs([queries, keep, got, w_joint, cosine, sine]) + dep_specs(deps),
        out_specs=whole_specs(shapes),
        cost_estimate=pl.CostEstimate(flops=0, bytes_accessed=2 << 20, transcendentals=0),
        compiler_params=pltpu.CompilerParams(vmem_limit_bytes=24 << 20),
    )(queries, keep, got, w_joint, cosine, sine, *deps)


def slot_tables(lengths, groups, group_id, first_slot, rows):
    seq_count = lengths.shape[0]
    seq_order = jnp.arange(seq_count, dtype=jnp.int32)
    same_group = groups[None, :] == groups[:, None]
    before = seq_order[None, :] < seq_order[:, None]
    begins = jnp.sum(jnp.where(same_group & before, lengths[None, :], 0), axis=1)
    ends = begins + lengths
    slots = first_slot + jnp.arange(rows, dtype=jnp.int32)
    inside = (
        (groups == group_id)[:, None]
        & (slots[None, :] >= begins[:, None])
        & (slots[None, :] < ends[:, None])
    )
    starts = jnp.where(
        jnp.any(inside, axis=0), jnp.sum(jnp.where(inside, begins[:, None], 0), axis=0), slots
    )
    return slots, starts


def block_bounds(slots, starts, size):
    first_row, last_row = slots[::QB], slots[QB - 1 :: QB]
    low, high = starts[::QB], starts[QB - 1 :: QB]
    first = low // size
    end = last_row // size + 1
    full_first = jnp.clip((high + size - 1) // size, first, end)
    full_end = jnp.clip((first_row + 1) // size, full_first, end)
    return jnp.stack([first, full_first, full_end, end], axis=1).reshape(-1).astype(jnp.int32)


def adamw_step(weight, first, second, grad, rate, decay):
    first_new = BETA_FIRST * first + (1.0 - BETA_FIRST) * grad
    second_new = BETA_SECOND * second + (1.0 - BETA_SECOND) * grad * grad
    first_hat = first_new / (1.0 - BETA_FIRST**STEP)
    second_hat = second_new / (1.0 - BETA_SECOND**STEP)
    weight_new = weight - rate * (first_hat / (jnp.sqrt(second_hat) + ADAM_EPS) + decay * weight)
    return (first_new, second_new, weight_new)


def after(kernel, inputs, deps):
    count = len(deps)
    if not count:
        return kernel
    return lambda *refs: kernel(*refs[:inputs], *refs[inputs + count :])


def any_specs(count):
    return [pl.BlockSpec(memory_space=pl.ANY)] * count


def dep_specs(deps):
    return [
        pl.BlockSpec((1,) * (d.ndim - 2) + (16, 128), lambda *at, n=d.ndim: (0,) * n) for d in deps
    ]


def whole_specs(arrays):
    return [pl.BlockSpec(v.shape, lambda *at, n=len(v.shape): (0,) * n) for v in arrays]


def tie(value, deps):
    deps = list(deps)
    return pl.pallas_call(
        lambda *refs: None,
        grid=(1,),
        out_shape=jax.ShapeDtypeStruct(value.shape, value.dtype),
        in_specs=any_specs(1) + dep_specs(deps),
        out_specs=pl.BlockSpec(memory_space=pl.ANY),
        input_output_aliases={0: 0},
    )(value, *deps)


def lay(pieces, plan, table, blocks, deps=(), weight=1, matrix=None):
    deps = list(deps)
    n, w = pieces[0].shape[-2:]
    extra = [] if matrix is None else [matrix]
    inputs = 1 + len(pieces) + len(extra)
    shapes = [jax.ShapeDtypeStruct((blocks, n, w), BF16), jax.ShapeDtypeStruct((16, 128), BF16)]
    shapes += [jax.ShapeDtypeStruct((blocks * n, m.shape[1]), BF16) for m in extra]

    def kernel(table_ref, *refs):
        out_ref, sign_ref = refs[inputs - 1 : inputs + 1]
        for piece, index, _, entry in plan:
            source = refs[piece]
            out_ref[table_ref[entry]] = source[...] if index is None else source[index]
        sign_ref[...] = jnp.zeros_like(sign_ref)
        if extra:
            rows = out_ref[...].reshape(blocks * n, w)
            refs[inputs + 1][...] = dot(rows, refs[inputs - 2][...]).astype(BF16)

    size = sum(p.size * p.dtype.itemsize for p in pieces)
    return pl.pallas_call(
        after(kernel, inputs, deps),
        out_shape=shapes,
        grid=(1,),
        in_specs=[pl.BlockSpec(memory_space=pltpu.SMEM)] + whole_specs(pieces + extra) + dep_specs(deps),
        out_specs=whole_specs(shapes),
        cost_estimate=pl.CostEstimate(flops=0, bytes_accessed=2 * weight * size, transcendentals=0),
        compiler_params=pltpu.CompilerParams(vmem_limit_bytes=3 * size + (8 << 20)),
    )(table, *pieces, *extra, *deps)


def tie_small(value, late):
    def kernel(value_ref, out_ref):
        out_ref[...] = value_ref[...]

    return in_vmem(kernel, [value], [jax.ShapeDtypeStruct(value.shape, F32)], [late])[0]


def in_vmem(kernel, inputs, out_shape, deps=(), weight=1):
    deps = list(deps)
    count = len(inputs)
    size = sum(v.size * v.dtype.itemsize for v in list(inputs) + list(out_shape))
    return pl.pallas_call(
        after(kernel, count, deps),
        out_shape=out_shape,
        grid=(1,),
        in_specs=whole_specs(inputs) + dep_specs(deps),
        out_specs=whole_specs(out_shape),
        cost_estimate=pl.CostEstimate(flops=0, bytes_accessed=weight * size, transcendentals=0),
        compiler_params=pltpu.CompilerParams(vmem_limit_bytes=2 * size + (6 << 20)),
    )(*inputs, *deps)


def join(parts, deps=()):
    arrays = []
    for array, _ in parts:
        if not any(array is known for known in arrays):
            arrays.append(array)
    spots = [next(n for n, known in enumerate(arrays) if known is array) for array, _ in parts]
    picked = [array.shape if index is None else array.shape[1:] for array, index in parts]

    def kernel(*refs):
        for n, (spot, (_, index)) in enumerate(zip(spots, parts)):
            refs[-1][n] = refs[spot][...] if index is None else refs[spot][index]

    shape = (len(parts),) + picked[0]
    return in_vmem(kernel, arrays, [jax.ShapeDtypeStruct(shape, BF16)], deps)[0]


def rms_inverse(value):
    return lax.rsqrt(jnp.mean(value * value, axis=-1, keepdims=True) + NORM_EPS)


def through_norm(d_normed, value, gain):
    inverse = rms_inverse(value)
    scaled = d_normed * gain
    pre = value * inverse
    return inverse * (scaled - pre * jnp.mean(scaled * pre, axis=-1, keepdims=True))


def load_weights(piece_refs, plan, table_ref, weights, held, sem, part, meanwhile=None):
    copies = []
    for n, (piece, index, entry) in enumerate(plan):
        source = piece_refs[piece] if index is None else piece_refs[piece].at[index]
        at = pl.ds(pl.multiple_of(table_ref[entry] * part, part), part)
        source = source.at[pl.ds(weights[0], len(weights))]
        copies.append(pltpu.make_async_copy(source, held.at[:, at, :], sem.at[n]))
    for copy in copies:
        copy.start()
    if meanwhile is not None:
        meanwhile()
    for copy in copies:
        copy.wait()


def upstream_hidden(upstream, pieces, plan, table, order):
    rows, units, part = upstream.shape[0], pieces[0].shape[-1], D // 16
    count, block = len(pieces), upstream.shape[0] // 2

    def kernel(order_ref, table_ref, u_ref, *refs):
        piece_refs, (dh_ref, ug_ref, uk_ref, w_ref, sem) = refs[:count], refs[count:]

        @pl.when(pl.program_id(0) == 0)
        def _():
            load_weights(piece_refs, plan, table_ref, (2,), w_ref, sem, part)

        for i in range(16):
            at = pl.ds(pl.multiple_of(order_ref[i] * part, part), part)
            to = slice((i % 8) * part, (i % 8 + 1) * part)
            (ug_ref if i < 8 else uk_ref)[:, to] = u_ref[:, at]
        for f in range(0, units, 256):
            at = slice(f, f + 256)
            dh_ref[:, at] = dot(u_ref[...], w_ref[0, :, at])

    by_row = lambda w: pl.BlockSpec((block, w), lambda i: (i, 0))
    shape = lambda w, t: jax.ShapeDtypeStruct((rows, w), t)
    return pl.pallas_call(
        kernel,
        grid=(2,),
        in_specs=[pl.BlockSpec(memory_space=pltpu.SMEM)] * 2 + [by_row(D)] + any_specs(count),
        out_specs=[by_row(units), by_row(D // 2), by_row(D // 2)],
        out_shape=[shape(units, F32), shape(D // 2, BF16), shape(D // 2, BF16)],
        scratch_shapes=[pltpu.VMEM((1, D, units), BF16), pltpu.SemaphoreType.DMA((len(plan),))],
        cost_estimate=pl.CostEstimate(
            flops=2 * rows * D * units, bytes_accessed=12 << 20, transcendentals=0
        ),
        compiler_params=pltpu.CompilerParams(vmem_limit_bytes=22 << 20),
    )(order, table, upstream, *pieces)


def feed_forward(row_pieces, row_plan, row_table, d_hidden, pieces, plan, table, order):
    rows, units, block = d_hidden.shape[0], pieces[0].shape[-1], d_hidden.shape[0] // 2
    count, part, own = len(pieces), D // 16, rows // 16
    row_count = len(row_pieces)

    def kernel(order_ref, table_ref, row_ref, dh_ref, *refs):
        piece_refs, refs = refs[:count], refs[count:]
        row_refs, refs = refs[:row_count], refs[row_count:]
        hid_ref, dg_ref, du_ref, dn_ref, ff_ref, ng_ref, nk_ref, w_ref, all_ref, sem = refs

        @pl.when(pl.program_id(0) == 0)
        def _():
            def lay_rows():
                for piece, index, _, entry in row_plan:
                    at = pl.ds(pl.multiple_of(row_ref[entry] * own, own), own)
                    all_ref[at, :] = row_refs[piece][index]

            load_weights(piece_refs, plan, table_ref, (0, 1, 2), w_ref, sem, part, lay_rows)

        n_ref = all_ref.at[pl.ds(pl.multiple_of(pl.program_id(0) * block, block), block), :]

        for i in range(16):
            at = pl.ds(pl.multiple_of(order_ref[i] * part, part), part)
            to = slice((i % 8) * part, (i % 8 + 1) * part)
            (ng_ref if i < 8 else nk_ref)[:, to] = n_ref[:, at]
        for f in range(0, units, 256):
            at = slice(f, f + 256)
            gate = dot(n_ref[...], w_ref[0, :, at])
            up = dot(n_ref[...], w_ref[1, :, at])
            d_hidden = dh_ref[:, at]
            sigmoid = jax.nn.sigmoid(gate)
            activated = gate * sigmoid
            hid_ref[:, at] = (activated * up).astype(BF16)
            dg_ref[:, at] = (
                d_hidden * up * sigmoid * (1.0 + gate * (1.0 - sigmoid))
            ).astype(BF16)
            du_ref[:, at] = (d_hidden * activated).astype(BF16)
        for d in range(0, D, 512):
            at = slice(d, d + 512)
            dn_ref[:, at] = (
                across(dg_ref[...], w_ref[0, at, :]) + across(du_ref[...], w_ref[1, at, :])
            ).astype(BF16)
            ff_ref[:, at] = across(hid_ref[...], w_ref[2, at, :]).astype(BF16)

    by_row = lambda w: pl.BlockSpec((block, w), lambda i: (i, 0))
    shape = lambda w: jax.ShapeDtypeStruct((rows, w), BF16)
    return pl.pallas_call(
        kernel,
        grid=(2,),
        in_specs=[pl.BlockSpec(memory_space=pltpu.SMEM)] * 3
        + [by_row(units)]
        + any_specs(count)
        + whole_specs(row_pieces),
        out_specs=[by_row(units)] * 3 + [by_row(D)] * 2 + [by_row(D // 2)] * 2,
        out_shape=[shape(units)] * 3 + [shape(D)] * 2 + [shape(D // 2)] * 2,
        scratch_shapes=[
            pltpu.VMEM((3, D, units), BF16),
            pltpu.VMEM((rows, D), BF16),
            pltpu.SemaphoreType.DMA((len(plan),)),
        ],
        cost_estimate=pl.CostEstimate(
            flops=10 * rows * D * units, bytes_accessed=24 << 20, transcendentals=0
        ),
        compiler_params=pltpu.CompilerParams(vmem_limit_bytes=58 << 20),
    )(order, table, row_table, d_hidden, *pieces, *row_pieces)


def outer_blocks(table, groups, deps=()):
    lefts, rights, plan = [], [], []
    for pairs in groups:
        entry = []
        for left, right in pairs:
            spot = next((n for n, known in enumerate(lefts) if known is left), None)
            if spot is None:
                spot = len(lefts)
                lefts.append(left)
            entry.append((spot, len(rights)))
            rights.append(right)
        plan.append(entry)
    width = sum(pairs[0][1].shape[1] for pairs in groups)
    block = D // 16

    def kernel(table_ref, *refs):
        left_refs, refs = refs[: len(lefts)], refs[len(lefts) :]
        right_refs, (give_ref, keep_ref) = refs[: len(rights)], refs[len(rights) :]
        step = pl.program_id(0)
        turned = [jnp.transpose(r[...]) for r in left_refs]
        parts = []
        for entry in plan:
            part = None
            for spot, n in entry:
                term = dot(turned[spot], right_refs[n][...])
                part = term if part is None else part + term
            parts.append(part.astype(BF16))
        whole = parts[0] if len(parts) == 1 else jnp.concatenate(parts, axis=1)

        @pl.when(step < 8)
        def _():
            give_ref[...] = whole

        @pl.when(step >= 8)
        def _():
            keep_ref[...] = whole

    flops = sum(2 * left.shape[0] * D * right.shape[1] for g in groups for left, right in g)
    return pl.pallas_call(
        after(kernel, 1 + len(lefts) + len(rights), deps),
        grid_spec=pltpu.PrefetchScalarGridSpec(
            num_scalar_prefetch=1,
            grid=(16,),
            in_specs=[pl.BlockSpec((v.shape[0], block), lambda i, t: (0, t[i])) for v in lefts]
            + [pl.BlockSpec(v.shape, lambda i, t: (0, 0)) for v in rights]
            + dep_specs(deps),
            out_specs=[
                pl.BlockSpec((block, width), lambda i, t: (jnp.minimum(i, 7), 0)),
                pl.BlockSpec((block, width), lambda i, t: (jnp.maximum(i - 8, 0), 0)),
            ],
        ),
        out_shape=[jax.ShapeDtypeStruct((8 * block, width), BF16)] * 2,
        cost_estimate=pl.CostEstimate(flops=flops, bytes_accessed=4 << 20, transcendentals=0),
        compiler_params=pltpu.CompilerParams(vmem_limit_bytes=12 << 20),
    )(table, *lefts, *rights, *deps)


def fold_core(keeps, gots, deps=()):
    count, pair = len(keeps), D // 8
    widths = [k.shape[1] for k in keeps]
    starts = [sum(widths[:n]) for n in range(count)]
    deps = list(deps)

    def kernel(*refs):
        keep_refs, got_refs, outs = refs[:count], refs[count : 2 * count], refs[2 * count :]
        for k in range(4):

            @pl.when(pl.program_id(0) == k)
            def _():
                for n in range(count):
                    total = keep_refs[n][...].astype(F32) + got_refs[n][...].astype(F32)
                    to = slice(starts[n], starts[n] + widths[n])
                    outs[k][:, to] = total.astype(outs[k].dtype)

    whole = pl.BlockSpec((pair, sum(widths)), lambda i: (0, 0))
    shape = lambda dtype: jax.ShapeDtypeStruct((pair, sum(widths)), dtype)
    return pl.pallas_call(
        after(kernel, 2 * count, deps),
        grid=(4,),
        in_specs=[pl.BlockSpec((pair, w), lambda i: (i, 0)) for w in widths * 2]
        + dep_specs(deps),
        out_specs=[whole] * 4,
        out_shape=[shape(F32)] + [shape(BF16)] * 3,
        cost_estimate=pl.CostEstimate(
            flops=0, bytes_accessed=12 * pair * sum(widths), transcendentals=0
        ),
        compiler_params=pltpu.CompilerParams(vmem_limit_bytes=(28 << 20) if count > 1 else (8 << 20)),
    )(*keeps, *gots, *deps)


def adamw_kernel(weight, first, second, sums, spot, rate, flip, deps=()):
    def kernel(w_ref, m_ref, v_ref, keep_ref, got_ref, m_out, v_out, w_out, sum_ref):
        grad = keep_ref[...] + got_ref[...].astype(F32)
        if flip:
            grad = jnp.transpose(grad)
        weight = w_ref[...]
        first_new, second_new, weight_new = adamw_step(
            weight, m_ref[...], v_ref[...], grad, rate, DECAY_RATE
        )
        m_out[...] = first_new
        v_out[...] = second_new
        w_out[...] = weight_new
        if flip:
            sum_ref[...] = jnp.zeros_like(sum_ref)
        else:
            sum_ref[...] = jnp.sum(weight.astype(BF16).astype(F32) * grad, axis=1, keepdims=True)

    shape = jax.ShapeDtypeStruct(weight.shape, F32)
    columns = weight.shape[0] if flip else weight.shape[1]
    whole = lambda *shape: pl.BlockSpec(shape, lambda i: (0,) * len(shape))
    view = pl.BlockSpec((D // 16, columns), lambda i: (0, spot // columns))
    return pl.pallas_call(
        after(kernel, 5, deps),
        grid=(1,),
        in_specs=[whole(*weight.shape)] * 3 + [view] * 2 + dep_specs(deps),
        out_specs=[whole(*weight.shape)] * 3 + [whole(D // 16, 1)],
        out_shape=[shape] * 3 + [jax.ShapeDtypeStruct((D // 16, 1), F32)],
        cost_estimate=pl.CostEstimate(
            flops=0, bytes_accessed=28 * weight.size, transcendentals=0
        ),
        compiler_params=pltpu.CompilerParams(vmem_limit_bytes=14 << 20),
    )(weight, first, second, *sums, *deps)


def pick(blocks, axis, index):
    return lax.dynamic_index_in_dim(blocks, index, axis, keepdims=False)


class Here:
    def __init__(self):
        self.x, self.yh, self.c, self.yl, self.z = (
            lax.axis_index(a) for a in ("x", "yh", "c", "yl", "z")
        )

    def ztable(self):
        own = [self.yl * 4 + (self.z + k) % 4 for k in range(4)]
        other = [(1 - self.yl) * 4 + (self.z + k) % 4 for k in range(4)]
        return jnp.stack(own + other).astype(jnp.int32)

    def xtable(self):
        table = []
        for dc in range(2):
            core = self.c if dc == 0 else 1 - self.c
            for k in range(4):
                for dy in range(2):
                    yh = self.yh if dy == 0 else 1 - self.yh
                    table.append(((self.x + k) % 4) * 4 + yh * 2 + core)
        return jnp.stack(table).astype(jnp.int32)

    def scatter_tp(self, terms, extras, finish, out_shape, deps=(), weight=1):
        parts = lax.all_to_all(terms, ("yl", "z"), 0, 0, tiled=True)
        return self.sum_tp_parts(parts, extras, finish, out_shape, deps, weight)

    def sum_tp_parts(self, parts, extras, finish, out_shape, deps=(), weight=1):
        parts = parts.reshape(8, -1, parts.shape[1])
        extras, deps = list(extras), list(deps)
        count = len(extras)

        def kernel(part_ref, *refs):
            far, refs = refs[:count], refs[count:]
            outs, refs = refs[: len(out_shape)], refs[len(out_shape) :]
            held, sem = refs[:count], refs[count]
            copies = [pltpu.make_async_copy(far[n], held[n], sem.at[n]) for n in range(count)]
            for copy in copies:
                copy.start()
            total = part_ref[0].astype(F32)
            for n in range(1, 8):
                total = total + part_ref[n].astype(F32)
            for copy in copies:
                copy.wait()
            finish(total, held, outs)

        arrays = [parts] + extras + list(out_shape)
        size = sum(v.size * v.dtype.itemsize for v in arrays)
        return pl.pallas_call(
            after(kernel, 1 + count, deps),
            grid=(1,),
            out_shape=out_shape,
            in_specs=whole_specs([parts]) + any_specs(count) + dep_specs(deps),
            out_specs=whole_specs(out_shape),
            scratch_shapes=[pltpu.VMEM(v.shape, v.dtype) for v in extras]
            + [pltpu.SemaphoreType.DMA((count,))],
            cost_estimate=pl.CostEstimate(
                flops=0, bytes_accessed=weight * size, transcendentals=0
            ),
            compiler_params=pltpu.CompilerParams(vmem_limit_bytes=2 * size + (6 << 20)),
        )(parts, *extras, *deps)

    def gather_first(self, both, second):
        over = lax.ppermute(both, "yl", SWAP)
        return [both, over] + [lax.ppermute(second, "z", ring(-k)) for k in (1, 2, 3)]

    def gather_join(self, first, deps=()):
        both, over, *rest = first
        rest = join([(part, None) for part in rest], deps)
        return both, over, join([(both, 0), (over, 0)]), rest

    def gather_second(self, joined):
        both, over, pair, rest = joined
        pieces = [pair] + [lax.ppermute(pair, "z", ring(-k)) for k in (1, 2, 3)]
        return pieces + [both, over, rest, lax.ppermute(rest, "yl", SWAP)]

    def gather_plan(self):
        spots = [(k, (d,), 4 * d + k) for k in range(4) for d in range(2)]
        spots += [(4, (1,), 8), (5, (1,), 12)]
        spots += [(6, (k,), k + 9) for k in range(3)] + [(7, (k,), k + 13) for k in range(3)]
        plan = [(piece, index, 0, entry) for piece, index, entry in spots]
        table = self.ztable()
        return plan, jnp.concatenate([2 * table, 2 * table + 1])

    def gather_last(self, pieces, deps=(), weight=1, matrix=None):
        plan, table = self.gather_plan()
        laid, *rest = lay(pieces, plan, table, 16, deps, weight, matrix)
        return laid.reshape(-1, laid.shape[-1]), rest[-1]

    def gather_product(self, both, second, matrix, deps=(), weight=1):
        joined = self.gather_join(self.gather_first(both, second))
        return self.gather_last(self.gather_second(joined), deps, weight, matrix)

    def gather_weights(self, shard):
        pair = jnp.stack([shard, lax.ppermute(shard, "yh", SWAP)])
        mine = [pair] + [lax.ppermute(pair, "x", ring(-k)) for k in (1, 2, 3)]
        return mine + [lax.ppermute(p, "c", SWAP) for p in mine]

    def gather_large(self, shard, over, deps):
        pair = join([(shard, None), (over, None)], deps)
        near = [lax.ppermute(pair, "x", ring(-1)), lax.ppermute(pair, "x", ring(1))]
        far = [
            lax.ppermute(near[0][0], "x", ring(-1)),
            lax.ppermute(near[1][1], "x", ring(1)),
        ]
        mine = [pair] + near + far
        plan = [(0, 0, 0), (0, 1, 1), (1, 0, 2), (1, 1, 3), (2, 0, 6), (2, 1, 7)]
        plan += [(3, None, 4), (4, None, 5)]
        plan += [(p + 5, i, e + 8) for p, i, e in plan]
        theirs = [lax.ppermute(p, "c", SWAP) for p in mine]
        return mine + theirs, plan, near

    def scatter_weights(self, total, sends, late=False):
        near = [lax.ppermute(sends[n], "x", ring(n + 1)) for n in (0, 2)]
        far = lax.ppermute(tie(sends[1], near) if late else sends[1], "x", ring(2))
        for part in near + [far]:
            total = total + part.astype(F32)
        n = D // 16
        give = total[n:].astype(BF16)
        return [total[:n], lax.ppermute(give, "yh", SWAP)], near, give

    def gather_ctx(self, own):
        over = lax.ppermute(own, "yh", SWAP)
        beside = lax.ppermute(own, "c", SWAP)
        pieces = [own, over, beside, lax.ppermute(over, "c", SWAP)]
        table = jnp.stack(
            [
                self.yh * 2 + self.c,
                (1 - self.yh) * 2 + self.c,
                self.yh * 2 + 1 - self.c,
                (1 - self.yh) * 2 + 1 - self.c,
            ]
        ).astype(jnp.int32)
        plan = [(i, None, 0, i) for i in range(4)]
        return lay(pieces, plan, table, 4)[0].reshape(-1, own.shape[1]), beside

    def scatter_ctx(self, give, keep, deps):
        got = lax.ppermute(give, "c", SWAP)
        give, keep = keys_middle(keep, got, self.yh.reshape(1).astype(jnp.int32), deps)
        return keep, lax.ppermute(give, "yh", SWAP)

    def sum_tp(self, value):
        value = value + lax.ppermute(value, "yl", SWAP)
        got = [lax.ppermute(value, "z", ring(k)) for k in (1, 2, 3)]
        parts = jnp.stack([value] + got)
        order = jnp.stack([(self.z - j) % 4 for j in range(4)])
        return jnp.sum(jnp.take(parts, order, axis=0), axis=0)


def per_device(
    tokens,
    cotangent,
    lengths,
    groups,
    query_weight,
    query_m,
    query_v,
    kv_weight,
    kv_m,
    kv_v,
    out_weight,
    out_m,
    out_v,
    gate_weight,
    gate_m,
    gate_v,
    up_weight,
    up_m,
    up_v,
    down_weight,
    down_m,
    down_v,
    norm_gains,
    gains_m,
    gains_v,
):
    here = Here()
    row_count = tokens.shape[0]
    group_rows = row_count * 4
    group_id = here.x
    ctx_id = here.yh * 2 + here.c
    tp_id = here.yl * 4 + here.z
    half = row_count // 2
    part = half // 8
    xtable = here.xtable()

    kv_flat = kv_weight.reshape(D // 16, 2 * HD)
    attn_shard = jnp.concatenate([query_weight, kv_flat, out_weight.T], axis=1).astype(BF16)
    q_cols, kv_cols, o_cols = query_weight.shape[1], 2 * HD, out_weight.shape[0]
    cols = q_cols + kv_cols + o_cols
    gains_low = norm_gains.astype(BF16)
    gain_rows = jnp.zeros((16, cols), BF16).at[:2, : D // 16].set(gains_low)
    attn_pieces = here.gather_weights(jnp.concatenate([attn_shard, gain_rows], axis=0))

    units = gate_weight.shape[1]
    ff_shard = jnp.stack([gate_weight, up_weight, down_weight.T]).astype(BF16)
    ff_over = lax.ppermute(ff_shard, "yh", SWAP)

    slots, starts = slot_tables(lengths, groups, group_id, ctx_id * row_count, row_count)
    frequency = ROPE_BASE ** (-2.0 * jnp.arange(HD // 2, dtype=F32) / HD)
    angles = frequency[:, None] * (slots - starts).astype(F32)[None, :]
    cosine, sine = jnp.cos(angles), jnp.sin(angles)
    bounds_forward = block_bounds(slots, starts, KB_FORWARD)
    bounds = block_bounds(slots, starts, KB)
    slot_rows, start_rows = slots.reshape(-1, 1, QB), starts.reshape(-1, 1, QB)

    normed_one, query_raw, kv_local, w_joint, w_out, gain_values = normed_projections(
        tokens,
        attn_pieces,
        xtable,
        (q_cols, kv_cols, o_cols),
        cosine,
        sine,
        NORM_EPS,
        deps=[ff_over],
    )
    kv_whole, kv_beside = here.gather_ctx(kv_local)
    ff_pieces, ff_plan, weights_near = here.gather_large(ff_shard, ff_over, [kv_beside])

    mixed, turned, raw, log_total = attention_forward(
        query_raw, kv_whole, bounds_forward, start_rows, slot_rows, cosine, sine, 0, row_count
    )
    mixed = tie(mixed, weights_near)
    own = lambda v: lax.dynamic_slice_in_dim(v, tp_id * 2 * part, 2 * part, axis=0)
    own_inputs, own_upstream = own(tokens), own(cotangent)
    own_wide = jax.ShapeDtypeStruct((2 * part, D), F32)
    own_low = [jax.ShapeDtypeStruct((2, part, D), BF16), jax.ShapeDtypeStruct((part, D), BF16)]

    def both(outs, value):
        outs[0][0] = value[:part]
        outs[0][1] = value[part:]
        outs[1][...] = value[part:]

    def close_attention(total, ins, outs):
        value = ins[0][...].astype(F32) + total
        outs[0][...] = value
        both(outs[1:], (value * rms_inverse(value) * ins[1][1:2, :]).astype(BF16))

    term = jnp.einsum("ra,da->rd", mixed, w_out, preferred_element_type=F32).astype(BF16)
    hidden_one, *own_normed = here.scatter_tp(
        term, [own_inputs, gain_values], close_attention, [own_wide] + own_low, deps=ff_pieces[5:]
    )
    order = here.xtable()
    order = jnp.concatenate([order[8:], order[:8]])
    d_hidden, upstream_give, upstream_keep = upstream_hidden(
        cotangent, ff_pieces, ff_plan, xtable, order
    )
    joined = here.gather_join(here.gather_first(*own_normed), [d_hidden])
    row_pieces = here.gather_second(joined)
    hidden, d_gate, d_up, d_two, out_term, normed_give, normed_keep = feed_forward(
        row_pieces, *here.gather_plan(), d_hidden, ff_pieces, ff_plan, xtable, order
    )
    outer = lambda a, b: jnp.einsum("rd,rf->df", a, b, preferred_element_type=F32).astype(BF16)
    gives = [outer(normed_give, d_gate), outer(normed_give, d_up), outer(upstream_give, hidden)]
    keeps = [outer(normed_keep, d_gate), outer(normed_keep, d_up), outer(upstream_keep, hidden)]
    gots = [lax.ppermute(give, "c", SWAP) for give in gives]

    ff_total, *ff_sends = fold_core(keeps, gots)

    def close_feed_forward(total, ins, outs):
        value = ins[1][...].astype(F32) + through_norm(total, ins[0][...], ins[2][1:2, :])
        outs[0][...] = value
        both(outs[1:], value.astype(BF16))

    d_hidden_one, *own_branch = here.scatter_tp(
        d_two,
        [hidden_one, own_upstream, gain_values],
        close_feed_forward,
        [own_wide] + own_low,
        weight=20,
    )
    d_branch, d_mixed = here.gather_product(*own_branch, w_out, deps=[ff_total], weight=20)


    ff_sums, ff_near, ff_give = here.scatter_weights(ff_total, ff_sends, True)

    def close_output(total, ins, outs):
        both(outs, (ins[0][...] + total).astype(BF16))

    own_output = here.scatter_tp(
        tie(out_term, [d_branch]), [hidden_one], close_output, own_low
    )
    out_joined = here.gather_join(here.gather_first(*own_output))

    d_query_low, *d_kv = attention_backward(
        d_mixed,
        kv_whole,
        turned,
        raw,
        log_total,
        bounds,
        start_rows,
        slot_rows,
        cosine,
        sine,
        here.c.reshape(1).astype(jnp.int32),
    )
    d_joint, term = keys_back(
        d_query_low, *here.scatter_ctx(*d_kv, ff_near), w_joint, cosine, sine, deps=out_joined[2:]
    )
    out_second = here.gather_second(out_joined)
    output, out_sign = here.gather_last(out_second)

    term = tie(term, [])

    give, keep = outer_blocks(
        order,
        [((d_branch, mixed),), ((normed_one, d_joint),)],
        deps=[term],
    )
    attn_got = lax.ppermute(give, "c", SWAP)
    attn_total, *attn_sends = fold_core([keep], [attn_got])
    attn_sums, _, attn_give = here.scatter_weights(attn_total, attn_sends)

    def close_inputs(total, ins, outs):
        value = ins[0][...] + through_norm(total, ins[1][...].astype(F32), ins[2][:1, :])
        both(outs, value.astype(BF16))

    own_results = here.scatter_tp(
        term,
        [d_hidden_one, own_inputs, gain_values],
        close_inputs,
        own_low,
        deps=[ff_give, out_sign],
        weight=50,
    )
    last_pieces = here.gather_second(here.gather_join(here.gather_first(*own_results)))
    tokens_grad, _ = here.gather_last(last_pieces, deps=attn_sums[1:], weight=50)

    late = own_results[1:2]
    flat = lambda v: v.reshape(kv_flat.shape)
    fan = D ** (-0.5)
    out_fan = max(1, 4 * D // group_rows) ** (-0.5)
    query_new = adamw_kernel(query_weight, query_m, query_v, attn_sums, o_cols, fan, False, late)
    out_new = adamw_kernel(out_weight, out_m, out_v, attn_sums, 0, out_fan, True)
    kv_new = adamw_kernel(
        kv_flat, flat(kv_m), flat(kv_v), attn_sums, q_cols + o_cols, fan, False
    )
    gate_new = adamw_kernel(gate_weight, gate_m, gate_v, ff_sums, 0, fan, False, late)
    up_new = adamw_kernel(up_weight, up_m, up_v, ff_sums, units, fan, False, late)
    down_new = adamw_kernel(down_weight, down_m, down_v, ff_sums, 2 * units, FF ** (-0.5), True, late)

    gain_sums = jnp.stack([query_new[3] + kv_new[3], gate_new[3] + up_new[3]])[:, :, 0]
    grad_gains = here.sum_tp(tie_small(gain_sums, last_pieces[1])) / gains_low.astype(F32)
    gains_new = adamw_step(norm_gains, gains_m, gains_v, grad_gains, 0.5, 0.0)
    return (
        output,
        tokens_grad,
        *query_new[:3],
        *[v.reshape(kv_weight.shape) for v in kv_new[:3]],
        *out_new[:3],
        *gate_new[:3],
        *up_new[:3],
        *down_new[:3],
        *gains_new,
    )


def solution(mesh):
    fine = Mesh(mesh.devices.reshape(4, 2, 2, 2, 4), ("x", "yh", "c", "yl", "z"))
    rows = ("x", "yh", "c")
    tp = ("yl", "z")
    by_row, by_col, by_unit = P(rows, None), P(rows, tp), P(tp, rows)
    by_kv, by_gain = P(rows, tp, None), P(None, rows)
    in_specs = (
        (by_row,) * 2
        + (P(),) * 2
        + (by_col,) * 3
        + (by_kv,) * 3
        + (by_unit,) * 3
        + (by_col,) * 6
        + (by_unit,) * 3
        + (by_gain,) * 3
    )
    out_specs = (
        (by_row,) * 2
        + (by_col,) * 3
        + (by_kv,) * 3
        + (by_unit,) * 3
        + (by_col,) * 6
        + (by_unit,) * 3
        + (by_gain,) * 3
    )
    return jax.shard_map(
        per_device, mesh=fine, in_specs=in_specs, out_specs=out_specs, check_vma=False
    )
```

```python
import functools

import jax
import jax.numpy as jnp
from jax import lax
from jax.experimental import pallas as pl
from jax.experimental.pallas import tpu as pltpu
from jax.sharding import Mesh
from jax.sharding import PartitionSpec as P

D = 2048
HD = 64
FF = 8192
STEP = 5


NORM_EPS = 1e-05
BETA_FIRST = 0.9
BETA_SECOND = 0.95
ADAM_EPS = 1e-08
DECAY_RATE = 0.1
ROPE_BASE = 500000.0
MASKED_SCORE = -1e30

F32 = jnp.float32
BF16 = jnp.bfloat16
QB = 128
KB = 512
KB_FORWARD = 1024


SWAP = ((0, 1), (1, 0))


def ring(step):
    return tuple((i, (i + step) % 4) for i in range(4))


def dot(a, b):
    return jnp.dot(a, b, preferred_element_type=F32)


def across(a, b):
    return lax.dot_general(a, b, (((1,), (1,)), ((), ())), preferred_element_type=F32)


def turn(value, cosine, sine):
    a, b = value[: HD // 2], value[HD // 2 :]
    return jnp.concatenate([a * cosine - b * sine, b * cosine + a * sine], axis=0)


def heads_to_lanes(wide, heads):
    return jnp.concatenate([wide[h * HD : (h + 1) * HD] for h in range(heads)], axis=1)


def lanes_to_heads(tall, heads):
    n = tall.shape[1] // heads
    return jnp.concatenate([tall[:, h * n : (h + 1) * n] for h in range(heads)], axis=0)


def normed_projections(tokens, pieces, table, widths, cosine, sine, eps, deps=()):
    rows, width = tokens.shape
    block, part = 256, D // 16
    q_cols, kv_cols, o_cols = widths
    deps = list(deps)
    count = len(pieces)

    def kernel(table_ref, t_ref, *refs):
        piece_refs, refs = refs[:count], refs[count:]
        cos_ref, sin_ref, n_ref, q_ref, kv_ref, w_ref, wo_ref, g_ref = refs

        @pl.when(pl.program_id(0) == 0)
        def _():
            for i in range(count):
                for d in range(2):
                    spot = table_ref[2 * i + d]
                    at = pl.ds(pl.multiple_of(spot * part, part), part)
                    body = piece_refs[i][d, :part, :]
                    w_ref[at, :] = body[:, : q_cols + kv_cols]
                    wo_ref[at, :] = body[:, q_cols + kv_cols :]
                    g_ref[:, at] = piece_refs[i][d, part:, :part].astype(F32)[:8]

        x = t_ref[...].astype(F32)
        inv = lax.rsqrt(jnp.mean(x * x, axis=-1, keepdims=True) + eps)
        normed = (x * inv * g_ref[:1, :]).astype(BF16)
        n_ref[...] = normed
        joint = dot(normed, w_ref[...])
        q_ref[...] = joint[:, :q_cols]
        kv = jnp.transpose(joint[:, q_cols:])
        kv = jnp.concatenate([turn(kv[:HD], cos_ref[...], sin_ref[...]), kv[HD:]], axis=0)
        kv_ref[...] = jnp.transpose(kv).astype(BF16)

    whole = lambda *shape: pl.BlockSpec(shape, lambda i: (0,) * len(shape))
    by_row = lambda w: pl.BlockSpec((block, w), lambda i: (i, 0))
    by_lane = pl.BlockSpec((HD // 2, block), lambda i: (0, i))
    return pl.pallas_call(
        after(kernel, 4 + count, deps),
        grid=(rows // block,),
        in_specs=[pl.BlockSpec(memory_space=pltpu.SMEM), by_row(width)]
        + [whole(*p.shape) for p in pieces]
        + [by_lane, by_lane]
        + dep_specs(deps),
        out_specs=[
            by_row(width),
            by_row(q_cols),
            by_row(kv_cols),
            whole(D, q_cols + kv_cols),
            whole(D, o_cols),
            whole(8, D),
        ],
        out_shape=[
            jax.ShapeDtypeStruct((rows, width), BF16),
            jax.ShapeDtypeStruct((rows, q_cols), F32),
            jax.ShapeDtypeStruct((rows, kv_cols), BF16),
            jax.ShapeDtypeStruct((D, q_cols + kv_cols), BF16),
            jax.ShapeDtypeStruct((D, o_cols), BF16),
            jax.ShapeDtypeStruct((8, D), F32),
        ],
        cost_estimate=pl.CostEstimate(
            flops=2 * rows * width * 384, bytes_accessed=12 << 20, transcendentals=0
        ),
        compiler_params=pltpu.CompilerParams(vmem_limit_bytes=24 << 20),
    )(table, tokens, *pieces, cosine, sine, *deps)


def key_ranges(bounds_ref, step):
    return [bounds_ref[step * 4 + n] for n in range(4)]


def attention_forward(query_raw, kv, bounds, starts, slots, cosine, sine, row_offset, rows):
    heads = query_raw.shape[1] // HD
    keys = kv.shape[0]
    wide = heads * QB
    steps, base = rows // QB, row_offset // QB

    def kernel(b_ref, q_ref, kv_ref, start_ref, slot_ref, cos_ref, sin_ref, m_ref, qt_ref, ot_ref, lse_ref, kvt_ref, qp_ref):
        step = pl.program_id(0)

        @pl.when(step == 0)
        def _():
            kvt_ref[...] = jnp.transpose(kv_ref[...].astype(F32)).astype(BF16)

        raw = jnp.transpose(q_ref[...])
        turned = jnp.concatenate(
            [turn(raw[h * HD : (h + 1) * HD], cos_ref[...], sin_ref[...]) for h in range(heads)],
            axis=1,
        ).astype(BF16)
        qt_ref[0] = turned
        scaled = (turned.astype(F32) * HD**-0.5).astype(BF16)
        qp_ref[...] = jnp.concatenate([scaled, jnp.zeros_like(scaled)], axis=0)
        start = jnp.concatenate([start_ref[0]] * heads, axis=1)
        slot = jnp.concatenate([slot_ref[0]] * heads, axis=1)

        def body(masked, j, carry):
            peak, total, acc = carry
            at = pl.multiple_of(j * KB_FORWARD, KB_FORWARD)
            scores = dot(kv_ref[pl.ds(at, KB_FORWARD), :], qp_ref[...])
            if masked:
                key = at + lax.broadcasted_iota(jnp.int32, (KB_FORWARD, wide), 0)
                scores = jnp.where((key >= start) & (key <= slot), scores, MASKED_SCORE)
            new_peak = jnp.maximum(peak, jnp.max(scores, axis=0, keepdims=True))
            powers = jnp.exp(scores - new_peak)
            shrink = jnp.exp(peak - new_peak)
            total = total * shrink + jnp.sum(powers, axis=0, keepdims=True)
            values = kvt_ref[HD:, pl.ds(at, KB_FORWARD)]
            acc = acc * shrink + dot(values, powers.astype(BF16))
            return (new_peak, total, acc)

        first, full_first, full_end, end = key_ranges(b_ref, base + step)
        carry = (
            jnp.full((1, wide), MASKED_SCORE, F32),
            jnp.zeros((1, wide), F32),
            jnp.zeros((HD, wide), F32),
        )
        carry = lax.fori_loop(first, full_first, functools.partial(body, True), carry)
        carry = lax.fori_loop(full_first, full_end, functools.partial(body, False), carry)
        carry = lax.fori_loop(full_end, end, functools.partial(body, True), carry)
        peak, total, acc = carry
        mixed = acc / total
        ot_ref[0] = mixed
        lse_ref[0] = peak + jnp.log(total)
        m_ref[...] = jnp.transpose(lanes_to_heads(mixed, heads)).astype(BF16)

    lane = lambda: pl.BlockSpec((HD // 2, QB), lambda i: (0, base + i))
    row = lambda: pl.BlockSpec((1, 1, QB), lambda i: (base + i, 0, 0))
    return pl.pallas_call(
        kernel,
        grid=(steps,),
        in_specs=[
            pl.BlockSpec(memory_space=pltpu.SMEM),
            pl.BlockSpec((QB, heads * HD), lambda i: (base + i, 0)),
            pl.BlockSpec((keys, 2 * HD), lambda i: (0, 0)),
            row(),
            row(),
            lane(),
            lane(),
        ],
        out_specs=[
            pl.BlockSpec((QB, heads * HD), lambda i: (i, 0)),
            pl.BlockSpec((1, HD, wide), lambda i: (i, 0, 0)),
            pl.BlockSpec((1, HD, wide), lambda i: (i, 0, 0)),
            pl.BlockSpec((1, 1, wide), lambda i: (i, 0, 0)),
        ],
        out_shape=[
            jax.ShapeDtypeStruct((rows, heads * HD), BF16),
            jax.ShapeDtypeStruct((steps, HD, wide), BF16),
            jax.ShapeDtypeStruct((steps, HD, wide), F32),
            jax.ShapeDtypeStruct((steps, 1, wide), F32),
        ],
        scratch_shapes=[pltpu.VMEM((2 * HD, keys), BF16), pltpu.VMEM((2 * HD, wide), BF16)],
        cost_estimate=pl.CostEstimate(
            flops=rows * keys * heads * HD // 8, bytes_accessed=2 << 20, transcendentals=0
        ),
        compiler_params=pltpu.CompilerParams(vmem_limit_bytes=14 << 20),
    )(bounds, query_raw, kv, starts, slots, cosine, sine)


def attention_backward(
    d_mixed, kv, queries, mixed, lse, bounds, starts, slots, cosine, sine, core, deps=()
):
    rows, width = d_mixed.shape
    heads = width // HD
    keys = kv.shape[0]
    wide = heads * QB
    steps = rows // QB
    deps = list(deps)

    def kernel(b_ref, core_ref, d_ref, kv_ref, qt_ref, ot_ref, lse_ref, start_ref, slot_ref, cos_ref, sin_ref, dq_ref, give_ref, keep_ref, dkv_ref, kvt_ref, qp_ref, dp_ref, qr_ref, dr_ref):
        step = pl.program_id(0)

        @pl.when(step == 0)
        def _():
            kvt_ref[...] = jnp.transpose(kv_ref[...].astype(F32)).astype(BF16)
            dkv_ref[...] = jnp.zeros_like(dkv_ref)

        scaled = qt_ref[0].astype(F32) * HD**-0.5
        grads = heads_to_lanes(jnp.transpose(d_ref[...].astype(F32)), heads)
        delta = jnp.sum(grads * ot_ref[0], axis=0, keepdims=True)
        empty = jnp.zeros_like(scaled)
        q_pad = jnp.concatenate([scaled, empty], axis=0)
        d_pad = jnp.concatenate([empty, grads], axis=0)
        qp_ref[...] = q_pad.astype(BF16)
        dp_ref[...] = d_pad.astype(BF16)
        qr_ref[...] = jnp.transpose(q_pad).astype(BF16)
        dr_ref[...] = jnp.transpose(d_pad).astype(BF16)
        start = jnp.concatenate([start_ref[0]] * heads, axis=1)
        slot = jnp.concatenate([slot_ref[0]] * heads, axis=1)
        log_total = lse_ref[0]

        def body(masked, j, d_query):
            at = pl.multiple_of(j * KB, KB)
            block = kv_ref[pl.ds(at, KB), :]
            scores = dot(block, qp_ref[...])
            if masked:
                key = at + lax.broadcasted_iota(jnp.int32, (KB, wide), 0)
                scores = jnp.where((key >= start) & (key <= slot), scores, MASKED_SCORE)
            chances = jnp.exp(scores - log_total)
            d_chances = dot(block, dp_ref[...])
            d_scores = (chances * (d_chances - delta)).astype(BF16)
            dkv_ref[pl.ds(at, KB), :] += dot(chances.astype(BF16), dr_ref[...]) + dot(
                d_scores, qr_ref[...]
            )
            return d_query + dot(kvt_ref[:HD, pl.ds(at, KB)], d_scores)

        first, full_first, full_end, end = key_ranges(b_ref, step)
        d_query = jnp.zeros((HD, wide), F32)
        d_query = lax.fori_loop(first, full_first, functools.partial(body, True), d_query)
        d_query = lax.fori_loop(full_first, full_end, functools.partial(body, False), d_query)
        d_query = lax.fori_loop(full_end, end, functools.partial(body, True), d_query)
        d_query = lanes_to_heads(d_query * HD**-0.5, heads)
        turned = jnp.concatenate(
            [turn(d_query[h * HD : (h + 1) * HD], cos_ref[...], -sin_ref[...]) for h in range(heads)],
            axis=0,
        )
        dq_ref[...] = jnp.transpose(turned).astype(BF16)

        @pl.when(step == steps - 1)
        def _():
            for n in range(2):
                give_at = pl.multiple_of((2 * n + 1 - core_ref[0]) * rows, rows)
                keep_at = pl.multiple_of((2 * n + core_ref[0]) * rows, rows)
                give_ref[n] = dkv_ref[pl.ds(give_at, rows), :].astype(BF16)
                keep_ref[n] = dkv_ref[pl.ds(keep_at, rows), :]

    lane = lambda: pl.BlockSpec((HD // 2, QB), lambda i: (0, i))
    row = lambda: pl.BlockSpec((1, 1, QB), lambda i: (i, 0, 0))
    kept = lambda n: pl.BlockSpec((1, n, wide), lambda i: (i, 0, 0))
    return pl.pallas_call(
        after(kernel, 11, deps),
        grid=(steps,),
        in_specs=[
            pl.BlockSpec(memory_space=pltpu.SMEM),
            pl.BlockSpec(memory_space=pltpu.SMEM),
            pl.BlockSpec((QB, width), lambda i: (i, 0)),
            pl.BlockSpec((keys, 2 * HD), lambda i: (0, 0)),
            kept(HD),
            kept(HD),
            kept(1),
            row(),
            row(),
            lane(),
            lane(),
        ]
        + dep_specs(deps),
        out_specs=[
            pl.BlockSpec((QB, width), lambda i: (i, 0)),
            pl.BlockSpec((2, rows, 2 * HD), lambda i: (0, 0, 0)),
            pl.BlockSpec((2, rows, 2 * HD), lambda i: (0, 0, 0)),
        ],
        out_shape=[
            jax.ShapeDtypeStruct((rows, width), BF16),
            jax.ShapeDtypeStruct((2, rows, 2 * HD), BF16),
            jax.ShapeDtypeStruct((2, rows, 2 * HD), F32),
        ],
        scratch_shapes=[
            pltpu.VMEM((keys, 2 * HD), F32),
            pltpu.VMEM((2 * HD, keys), BF16),
            pltpu.VMEM((2 * HD, wide), BF16),
            pltpu.VMEM((2 * HD, wide), BF16),
            pltpu.VMEM((wide, 2 * HD), BF16),
            pltpu.VMEM((wide, 2 * HD), BF16),
        ],
        cost_estimate=pl.CostEstimate(
            flops=rows * 2 * keys * heads * HD, bytes_accessed=2 << 20, transcendentals=0
        ),
        compiler_params=pltpu.CompilerParams(vmem_limit_bytes=60 << 20),
    )(bounds, core, d_mixed, kv, queries, mixed, lse, starts, slots, cosine, sine, *deps)


def keys_middle(keep, got, row, deps=()):
    _, rows, width = keep.shape

    def kernel(row_ref, keep_ref, got_ref, give_out, keep_out):
        row = row_ref[0]
        give_out[...] = (keep_ref[1 - row] + got_ref[1 - row].astype(F32)).astype(BF16)
        keep_out[...] = keep_ref[row] + got_ref[row].astype(F32)

    shapes = [jax.ShapeDtypeStruct((rows, width), t) for t in (BF16, F32)]
    deps = list(deps)
    return pl.pallas_call(
        after(kernel, 3, deps),
        grid=(1,),
        out_shape=shapes,
        in_specs=[pl.BlockSpec(memory_space=pltpu.SMEM)] + whole_specs([keep, got])
        + dep_specs(deps),
        out_specs=whole_specs(shapes),
        cost_estimate=pl.CostEstimate(flops=0, bytes_accessed=2 << 20, transcendentals=0),
    )(row, keep, got, *deps)


def keys_back(queries, keep, got, w_joint, cosine, sine, deps=()):
    deps = list(deps)

    rows, q_cols = queries.shape
    shapes = [jax.ShapeDtypeStruct((rows, n), BF16) for n in (q_cols + 2 * HD, D)]

    def kernel(q_ref, keep_ref, got_ref, w_ref, cos_ref, sin_ref, out_ref, term_ref):
        out_ref[:, :q_cols] = q_ref[...]
        total = jnp.transpose(keep_ref[...] + got_ref[...].astype(F32))
        turned = turn(total[:HD], cos_ref[...], -sin_ref[...])
        both = jnp.concatenate([turned, total[HD:]], axis=0)
        out_ref[:, q_cols:] = jnp.transpose(both).astype(BF16)
        for n in range(0, rows, 256):
            at = slice(n, n + 256)
            term_ref[at, :] = across(out_ref[at, :], w_ref[...]).astype(BF16)

    return pl.pallas_call(
        after(kernel, 6, deps),
        out_shape=shapes,
        grid=(1,),
        in_specs=whole_specs([queries, keep, got, w_joint, cosine, sine]) + dep_specs(deps),
        out_specs=whole_specs(shapes),
        cost_estimate=pl.CostEstimate(flops=0, bytes_accessed=2 << 20, transcendentals=0),
        compiler_params=pltpu.CompilerParams(vmem_limit_bytes=24 << 20),
    )(queries, keep, got, w_joint, cosine, sine, *deps)


def slot_tables(lengths, groups, group_id, first_slot, rows):
    seq_count = lengths.shape[0]
    seq_order = jnp.arange(seq_count, dtype=jnp.int32)
    same_group = groups[None, :] == groups[:, None]
    before = seq_order[None, :] < seq_order[:, None]
    begins = jnp.sum(jnp.where(same_group & before, lengths[None, :], 0), axis=1)
    ends = begins + lengths
    slots = first_slot + jnp.arange(rows, dtype=jnp.int32)
    inside = (
        (groups == group_id)[:, None]
        & (slots[None, :] >= begins[:, None])
        & (slots[None, :] < ends[:, None])
    )
    starts = jnp.where(
        jnp.any(inside, axis=0), jnp.sum(jnp.where(inside, begins[:, None], 0), axis=0), slots
    )
    return slots, starts


def block_bounds(slots, starts, size):
    first_row, last_row = slots[::QB], slots[QB - 1 :: QB]
    low, high = starts[::QB], starts[QB - 1 :: QB]
    first = low // size
    end = last_row // size + 1
    full_first = jnp.clip((high + size - 1) // size, first, end)
    full_end = jnp.clip((first_row + 1) // size, full_first, end)
    return jnp.stack([first, full_first, full_end, end], axis=1).reshape(-1).astype(jnp.int32)


def adamw_step(weight, first, second, grad, rate, decay):
    first_new = BETA_FIRST * first + (1.0 - BETA_FIRST) * grad
    second_new = BETA_SECOND * second + (1.0 - BETA_SECOND) * grad * grad
    first_hat = first_new / (1.0 - BETA_FIRST**STEP)
    second_hat = second_new / (1.0 - BETA_SECOND**STEP)
    weight_new = weight - rate * (first_hat / (jnp.sqrt(second_hat) + ADAM_EPS) + decay * weight)
    return (first_new, second_new, weight_new)


def after(kernel, inputs, deps):
    count = len(deps)
    if not count:
        return kernel
    return lambda *refs: kernel(*refs[:inputs], *refs[inputs + count :])


def any_specs(count):
    return [pl.BlockSpec(memory_space=pl.ANY)] * count


def dep_specs(deps):
    return [
        pl.BlockSpec((1,) * (d.ndim - 2) + (16, 128), lambda *at, n=d.ndim: (0,) * n) for d in deps
    ]


def whole_specs(arrays):
    return [pl.BlockSpec(v.shape, lambda *at, n=len(v.shape): (0,) * n) for v in arrays]


def tie(value, deps):
    deps = list(deps)
    return pl.pallas_call(
        lambda *refs: None,
        grid=(1,),
        out_shape=jax.ShapeDtypeStruct(value.shape, value.dtype),
        in_specs=any_specs(1) + dep_specs(deps),
        out_specs=pl.BlockSpec(memory_space=pl.ANY),
        input_output_aliases={0: 0},
    )(value, *deps)


def lay(pieces, plan, table, blocks, deps=(), weight=1, matrix=None):
    deps = list(deps)
    n, w = pieces[0].shape[-2:]
    extra = [] if matrix is None else [matrix]
    inputs = 1 + len(pieces) + len(extra)
    shapes = [jax.ShapeDtypeStruct((blocks, n, w), BF16), jax.ShapeDtypeStruct((16, 128), BF16)]
    shapes += [jax.ShapeDtypeStruct((blocks * n, m.shape[1]), BF16) for m in extra]

    def kernel(table_ref, *refs):
        out_ref, sign_ref = refs[inputs - 1 : inputs + 1]
        for piece, index, _, entry in plan:
            source = refs[piece]
            out_ref[table_ref[entry]] = source[...] if index is None else source[index]
        sign_ref[...] = jnp.zeros_like(sign_ref)
        if extra:
            rows = out_ref[...].reshape(blocks * n, w)
            refs[inputs + 1][...] = dot(rows, refs[inputs - 2][...]).astype(BF16)

    size = sum(p.size * p.dtype.itemsize for p in pieces)
    return pl.pallas_call(
        after(kernel, inputs, deps),
        out_shape=shapes,
        grid=(1,),
        in_specs=[pl.BlockSpec(memory_space=pltpu.SMEM)] + whole_specs(pieces + extra) + dep_specs(deps),
        out_specs=whole_specs(shapes),
        cost_estimate=pl.CostEstimate(flops=0, bytes_accessed=2 * weight * size, transcendentals=0),
        compiler_params=pltpu.CompilerParams(vmem_limit_bytes=3 * size + (8 << 20)),
    )(table, *pieces, *extra, *deps)


def tie_small(value, late):
    def kernel(value_ref, out_ref):
        out_ref[...] = value_ref[...]

    return in_vmem(kernel, [value], [jax.ShapeDtypeStruct(value.shape, F32)], [late])[0]


def in_vmem(kernel, inputs, out_shape, deps=(), weight=1):
    deps = list(deps)
    count = len(inputs)
    size = sum(v.size * v.dtype.itemsize for v in list(inputs) + list(out_shape))
    return pl.pallas_call(
        after(kernel, count, deps),
        out_shape=out_shape,
        grid=(1,),
        in_specs=whole_specs(inputs) + dep_specs(deps),
        out_specs=whole_specs(out_shape),
        cost_estimate=pl.CostEstimate(flops=0, bytes_accessed=weight * size, transcendentals=0),
        compiler_params=pltpu.CompilerParams(vmem_limit_bytes=2 * size + (6 << 20)),
    )(*inputs, *deps)


def join(parts, deps=()):
    arrays = []
    for array, _ in parts:
        if not any(array is known for known in arrays):
            arrays.append(array)
    spots = [next(n for n, known in enumerate(arrays) if known is array) for array, _ in parts]
    picked = [array.shape if index is None else array.shape[1:] for array, index in parts]

    def kernel(*refs):
        for n, (spot, (_, index)) in enumerate(zip(spots, parts)):
            refs[-1][n] = refs[spot][...] if index is None else refs[spot][index]

    shape = (len(parts),) + picked[0]
    return in_vmem(kernel, arrays, [jax.ShapeDtypeStruct(shape, BF16)], deps)[0]


def rms_inverse(value):
    return lax.rsqrt(jnp.mean(value * value, axis=-1, keepdims=True) + NORM_EPS)


def through_norm(d_normed, value, gain):
    inverse = rms_inverse(value)
    scaled = d_normed * gain
    pre = value * inverse
    return inverse * (scaled - pre * jnp.mean(scaled * pre, axis=-1, keepdims=True))


def load_weights(piece_refs, plan, table_ref, weights, held, sem, part, meanwhile=None):
    copies = []
    for n, (piece, index, entry) in enumerate(plan):
        source = piece_refs[piece] if index is None else piece_refs[piece].at[index]
        at = pl.ds(pl.multiple_of(table_ref[entry] * part, part), part)
        source = source.at[pl.ds(weights[0], len(weights))]
        copies.append(pltpu.make_async_copy(source, held.at[:, at, :], sem.at[n]))
    for copy in copies:
        copy.start()
    if meanwhile is not None:
        meanwhile()
    for copy in copies:
        copy.wait()


def upstream_hidden(upstream, pieces, plan, table, order):
    rows, units, part = upstream.shape[0], pieces[0].shape[-1], D // 16
    count, block = len(pieces), upstream.shape[0] // 2

    def kernel(order_ref, table_ref, u_ref, *refs):
        piece_refs, (dh_ref, ug_ref, uk_ref, w_ref, sem) = refs[:count], refs[count:]

        @pl.when(pl.program_id(0) == 0)
        def _():
            load_weights(piece_refs, plan, table_ref, (2,), w_ref, sem, part)

        for i in range(16):
            at = pl.ds(pl.multiple_of(order_ref[i] * part, part), part)
            to = slice((i % 8) * part, (i % 8 + 1) * part)
            (ug_ref if i < 8 else uk_ref)[:, to] = u_ref[:, at]
        for f in range(0, units, 256):
            at = slice(f, f + 256)
            dh_ref[:, at] = dot(u_ref[...], w_ref[0, :, at])

    by_row = lambda w: pl.BlockSpec((block, w), lambda i: (i, 0))
    shape = lambda w, t: jax.ShapeDtypeStruct((rows, w), t)
    return pl.pallas_call(
        kernel,
        grid=(2,),
        in_specs=[pl.BlockSpec(memory_space=pltpu.SMEM)] * 2 + [by_row(D)] + any_specs(count),
        out_specs=[by_row(units), by_row(D // 2), by_row(D // 2)],
        out_shape=[shape(units, F32), shape(D // 2, BF16), shape(D // 2, BF16)],
        scratch_shapes=[pltpu.VMEM((1, D, units), BF16), pltpu.SemaphoreType.DMA((len(plan),))],
        cost_estimate=pl.CostEstimate(
            flops=2 * rows * D * units, bytes_accessed=12 << 20, transcendentals=0
        ),
        compiler_params=pltpu.CompilerParams(vmem_limit_bytes=22 << 20),
    )(order, table, upstream, *pieces)


def feed_forward(row_pieces, row_plan, row_table, d_hidden, pieces, plan, table, order):
    rows, units, block = d_hidden.shape[0], pieces[0].shape[-1], d_hidden.shape[0] // 2
    count, part, own = len(pieces), D // 16, rows // 16
    row_count = len(row_pieces)

    def kernel(order_ref, table_ref, row_ref, dh_ref, *refs):
        piece_refs, refs = refs[:count], refs[count:]
        row_refs, refs = refs[:row_count], refs[row_count:]
        hid_ref, dg_ref, du_ref, dn_ref, ff_ref, ng_ref, nk_ref, w_ref, all_ref, sem = refs

        @pl.when(pl.program_id(0) == 0)
        def _():
            def lay_rows():
                for piece, index, _, entry in row_plan:
                    at = pl.ds(pl.multiple_of(row_ref[entry] * own, own), own)
                    all_ref[at, :] = row_refs[piece][index]

            load_weights(piece_refs, plan, table_ref, (0, 1, 2), w_ref, sem, part, lay_rows)

        n_ref = all_ref.at[pl.ds(pl.multiple_of(pl.program_id(0) * block, block), block), :]

        for i in range(16):
            at = pl.ds(pl.multiple_of(order_ref[i] * part, part), part)
            to = slice((i % 8) * part, (i % 8 + 1) * part)
            (ng_ref if i < 8 else nk_ref)[:, to] = n_ref[:, at]
        for f in range(0, units, 256):
            at = slice(f, f + 256)
            gate = dot(n_ref[...], w_ref[0, :, at])
            up = dot(n_ref[...], w_ref[1, :, at])
            d_hidden = dh_ref[:, at]
            sigmoid = jax.nn.sigmoid(gate)
            activated = gate * sigmoid
            hid_ref[:, at] = (activated * up).astype(BF16)
            dg_ref[:, at] = (
                d_hidden * up * sigmoid * (1.0 + gate * (1.0 - sigmoid))
            ).astype(BF16)
            du_ref[:, at] = (d_hidden * activated).astype(BF16)
        for d in range(0, D, 512):
            at = slice(d, d + 512)
            dn_ref[:, at] = (
                across(dg_ref[...], w_ref[0, at, :]) + across(du_ref[...], w_ref[1, at, :])
            ).astype(BF16)
            ff_ref[:, at] = across(hid_ref[...], w_ref[2, at, :]).astype(BF16)

    by_row = lambda w: pl.BlockSpec((block, w), lambda i: (i, 0))
    shape = lambda w: jax.ShapeDtypeStruct((rows, w), BF16)
    return pl.pallas_call(
        kernel,
        grid=(2,),
        in_specs=[pl.BlockSpec(memory_space=pltpu.SMEM)] * 3
        + [by_row(units)]
        + any_specs(count)
        + whole_specs(row_pieces),
        out_specs=[by_row(units)] * 3 + [by_row(D)] * 2 + [by_row(D // 2)] * 2,
        out_shape=[shape(units)] * 3 + [shape(D)] * 2 + [shape(D // 2)] * 2,
        scratch_shapes=[
            pltpu.VMEM((3, D, units), BF16),
            pltpu.VMEM((rows, D), BF16),
            pltpu.SemaphoreType.DMA((len(plan),)),
        ],
        cost_estimate=pl.CostEstimate(
            flops=10 * rows * D * units, bytes_accessed=24 << 20, transcendentals=0
        ),
        compiler_params=pltpu.CompilerParams(vmem_limit_bytes=58 << 20),
    )(order, table, row_table, d_hidden, *pieces, *row_pieces)


def outer_blocks(table, groups, deps=()):
    lefts, rights, plan = [], [], []
    for pairs in groups:
        entry = []
        for left, right in pairs:
            spot = next((n for n, known in enumerate(lefts) if known is left), None)
            if spot is None:
                spot = len(lefts)
                lefts.append(left)
            entry.append((spot, len(rights)))
            rights.append(right)
        plan.append(entry)
    width = sum(pairs[0][1].shape[1] for pairs in groups)
    block = D // 16

    def kernel(table_ref, *refs):
        left_refs, refs = refs[: len(lefts)], refs[len(lefts) :]
        right_refs, (give_ref, keep_ref) = refs[: len(rights)], refs[len(rights) :]
        step = pl.program_id(0)
        turned = [jnp.transpose(r[...]) for r in left_refs]
        parts = []
        for entry in plan:
            part = None
            for spot, n in entry:
                term = dot(turned[spot], right_refs[n][...])
                part = term if part is None else part + term
            parts.append(part.astype(BF16))
        whole = parts[0] if len(parts) == 1 else jnp.concatenate(parts, axis=1)

        @pl.when(step < 8)
        def _():
            give_ref[...] = whole

        @pl.when(step >= 8)
        def _():
            keep_ref[...] = whole

    flops = sum(2 * left.shape[0] * D * right.shape[1] for g in groups for left, right in g)
    return pl.pallas_call(
        after(kernel, 1 + len(lefts) + len(rights), deps),
        grid_spec=pltpu.PrefetchScalarGridSpec(
            num_scalar_prefetch=1,
            grid=(16,),
            in_specs=[pl.BlockSpec((v.shape[0], block), lambda i, t: (0, t[i])) for v in lefts]
            + [pl.BlockSpec(v.shape, lambda i, t: (0, 0)) for v in rights]
            + dep_specs(deps),
            out_specs=[
                pl.BlockSpec((block, width), lambda i, t: (jnp.minimum(i, 7), 0)),
                pl.BlockSpec((block, width), lambda i, t: (jnp.maximum(i - 8, 0), 0)),
            ],
        ),
        out_shape=[jax.ShapeDtypeStruct((8 * block, width), BF16)] * 2,
        cost_estimate=pl.CostEstimate(flops=flops, bytes_accessed=4 << 20, transcendentals=0),
        compiler_params=pltpu.CompilerParams(vmem_limit_bytes=12 << 20),
    )(table, *lefts, *rights, *deps)


def fold_core(keeps, gots, deps=()):
    count, pair = len(keeps), D // 8
    widths = [k.shape[1] for k in keeps]
    starts = [sum(widths[:n]) for n in range(count)]
    deps = list(deps)

    def kernel(*refs):
        keep_refs, got_refs, outs = refs[:count], refs[count : 2 * count], refs[2 * count :]
        for k in range(4):

            @pl.when(pl.program_id(0) == k)
            def _():
                for n in range(count):
                    total = keep_refs[n][...].astype(F32) + got_refs[n][...].astype(F32)
                    to = slice(starts[n], starts[n] + widths[n])
                    outs[k][:, to] = total.astype(outs[k].dtype)

    whole = pl.BlockSpec((pair, sum(widths)), lambda i: (0, 0))
    shape = lambda dtype: jax.ShapeDtypeStruct((pair, sum(widths)), dtype)
    return pl.pallas_call(
        after(kernel, 2 * count, deps),
        grid=(4,),
        in_specs=[pl.BlockSpec((pair, w), lambda i: (i, 0)) for w in widths * 2]
        + dep_specs(deps),
        out_specs=[whole] * 4,
        out_shape=[shape(F32)] + [shape(BF16)] * 3,
        cost_estimate=pl.CostEstimate(
            flops=0, bytes_accessed=12 * pair * sum(widths), transcendentals=0
        ),
        compiler_params=pltpu.CompilerParams(vmem_limit_bytes=(28 << 20) if count > 1 else (8 << 20)),
    )(*keeps, *gots, *deps)


def adamw_kernel(weight, first, second, sums, spot, rate, flip, deps=()):
    def kernel(w_ref, m_ref, v_ref, keep_ref, got_ref, m_out, v_out, w_out, sum_ref):
        grad = keep_ref[...] + got_ref[...].astype(F32)
        if flip:
            grad = jnp.transpose(grad)
        weight = w_ref[...]
        first_new, second_new, weight_new = adamw_step(
            weight, m_ref[...], v_ref[...], grad, rate, DECAY_RATE
        )
        m_out[...] = first_new
        v_out[...] = second_new
        w_out[...] = weight_new
        if flip:
            sum_ref[...] = jnp.zeros_like(sum_ref)
        else:
            sum_ref[...] = jnp.sum(weight.astype(BF16).astype(F32) * grad, axis=1, keepdims=True)

    shape = jax.ShapeDtypeStruct(weight.shape, F32)
    columns = weight.shape[0] if flip else weight.shape[1]
    whole = lambda *shape: pl.BlockSpec(shape, lambda i: (0,) * len(shape))
    view = pl.BlockSpec((D // 16, columns), lambda i: (0, spot // columns))
    return pl.pallas_call(
        after(kernel, 5, deps),
        grid=(1,),
        in_specs=[whole(*weight.shape)] * 3 + [view] * 2 + dep_specs(deps),
        out_specs=[whole(*weight.shape)] * 3 + [whole(D // 16, 1)],
        out_shape=[shape] * 3 + [jax.ShapeDtypeStruct((D // 16, 1), F32)],
        cost_estimate=pl.CostEstimate(
            flops=0, bytes_accessed=28 * weight.size, transcendentals=0
        ),
        compiler_params=pltpu.CompilerParams(vmem_limit_bytes=14 << 20),
    )(weight, first, second, *sums, *deps)


def pick(blocks, axis, index):
    return lax.dynamic_index_in_dim(blocks, index, axis, keepdims=False)


class Here:
    def __init__(self):
        self.x, self.yh, self.c, self.yl, self.z = (
            lax.axis_index(a) for a in ("x", "yh", "c", "yl", "z")
        )

    def ztable(self):
        own = [self.yl * 4 + (self.z + k) % 4 for k in range(4)]
        other = [(1 - self.yl) * 4 + (self.z + k) % 4 for k in range(4)]
        return jnp.stack(own + other).astype(jnp.int32)

    def xtable(self):
        table = []
        for dc in range(2):
            core = self.c if dc == 0 else 1 - self.c
            for k in range(4):
                for dy in range(2):
                    yh = self.yh if dy == 0 else 1 - self.yh
                    table.append(((self.x + k) % 4) * 4 + yh * 2 + core)
        return jnp.stack(table).astype(jnp.int32)

    def scatter_tp(self, terms, extras, finish, out_shape, deps=(), weight=1):
        parts = lax.all_to_all(terms, ("yl", "z"), 0, 0, tiled=True)
        return self.sum_tp_parts(parts, extras, finish, out_shape, deps, weight)

    def sum_tp_parts(self, parts, extras, finish, out_shape, deps=(), weight=1):
        parts = parts.reshape(8, -1, parts.shape[1])
        extras, deps = list(extras), list(deps)
        count = len(extras)

        def kernel(part_ref, *refs):
            far, refs = refs[:count], refs[count:]
            outs, refs = refs[: len(out_shape)], refs[len(out_shape) :]
            held, sem = refs[:count], refs[count]
            copies = [pltpu.make_async_copy(far[n], held[n], sem.at[n]) for n in range(count)]
            for copy in copies:
                copy.start()
            total = part_ref[0].astype(F32)
            for n in range(1, 8):
                total = total + part_ref[n].astype(F32)
            for copy in copies:
                copy.wait()
            finish(total, held, outs)

        arrays = [parts] + extras + list(out_shape)
        size = sum(v.size * v.dtype.itemsize for v in arrays)
        return pl.pallas_call(
            after(kernel, 1 + count, deps),
            grid=(1,),
            out_shape=out_shape,
            in_specs=whole_specs([parts]) + any_specs(count) + dep_specs(deps),
            out_specs=whole_specs(out_shape),
            scratch_shapes=[pltpu.VMEM(v.shape, v.dtype) for v in extras]
            + [pltpu.SemaphoreType.DMA((count,))],
            cost_estimate=pl.CostEstimate(
                flops=0, bytes_accessed=weight * size, transcendentals=0
            ),
            compiler_params=pltpu.CompilerParams(vmem_limit_bytes=2 * size + (6 << 20)),
        )(parts, *extras, *deps)

    def gather_first(self, both, second):
        over = lax.ppermute(both, "yl", SWAP)
        return [both, over] + [lax.ppermute(second, "z", ring(-k)) for k in (1, 2, 3)]

    def gather_join(self, first, deps=()):
        both, over, *rest = first
        rest = join([(part, None) for part in rest], deps)
        return both, over, join([(both, 0), (over, 0)]), rest

    def gather_second(self, joined):
        both, over, pair, rest = joined
        pieces = [pair] + [lax.ppermute(pair, "z", ring(-k)) for k in (1, 2, 3)]
        return pieces + [both, over, rest, lax.ppermute(rest, "yl", SWAP)]

    def gather_plan(self):
        spots = [(k, (d,), 4 * d + k) for k in range(4) for d in range(2)]
        spots += [(4, (1,), 8), (5, (1,), 12)]
        spots += [(6, (k,), k + 9) for k in range(3)] + [(7, (k,), k + 13) for k in range(3)]
        plan = [(piece, index, 0, entry) for piece, index, entry in spots]
        table = self.ztable()
        return plan, jnp.concatenate([2 * table, 2 * table + 1])

    def gather_last(self, pieces, deps=(), weight=1, matrix=None):
        plan, table = self.gather_plan()
        laid, *rest = lay(pieces, plan, table, 16, deps, weight, matrix)
        return laid.reshape(-1, laid.shape[-1]), rest[-1]

    def gather_product(self, both, second, matrix, deps=(), weight=1):
        joined = self.gather_join(self.gather_first(both, second))
        return self.gather_last(self.gather_second(joined), deps, weight, matrix)

    def gather_weights(self, shard):
        pair = jnp.stack([shard, lax.ppermute(shard, "yh", SWAP)])
        mine = [pair] + [lax.ppermute(pair, "x", ring(-k)) for k in (1, 2, 3)]
        return mine + [lax.ppermute(p, "c", SWAP) for p in mine]

    def gather_large(self, shard, over, deps):
        pair = join([(shard, None), (over, None)], deps)
        near = [lax.ppermute(pair, "x", ring(-1)), lax.ppermute(pair, "x", ring(1))]
        far = [
            lax.ppermute(near[0][0], "x", ring(-1)),
            lax.ppermute(near[1][1], "x", ring(1)),
        ]
        mine = [pair] + near + far
        plan = [(0, 0, 0), (0, 1, 1), (1, 0, 2), (1, 1, 3), (2, 0, 6), (2, 1, 7)]
        plan += [(3, None, 4), (4, None, 5)]
        plan += [(p + 5, i, e + 8) for p, i, e in plan]
        theirs = [lax.ppermute(p, "c", SWAP) for p in mine]
        return mine + theirs, plan, near

    def scatter_weights(self, total, sends, late=False):
        near = [lax.ppermute(sends[n], "x", ring(n + 1)) for n in (0, 2)]
        far = lax.ppermute(tie(sends[1], near) if late else sends[1], "x", ring(2))
        for part in near + [far]:
            total = total + part.astype(F32)
        n = D // 16
        give = total[n:].astype(BF16)
        return [total, lax.ppermute(give, "yh", SWAP)], near, give

    def gather_ctx(self, own):
        over = lax.ppermute(own, "yh", SWAP)
        beside = lax.ppermute(own, "c", SWAP)
        pieces = [own, over, beside, lax.ppermute(over, "c", SWAP)]
        table = jnp.stack(
            [
                self.yh * 2 + self.c,
                (1 - self.yh) * 2 + self.c,
                self.yh * 2 + 1 - self.c,
                (1 - self.yh) * 2 + 1 - self.c,
            ]
        ).astype(jnp.int32)
        plan = [(i, None, 0, i) for i in range(4)]
        return lay(pieces, plan, table, 4)[0].reshape(-1, own.shape[1]), beside

    def scatter_ctx(self, give, keep, deps):
        got = lax.ppermute(give, "c", SWAP)
        give, keep = keys_middle(keep, got, self.yh.reshape(1).astype(jnp.int32), deps)
        return keep, lax.ppermute(give, "yh", SWAP)

    def sum_tp(self, value):
        value = value + lax.ppermute(value, "yl", SWAP)
        got = [lax.ppermute(value, "z", ring(k)) for k in (1, 2, 3)]
        parts = jnp.stack([value] + got)
        order = jnp.stack([(self.z - j) % 4 for j in range(4)])
        return jnp.sum(jnp.take(parts, order, axis=0), axis=0)


def per_device(
    tokens,
    cotangent,
    lengths,
    groups,
    query_weight,
    query_m,
    query_v,
    kv_weight,
    kv_m,
    kv_v,
    out_weight,
    out_m,
    out_v,
    gate_weight,
    gate_m,
    gate_v,
    up_weight,
    up_m,
    up_v,
    down_weight,
    down_m,
    down_v,
    norm_gains,
    gains_m,
    gains_v,
):
    here = Here()
    row_count = tokens.shape[0]
    group_rows = row_count * 4
    group_id = here.x
    ctx_id = here.yh * 2 + here.c
    tp_id = here.yl * 4 + here.z
    half = row_count // 2
    part = half // 8
    xtable = here.xtable()

    kv_flat = kv_weight.reshape(D // 16, 2 * HD)
    attn_shard = jnp.concatenate([query_weight, kv_flat, out_weight.T], axis=1).astype(BF16)
    q_cols, kv_cols, o_cols = query_weight.shape[1], 2 * HD, out_weight.shape[0]
    cols = q_cols + kv_cols + o_cols
    gains_low = norm_gains.astype(BF16)
    gain_rows = jnp.zeros((16, cols), BF16).at[:2, : D // 16].set(gains_low)
    attn_pieces = here.gather_weights(jnp.concatenate([attn_shard, gain_rows], axis=0))

    units = gate_weight.shape[1]
    ff_shard = jnp.stack([gate_weight, up_weight, down_weight.T]).astype(BF16)
    ff_over = lax.ppermute(ff_shard, "yh", SWAP)

    slots, starts = slot_tables(lengths, groups, group_id, ctx_id * row_count, row_count)
    frequency = ROPE_BASE ** (-2.0 * jnp.arange(HD // 2, dtype=F32) / HD)
    angles = frequency[:, None] * (slots - starts).astype(F32)[None, :]
    cosine, sine = jnp.cos(angles), jnp.sin(angles)
    bounds_forward = block_bounds(slots, starts, KB_FORWARD)
    bounds = block_bounds(slots, starts, KB)
    slot_rows, start_rows = slots.reshape(-1, 1, QB), starts.reshape(-1, 1, QB)

    normed_one, query_raw, kv_local, w_joint, w_out, gain_values = normed_projections(
        tokens,
        attn_pieces,
        xtable,
        (q_cols, kv_cols, o_cols),
        cosine,
        sine,
        NORM_EPS,
        deps=[ff_over],
    )
    kv_whole, kv_beside = here.gather_ctx(kv_local)
    ff_pieces, ff_plan, weights_near = here.gather_large(ff_shard, ff_over, [kv_beside])

    mixed, turned, raw, log_total = attention_forward(
        query_raw, kv_whole, bounds_forward, start_rows, slot_rows, cosine, sine, 0, row_count
    )
    mixed = tie(mixed, weights_near)
    own = lambda v: lax.dynamic_slice_in_dim(v, tp_id * 2 * part, 2 * part, axis=0)
    own_inputs, own_upstream = own(tokens), own(cotangent)
    own_wide = jax.ShapeDtypeStruct((2 * part, D), F32)
    own_low = [jax.ShapeDtypeStruct((2, part, D), BF16), jax.ShapeDtypeStruct((part, D), BF16)]

    def both(outs, value):
        outs[0][0] = value[:part]
        outs[0][1] = value[part:]
        outs[1][...] = value[part:]

    def close_attention(total, ins, outs):
        value = ins[0][...].astype(F32) + total
        outs[0][...] = value
        both(outs[1:], (value * rms_inverse(value) * ins[1][1:2, :]).astype(BF16))

    term = jnp.einsum("ra,da->rd", mixed, w_out, preferred_element_type=F32).astype(BF16)
    hidden_one, *own_normed = here.scatter_tp(
        term, [own_inputs, gain_values], close_attention, [own_wide] + own_low, deps=ff_pieces[5:]
    )
    order = here.xtable()
    order = jnp.concatenate([order[8:], order[:8]])
    d_hidden, upstream_give, upstream_keep = upstream_hidden(
        cotangent, ff_pieces, ff_plan, xtable, order
    )
    joined = here.gather_join(here.gather_first(*own_normed), [d_hidden])
    row_pieces = here.gather_second(joined)
    hidden, d_gate, d_up, d_two, out_term, normed_give, normed_keep = feed_forward(
        row_pieces, *here.gather_plan(), d_hidden, ff_pieces, ff_plan, xtable, order
    )
    outer = lambda a, b: jnp.einsum("rd,rf->df", a, b, preferred_element_type=F32).astype(BF16)
    gives = [outer(normed_give, d_gate), outer(normed_give, d_up), outer(upstream_give, hidden)]
    keeps = [outer(normed_keep, d_gate), outer(normed_keep, d_up), outer(upstream_keep, hidden)]
    gots = [lax.ppermute(give, "c", SWAP) for give in gives]

    ff_total, *ff_sends = fold_core(keeps, gots)

    def close_feed_forward(total, ins, outs):
        value = ins[1][...].astype(F32) + through_norm(total, ins[0][...], ins[2][1:2, :])
        outs[0][...] = value
        both(outs[1:], value.astype(BF16))

    d_hidden_one, *own_branch = here.scatter_tp(
        d_two,
        [hidden_one, own_upstream, gain_values],
        close_feed_forward,
        [own_wide] + own_low,
        weight=20,
    )
    d_branch, d_mixed = here.gather_product(*own_branch, w_out, deps=[ff_total], weight=20)


    ff_sums, ff_near, ff_give = here.scatter_weights(ff_total, ff_sends, True)

    def close_output(total, ins, outs):
        both(outs, (ins[0][...] + total).astype(BF16))

    own_output = here.scatter_tp(
        tie(out_term, [d_branch]), [hidden_one], close_output, own_low
    )
    out_joined = here.gather_join(here.gather_first(*own_output))

    d_query_low, *d_kv = attention_backward(
        d_mixed,
        kv_whole,
        turned,
        raw,
        log_total,
        bounds,
        start_rows,
        slot_rows,
        cosine,
        sine,
        here.c.reshape(1).astype(jnp.int32),
    )
    d_joint, term = keys_back(
        d_query_low, *here.scatter_ctx(*d_kv, ff_near), w_joint, cosine, sine, deps=out_joined[2:]
    )
    out_second = here.gather_second(out_joined)
    output, out_sign = here.gather_last(out_second)

    term = tie(term, [])

    give, keep = outer_blocks(
        order,
        [((d_branch, mixed),), ((normed_one, d_joint),)],
        deps=[term],
    )
    attn_got = lax.ppermute(give, "c", SWAP)
    attn_total, *attn_sends = fold_core([keep], [attn_got])
    attn_sums, _, attn_give = here.scatter_weights(attn_total, attn_sends)

    def close_inputs(total, ins, outs):
        value = ins[0][...] + through_norm(total, ins[1][...].astype(F32), ins[2][:1, :])
        both(outs, value.astype(BF16))

    own_results = here.scatter_tp(
        term,
        [d_hidden_one, own_inputs, gain_values],
        close_inputs,
        own_low,
        deps=[ff_give, out_sign],
        weight=50,
    )
    last_pieces = here.gather_second(here.gather_join(here.gather_first(*own_results)))
    tokens_grad, _ = here.gather_last(last_pieces, deps=attn_sums[1:], weight=50)

    late = own_results[1:2]
    flat = lambda v: v.reshape(kv_flat.shape)
    fan = D ** (-0.5)
    out_fan = max(1, 4 * D // group_rows) ** (-0.5)
    query_new = adamw_kernel(query_weight, query_m, query_v, attn_sums, o_cols, fan, False, late)
    out_new = adamw_kernel(out_weight, out_m, out_v, attn_sums, 0, out_fan, True)
    kv_new = adamw_kernel(
        kv_flat, flat(kv_m), flat(kv_v), attn_sums, q_cols + o_cols, fan, False
    )
    gate_new = adamw_kernel(gate_weight, gate_m, gate_v, ff_sums, 0, fan, False, late)
    up_new = adamw_kernel(up_weight, up_m, up_v, ff_sums, units, fan, False, late)
    down_new = adamw_kernel(down_weight, down_m, down_v, ff_sums, 2 * units, FF ** (-0.5), True, late)

    gain_sums = jnp.stack([query_new[3] + kv_new[3], gate_new[3] + up_new[3]])[:, :, 0]
    grad_gains = here.sum_tp(tie_small(gain_sums, last_pieces[1])) / gains_low.astype(F32)
    gains_new = adamw_step(norm_gains, gains_m, gains_v, grad_gains, 0.5, 0.0)
    return (
        output,
        tokens_grad,
        *query_new[:3],
        *[v.reshape(kv_weight.shape) for v in kv_new[:3]],
        *out_new[:3],
        *gate_new[:3],
        *up_new[:3],
        *down_new[:3],
        *gains_new,
    )


def solution(mesh):
    fine = Mesh(mesh.devices.reshape(4, 2, 2, 2, 4), ("x", "yh", "c", "yl", "z"))
    rows = ("x", "yh", "c")
    tp = ("yl", "z")
    by_row, by_col, by_unit = P(rows, None), P(rows, tp), P(tp, rows)
    by_kv, by_gain = P(rows, tp, None), P(None, rows)
    in_specs = (
        (by_row,) * 2
        + (P(),) * 2
        + (by_col,) * 3
        + (by_kv,) * 3
        + (by_unit,) * 3
        + (by_col,) * 6
        + (by_unit,) * 3
        + (by_gain,) * 3
    )
    out_specs = (
        (by_row,) * 2
        + (by_col,) * 3
        + (by_kv,) * 3
        + (by_unit,) * 3
        + (by_col,) * 6
        + (by_unit,) * 3
        + (by_gain,) * 3
    )
    return jax.shard_map(
        per_device, mesh=fine, in_specs=in_specs, out_specs=out_specs, check_vma=False
    )
```
